32 devices in a mesh: energy: 4 (over x, core), atom: 8 (over z, y).
Axes of the slice: x: 2, y: 2, z: 4, core: 2. Of those that a mesh axis runs over, the one named last changes fastest.
Arguments:
- green: float32 [2, 8, 16, 128, 128], P(None, 'energy', 'atom'), may hold values from -6 to 6
- coupling: float32 [16, 6, 128, 128], P('atom'), may hold values from -0.5 to 0.5
- phonon: float32 [16, 6, 4], P('atom'), may hold values from 0.2 to 2
- neighbours: int32 [16, 6], P('atom'), may hold values from 0 to 15, as said below
Outputs:
- self_energy: float32 [2, 8, 16, 128, 128], P(None, 'energy', 'atom')
- rates: float32 [16, 128], P('atom')
The draws below stay inside these ranges and needn't reach their ends.
Inputs may be any that keep to these rules, and one draw needn't show every extreme that they name: `neighbours`: each entry lies within 2 of its row's index and within 0 to 15; offsets +2 and -2 both occur.
All inputs are finite; a program needn't handle non-finite values.
Results may differ from the reference program's by a relative error of at most 0.000071.
Values sent between devices are 32-bit elements; how exact they have to be, the bound alone decides.
No kernel may reach another device: no remote copies, remote signals or barrier semaphores. Data moves between devices by JAX's collectives and lax.ppermute only.
A program may use at most 64 MiB of HBM per device.

```python
import math
import jax
import jax.numpy as jnp
from jax import lax

ORB = 128
NBR = 6
NE = 8
NA = 16


def draw_neighbours(key, part):
    key_offsets, key_rows = jax.random.split(jax.random.fold_in(key, 17))
    offsets = jax.random.randint(key_offsets, (NA, NBR), -2, 3)
    picked = jax.random.randint(key_rows, (2,), 2, NA - 2)
    offsets = offsets.at[picked[0], 0].set(2)
    offsets = offsets.at[picked[1], 1].set(-2)
    base = jnp.arange(NA, dtype=jnp.int32)[:, None]
    return jnp.clip(base + offsets, 0, NA - 1).astype(jnp.int32)


def block_scale(key, dims, cuts, least, largest):
    def one(dim, shards_of):
        steps = jax.random.uniform(jax.random.fold_in(jax.random.fold_in(key, 6), dim), (shards_of,), jnp.float32, least / len(cuts), largest / len(cuts))
        return jnp.repeat(jnp.exp(steps), dims[dim] // shards_of).reshape((-1,) + (1,) * (len(dims) - dim - 1))

    level = one(*cuts[0])
    for cut in cuts[1:]:
        level = level * one(*cut)
    return level


def centred(rng, dims, scale, reach, pieces=(), kind=jnp.bfloat16):
    result = scale * jax.random.normal(rng, dims, jnp.float32)
    if pieces:
        result = result * block_scale(rng, dims, pieces, -0.22, 0.18)
    return jnp.clip(result, -reach, reach).astype(kind)


def setup_inputs(seed: int = 0) -> dict:
    arg_keys = jax.random.split(jax.random.key(seed), 5)
    green = centred(arg_keys[0], (2, NE, NA, ORB, ORB), 1.0, 6.0, ((1, 4), (2, 8)), jnp.float32)
    coupling = centred(arg_keys[1], (NA, NBR, ORB, ORB), ORB ** -0.5, 0.5, ((0, 8),), jnp.float32)
    phonon = jnp.clip(jnp.exp(math.log(2.0) - 2.3025851 * jax.random.uniform(arg_keys[2], (NA, NBR, 4), jnp.float32) ** block_scale(arg_keys[2], (NA, NBR, 4), ((0, 8),), -0.2, 0.2)), 0.2, 2.0)
    neighbours = draw_neighbours(jax.random.fold_in(arg_keys[4], 71), 0)
    return {"green": green, "coupling": coupling, "phonon": phonon, "neighbours": neighbours}


def reference(green, coupling, phonon, neighbours):
    highest = lax.Precision.HIGHEST
    shifts = (-2, -1, 1, 2)

    def one_block(index):
        rows = neighbours[index]
        near = jnp.take(green, rows, axis=2)
        padded = jnp.pad(near, ((0, 0), (2, 2), (0, 0), (0, 0), (0, 0)))
        mixed = jnp.zeros_like(near)
        for step in range(4):
            start = 2 + shifts[step]
            factor = phonon[index, :, step][None, None, :, None, None]
            mixed = mixed + factor * padded[:, start:start + NE]
        mats = coupling[index]
        inner = jnp.einsum('jik,cejkl->cejil', mats, mixed, precision=highest)
        sigma = jnp.einsum('cejil,jml->ceim', inner, mats, precision=highest)
        own = green[:, :, index]
        rate = jnp.einsum('eil,eli->i', sigma[0], own[0], precision=highest) - jnp.einsum('eil,eli->i', sigma[1], own[1], precision=highest)
        return sigma, rate / (4.0 * NE)

    sigmas, rates = lax.map(one_block, jnp.arange(NA, dtype=jnp.int32))
    self_energy = jnp.transpose(sigmas, (1, 2, 0, 3, 4))
    return self_energy, rates
```

```python
import functools

import jax
import jax.numpy as jnp
from jax import lax
from jax.experimental import pallas as pl
from jax.experimental.pallas import tpu as pltpu
from jax.sharding import PartitionSpec as P

SHIFTS = (-2, -1, 1, 2)
VMEM = pl.BlockSpec(memory_space=pltpu.VMEM)
SMEM = pl.BlockSpec(memory_space=pltpu.SMEM)


def halves(x):
    high = x.astype(jnp.bfloat16)
    return high, (x - high.astype(jnp.float32)).astype(jnp.bfloat16)


def swap(x, axis, first):
    low = range(first, lax.axis_size(axis) - 1, 2)
    return lax.ppermute(x, axis, [(i, i + 1) for i in low] + [(i + 1, i) for i in low])


def shift(x, axis, up):
    pairs = [(i, i + 1) for i in range(lax.axis_size(axis) - 1)]
    return lax.ppermute(x, axis, pairs if up else [(j, i) for i, j in pairs])


def add_pairs(place, phonon, coupling, blocks, total, base, count):
    atoms, slots, orb = coupling.shape[0], coupling.shape[1], coupling.shape[-1]
    e_local = blocks.shape[2]
    reach = max(SHIFTS)
    rows = 2 * e_local * orb

    def one(index, _):
        a, j = index // slots, index % slots
        b = place[a, j] - base

        @pl.when((b >= 0) & (b < count))
        def _():
            high, low = halves(coupling[a, j])
            right = jnp.concatenate(
                [jnp.concatenate([high, high], 1), jnp.concatenate([low, low], 1)], 0
            )
            left = jnp.concatenate([high, low], 1)
            near = blocks[b].reshape(rows, 2 * orb)
            inner = lax.dot_general(
                near, right, (((1,), (1,)), ((), ())), preferred_element_type=jnp.float32
            )
            inner = inner[:, :orb] + inner[:, orb:]
            for c in range(2):
                for e in range(e_local):
                    start = (c * e_local + e) * orb
                    high, low = halves(inner[start : start + orb])
                    both = jnp.concatenate([high, low], 1)
                    outer = jnp.dot(
                        left,
                        jnp.concatenate([both, both], 0),
                        preferred_element_type=jnp.float32,
                    )
                    outer = outer[:, :orb] + outer[:, orb:]
                    for k, s in enumerate(SHIFTS):
                        total[e - s + reach, c, a] += phonon[a, j, k] * outer
    lax.fori_loop(0, atoms * slots, one, None)


def put_blocks(blocks, at, green):
    orb = green.shape[-1]
    for c in range(green.shape[0]):
        for e in range(green.shape[1]):
            for a in range(green.shape[2]):
                high, low = halves(green[c, e, a])
                blocks[at + a, c, e, :, :orb] = high
                blocks[at + a, c, e, :, orb:] = low


def first_kernel(place, phonon, coupling, green, near, below, above, total, turned, blocks):
    e_local, a_local = green.shape[1], green.shape[2]
    reach = max(SHIFTS)
    put_blocks(blocks, 0, green)
    put_blocks(blocks, a_local, near)
    total[...] = jnp.zeros_like(total)
    for c in range(2):
        for a in range(a_local):
            for e in range(e_local):
                turned[reach + e, c, a] = green[c, e, a].T
            for e in range(reach):
                turned[e, c, a] = below[c, e, a].T
                turned[reach + e_local + e, c, a] = above[c, e, a].T
    add_pairs(place, phonon, coupling, blocks, total, 0, 2 * a_local)


def second_kernel(place, phonon, coupling, near, turned, before, down, own, up, rate, total, blocks):
    a_local, e_local, orb = near.shape[2], near.shape[1], near.shape[-1]
    reach = max(SHIFTS)
    total[...] = before[...]
    put_blocks(blocks, 0, near)
    add_pairs(place, phonon, coupling, blocks, total, 2 * a_local, a_local)
    for a in range(a_local):
        sums = jnp.zeros((orb, orb), jnp.float32)
        for d in range(total.shape[0]):
            sums += total[d, 0, a] * turned[d, 0, a] - total[d, 1, a] * turned[d, 1, a]
        rate[a : a + 1, :] = jnp.sum(sums.T, axis=0, keepdims=True)
    for c in range(2):
        for a in range(a_local):
            for e in range(reach):
                down[c, e, a] = total[e, c, a]
                up[c, e, a] = total[reach + e_local + e, c, a]
            for e in range(e_local):
                own[c, e, a] = total[reach + e, c, a]


def per_device(green, coupling, phonon, neighbours):
    _, e_local, a_local, orb, _ = green.shape
    reach = max(SHIFTS)
    ahead = swap(green, "atom", 0)
    across = swap(green, "atom", 1)
    below = shift(green, "energy", True)
    above = shift(green, "energy", False)

    index = lax.axis_index("atom")
    rows = neighbours - index * a_local
    even = index % 2 == 0
    side = jnp.where(rows < 0, -1, jnp.where(rows >= a_local, 1, 0))
    group = jnp.where(side == 0, 0, jnp.where((side > 0) == even, 1, 2))
    place = group * a_local + rows - side * a_local

    spread = (e_local + 2 * reach, 2, a_local, orb, orb)
    total, turned = pl.pallas_call(
        first_kernel,
        out_shape=[jax.ShapeDtypeStruct(spread, jnp.float32)] * 2,
        in_specs=[SMEM, SMEM] + [VMEM] * 5,
        out_specs=[VMEM] * 2,
        scratch_shapes=[pltpu.VMEM((2 * a_local, 2, e_local, orb, 2 * orb), jnp.bfloat16)],
        compiler_params=pltpu.CompilerParams(vmem_limit_bytes=24 * 2**20),
        cost_estimate=pl.CostEstimate(flops=2 * 10**9, bytes_accessed=2 * 10**6, transcendentals=0),
    )(place, phonon, coupling, green, ahead, below, above)
    edge = jax.ShapeDtypeStruct((2, reach, a_local, orb, orb), jnp.float32)
    down, own, up, rate = pl.pallas_call(
        second_kernel,
        out_shape=[
            edge,
            jax.ShapeDtypeStruct(green.shape, jnp.float32),
            edge,
            jax.ShapeDtypeStruct((a_local, orb), jnp.float32),
        ],
        in_specs=[SMEM, SMEM] + [VMEM] * 4,
        out_specs=[VMEM] * 4,
        scratch_shapes=[
            pltpu.VMEM(spread, jnp.float32),
            pltpu.VMEM((a_local, 2, e_local, orb, 2 * orb), jnp.bfloat16),
        ],
        compiler_params=pltpu.CompilerParams(vmem_limit_bytes=24 * 2**20),
        cost_estimate=pl.CostEstimate(flops=10**9, bytes_accessed=2 * 10**6, transcendentals=0),
    )(place, phonon, coupling, across, turned, total)

    from_above = shift(down, "energy", False)
    from_below = shift(up, "energy", True)
    points = e_local * lax.axis_size("energy")
    rates = lax.psum(rate, "energy") / (4.0 * points)
    return own + from_below + from_above, rates


def solution(mesh):
    return jax.shard_map(
        per_device,
        mesh=mesh,
        in_specs=(
            P(None, "energy", "atom", None, None),
            P("atom", None, None, None),
            P("atom", None, None),
            P("atom", None),
        ),
        out_specs=(P(None, "energy", "atom", None, None), P("atom", None)),
        check_vma=False,
    )
```

```python
import functools

import jax
import jax.numpy as jnp
from jax import lax
from jax.experimental import pallas as pl
from jax.experimental.pallas import tpu as pltpu
from jax.sharding import PartitionSpec as P

SHIFTS = (-2, -1, 1, 2)
REACH = max(SHIFTS)
BATCH = 3
VMEM = pl.BlockSpec(memory_space=pltpu.VMEM)
SMEM = pl.BlockSpec(memory_space=pltpu.SMEM)


def halves(x):
    high = x.astype(jnp.bfloat16)
    return high, (x - high.astype(jnp.float32)).astype(jnp.bfloat16)


def swap(x, axis, first):
    low = range(first, lax.axis_size(axis) - 1, 2)
    return lax.ppermute(x, axis, [(i, i + 1) for i in low] + [(i + 1, i) for i in low])


def forward(x, axis):
    size = lax.axis_size(axis)
    ups = [(i, i + 2) for i in range(0, size - 2, 2)]
    downs = [(i + 2, i) for i in range(1, size - 2, 2)]
    return lax.ppermute(x, axis, ups + downs)


def shift(x, axis, up):
    pairs = [(i, i + 1) for i in range(lax.axis_size(axis) - 1)]
    return lax.ppermute(x, axis, pairs if up else [(j, i) for i, j in pairs])


def put_blocks(blocks, at, green):
    orb = green.shape[-1]
    for e in range(green.shape[0]):
        for a in range(green.shape[1]):
            high, low = halves(green[e, a])
            blocks[at + a, e, :, :orb] = high
            blocks[at + a, e, :, orb:] = low


def add_pairs(place, phonon, coupling, blocks, total, picked, base, count):
    atoms, slots, orb = coupling.shape[0], coupling.shape[1], coupling.shape[-1]
    e_local = blocks.shape[1]

    def outers(a, j, b):
        high, low = halves(coupling[a, j])
        right = jnp.concatenate(
            [jnp.concatenate([high, high], 1), jnp.concatenate([low, low], 1)], 0
        )
        left = jnp.concatenate([high, low], 1)
        near = blocks[b].reshape(e_local * orb, 2 * orb)
        inner = lax.dot_general(
            near, right, (((1,), (1,)), ((), ())), preferred_element_type=jnp.float32
        )
        inner = inner[:, :orb] + inner[:, orb:]
        result = []
        for e in range(e_local):
            high, low = halves(inner[e * orb : (e + 1) * orb])
            both = jnp.concatenate([high, low], 1)
            outer = jnp.dot(
                left, jnp.concatenate([both, both], 0), preferred_element_type=jnp.float32
            )
            result.append(outer[:, :orb] + outer[:, orb:])
        return result

    for a in range(atoms):

        def note(j, found):
            b = place[a, j] - base
            here = (b >= 0) & (b < count)

            @pl.when(here)
            def _():
                picked[found] = j

            return found + here.astype(jnp.int32)

        found = lax.fori_loop(0, slots, note, jnp.int32(0))

        def batch(index, _):
            sums = [None] * (e_local + 2 * REACH)
            for u in range(BATCH):
                at = index * BATCH + u
                j = picked[jnp.minimum(at, found - 1)]
                live = jnp.where(at < found, 1.0, 0.0)
                for e, outer in enumerate(outers(a, j, place[a, j] - base)):
                    for k, s in enumerate(SHIFTS):
                        d = e - s + REACH
                        term = (phonon[a, j, k] * live) * outer
                        sums[d] = term if sums[d] is None else sums[d] + term
            for d, value in enumerate(sums):
                if value is not None:
                    total[d, a] += value

        lax.fori_loop(0, (found + BATCH - 1) // BATCH, batch, None)


def turn(turned, c, green, below, above):
    e_local = green.shape[1]
    for a in range(green.shape[2]):
        for e in range(e_local):
            turned[REACH + e, a] = green[c, e, a].T
        for e in range(REACH):
            turned[e, a] = below[c, e, a].T
            turned[REACH + e_local + e, a] = above[c, e, a].T


def finish(c, total, down, own, up):
    e_local = own.shape[1]
    for a in range(own.shape[2]):
        for e in range(REACH):
            down[c, e, a] = total[e, a]
            up[c, e, a] = total[REACH + e_local + e, a]
        for e in range(e_local):
            own[c, e, a] = total[REACH + e, a]


def rate_sums(total, turned, a):
    sums = total[0, a] * turned[0, a]
    for d in range(1, total.shape[0]):
        sums += total[d, a] * turned[d, a]
    return sums


def early_kernel(c, place, phonon, coupling, green, near, total, blocks, picked):
    a_local = green.shape[2]
    put_blocks(blocks, 0, green.at[c])
    put_blocks(blocks, a_local, near)
    total[...] = jnp.zeros_like(total)
    add_pairs(place, phonon, coupling, blocks, total, picked, 0, 2 * a_local)


def own_kernel(c, place, phonon, coupling, green, below, above, total, turned, blocks, picked):
    a_local = green.shape[2]
    put_blocks(blocks, 0, green.at[c])
    total[...] = jnp.zeros_like(total)
    add_pairs(place, phonon, coupling, blocks, total, picked, 0, a_local)
    turn(turned, c, green, below, above)


def middle_kernel(
    c, place, phonon, coupling, green, near, before, below, above,
    down, own, up, partial, total, turned, blocks, picked,
):
    a_local = green.shape[2]
    turn(turned, c, green, below, above)
    put_blocks(blocks, 0, near)
    total[...] = before[...]
    add_pairs(place, phonon, coupling, blocks, total, picked, 2 * a_local, a_local)
    finish(c, total, down, own, up)
    for a in range(a_local):
        partial[a] = rate_sums(total, turned, a)


def late_kernel(
    c, scale, place, phonon, coupling, ahead, across, before, turned, partial, down_in, own_in, up_in,
    down, own, up, rate, total, blocks, picked,
):
    a_local = ahead.shape[1]
    put_blocks(blocks, 0, ahead)
    put_blocks(blocks, a_local, across)
    total[...] = before[...]
    add_pairs(place, phonon, coupling, blocks, total, picked, a_local, 2 * a_local)
    finish(c, total, down, own, up)
    for a in range(a_local):
        sums = partial[a] - rate_sums(total, turned, a)
        rate[a : a + 1, :] = jnp.sum(sums.T, axis=0, keepdims=True) * scale


def call(kernel, out, ins, sources, spread, orb, flops, scratch=(), aliases={}):
    params = pltpu.CompilerParams(vmem_limit_bytes=24 * 2**20)
    cost = pl.CostEstimate(flops=flops, bytes_accessed=2 * 10**6, transcendentals=0)
    return pl.pallas_call(
        kernel,
        out_shape=[jax.ShapeDtypeStruct(shape, jnp.float32) for shape in out],
        in_specs=[SMEM, SMEM] + [VMEM] * (len(ins) - 2),
        out_specs=[VMEM] * len(out),
        scratch_shapes=list(scratch)
        + [
            pltpu.VMEM((sources, spread[0] - 2 * REACH, orb, 2 * orb), jnp.bfloat16),
            pltpu.SMEM((ins[2].shape[1],), jnp.int32),
        ],
        input_output_aliases=aliases,
        compiler_params=params,
        cost_estimate=cost,
    )(*ins)


def per_device(green, coupling, phonon, neighbours):
    _, e_local, a_local, orb, _ = green.shape
    points = e_local * lax.axis_size("energy")
    ahead0 = swap(green[0], "atom", 0)
    ahead1 = swap(green[1], "atom", 0)
    across1 = swap(green[1], "atom", 1)
    across0 = forward(ahead0, "atom")
    below = shift(green, "energy", True)
    above = shift(green, "energy", False)

    index = lax.axis_index("atom")
    rows = neighbours - index * a_local
    even = index % 2 == 0
    side = jnp.where(rows < 0, -1, jnp.where(rows >= a_local, 1, 0))
    group = jnp.where(side == 0, 0, jnp.where((side > 0) == even, 1, 2))
    place = group * a_local + rows - side * a_local

    spread = (e_local + 2 * REACH, a_local, orb, orb)
    whole = (2, e_local, a_local, orb, orb)
    edge = (2, REACH, a_local, orb, orb)
    run = functools.partial(call, spread=spread, orb=orb)
    work = pltpu.VMEM(spread, jnp.float32)
    shared = (place, phonon, coupling)
    (early,) = run(
        functools.partial(early_kernel, 0), [spread], shared + (green, ahead0), 2 * a_local, flops=10**9
    )
    down, own, up, partial = run(
        functools.partial(middle_kernel, 0),
        [edge, whole, edge, (a_local, orb, orb)],
        shared + (green, across0, early, below, above),
        a_local,
        flops=10**9,
        scratch=(work, work),
    )
    before, turned = run(
        functools.partial(own_kernel, 1),
        [spread, spread],
        shared + (green, below, above),
        a_local,
        flops=10**9,
    )
    down, own, up, rate = run(
        functools.partial(late_kernel, 1, 1.0 / (4.0 * points)),
        [edge, whole, edge, (a_local, orb)],
        shared + (ahead1, across1, before, turned, partial, down, own, up),
        2 * a_local,
        flops=10**9,
        scratch=(work,),
        aliases={8: 0, 9: 1, 10: 2},
    )

    from_above = shift(down, "energy", False)
    from_below = shift(up, "energy", True)
    rates = lax.psum(rate, "energy")
    return own + from_below + from_above, rates


def solution(mesh):
    return jax.shard_map(
        per_device,
        mesh=mesh,
        in_specs=(
            P(None, "energy", "atom", None, None),
            P("atom", None, None, None),
            P("atom", None, None),
            P("atom", None),
        ),
        out_specs=(P(None, "energy", "atom", None, None), P("atom", None)),
        check_vma=False,
    )
```

```python
import functools

import jax
import jax.numpy as jnp
from jax import lax
from jax.experimental import pallas as pl
from jax.experimental.pallas import tpu as pltpu
from jax.sharding import PartitionSpec as P

SHIFTS = (-2, -1, 1, 2)
REACH = max(SHIFTS)
OWN, PAIR, FAR = 0, 1, 2
VMEM = pl.BlockSpec(memory_space=pltpu.VMEM)
SMEM = pl.BlockSpec(memory_space=pltpu.SMEM)
HBM = pl.BlockSpec(memory_space=pltpu.HBM)


def halves(x):
    high = x.astype(jnp.bfloat16)
    return high, (x - high.astype(jnp.float32)).astype(jnp.bfloat16)


def swap(x, axis, first):
    low = range(first, lax.axis_size(axis) - 1, 2)
    return lax.ppermute(x, axis, [(i, i + 1) for i in low] + [(i + 1, i) for i in low])


def forward(x, axis):
    size = lax.axis_size(axis)
    ups = [(i, i + 2) for i in range(0, size - 2, 2)]
    downs = [(i + 2, i) for i in range(1, size - 2, 2)]
    return lax.ppermute(x, axis, ups + downs)


def shift(x, axis, up):
    pairs = [(i, i + 1) for i in range(lax.axis_size(axis) - 1)]
    return lax.ppermute(x, axis, pairs if up else [(j, i) for i, j in pairs])


def put_blocks(blocks, c, green):
    orb = green.shape[-1]
    for e in range(green.shape[0]):
        for a in range(green.shape[1]):
            high, low = halves(green[e, a])
            blocks[c, a, e, :, :orb] = high
            blocks[c, a, e, :, orb:] = low


def add_pairs(group, neighbours, phonon, coupling, blocks, totals, picked, size):
    atoms, slots, orb = coupling.shape[0], coupling.shape[1], coupling.shape[-1]
    e_local = blocks.shape[2]
    index = lax.axis_index("atom")
    base = index * atoms
    if group != OWN:
        upper = (index & 1) == (0 if group == PAIR else 1)
        base += jnp.where(upper, atoms, -atoms)

    def note(at, found):
        a = at // slots
        b = neighbours[a, at - a * slots] - base
        here = (b >= 0) & (b < atoms)

        @pl.when(here)
        def _():
            picked[found] = at

        return found + here.astype(jnp.int32)

    found = lax.fori_loop(0, atoms * slots, note, jnp.int32(0))

    def one(at):
        item = picked[jnp.minimum(at, found - 1)]
        live = jnp.where(at < found, 1.0, 0.0)
        a = item // slots
        j = item - a * slots
        high, low = halves(coupling[a, j])
        right = jnp.concatenate(
            [jnp.concatenate([high, high], 1), jnp.concatenate([low, low], 1)], 0
        )
        left = jnp.concatenate([high, low], 1)
        b = neighbours[a, j] - base
        for c, total in enumerate(totals):
            near = blocks[c, b].reshape(e_local * orb, 2 * orb)
            inner = lax.dot_general(
                near, right, (((1,), (1,)), ((), ())), preferred_element_type=jnp.float32
            )
            inner = inner[:, :orb] + inner[:, orb:]
            sums = [None] * (e_local + 2 * REACH)
            for e in range(e_local):
                high, low = halves(inner[e * orb : (e + 1) * orb])
                both = jnp.concatenate([high, low], 1)
                outer = jnp.dot(
                    left, jnp.concatenate([both, both], 0), preferred_element_type=jnp.float32
                )
                outer = outer[:, :orb] + outer[:, orb:]
                for k, s in enumerate(SHIFTS):
                    d = e - s + REACH
                    term = (phonon[a, k, j] * live) * outer
                    sums[d] = term if sums[d] is None else sums[d] + term
            yield total, a, sums

    def batch(step, _):
        results = [r for u in range(size) for r in one(step * size + u)]
        for total, a, sums in results:
            for d, value in enumerate(sums):
                if value is not None:
                    total[d, a] += value

    lax.fori_loop(0, (found + size - 1) // size, batch, None)


def part_kernel(green, first, second, sems):
    copies = [
        pltpu.make_async_copy(green.at[c], part, sems.at[c]) for c, part in enumerate((first, second))
    ]
    for copy in copies:
        copy.start()
    for copy in copies:
        copy.wait()


def own_kernel(neighbours, phonon, coupling, green, total0, total1, blocks, picked):
    for c, total in enumerate((total0, total1)):
        put_blocks(blocks, c, green.at[c])
        total[...] = jnp.zeros_like(total)
    add_pairs(OWN, neighbours, phonon, coupling, blocks, (total0, total1), picked, 2)


def turn(turned, c, green, below, above):
    e_local = green.shape[1]
    for a in range(green.shape[2]):
        for e in range(e_local):
            turned[REACH + e, a] = green[c, e, a].T
        for e in range(REACH):
            turned[e, a] = below[c, e, a].T
            turned[REACH + e_local + e, a] = above[c, e, a].T


def pair_kernel(neighbours, phonon, coupling, ahead0, before0, total0, blocks, picked):
    put_blocks(blocks, 0, ahead0)
    total0[...] = before0[...]
    add_pairs(PAIR, neighbours, phonon, coupling, blocks, (total0,), picked, 4)


def finish(c, total, own, core, cross):
    e_local = own.shape[1]
    odd = lax.axis_index("energy") & 1
    up = REACH + e_local
    to_core, to_cross = jnp.where(odd == 0, up, 0), jnp.where(odd == 0, 0, up)
    for e in range(REACH):
        core[c, e] = total[to_core + e]
        cross[c, e] = total[to_cross + e]
    for e in range(e_local):
        own[c, e] = total[REACH + e]


def rate_sums(total, turned, a):
    sums = total[0, a] * turned[0, a]
    for d in range(1, total.shape[0]):
        sums += total[d, a] * turned[d, a]
    return sums


def middle_kernel(
    neighbours, phonon, coupling, green, below, above, across0, ahead1, before0, before1,
    own, core, cross, partial, total1, turned1, total0, turned0, blocks, picked,
):
    turn(turned0, 0, green, below, above)
    turn(turned1, 1, green, below, above)
    total0[...] = before0[...]
    total1[...] = before1[...]
    put_blocks(blocks, 0, across0)
    add_pairs(FAR, neighbours, phonon, coupling, blocks, (total0,), picked, 4)
    put_blocks(blocks, 0, ahead1)
    add_pairs(PAIR, neighbours, phonon, coupling, blocks, (total1,), picked, 4)
    finish(0, total0, own, core, cross)
    for a in range(partial.shape[0]):
        partial[a] = rate_sums(total0, turned0, a)


def last_kernel(
    scale, neighbours, phonon, coupling, across1, turned1, partial, before1, own_in, core_in, cross_in,
    own, core, cross, rate, total1, blocks, picked,
):
    put_blocks(blocks, 0, across1)
    total1[...] = before1[...]
    add_pairs(FAR, neighbours, phonon, coupling, blocks, (total1,), picked, 4)
    finish(1, total1, own, core, cross)
    for a in range(partial.shape[0]):
        sums = partial[a] - rate_sums(total1, turned1, a)
        rate[a : a + 1, :] = jnp.sum(sums.T, axis=0, keepdims=True) * scale


def per_device(green, coupling, phonon, neighbours):
    _, e_local, a_local, orb, _ = green.shape
    points = e_local * lax.axis_size("energy")
    spread = (e_local + 2 * REACH, a_local, orb, orb)
    edge = (2, REACH, a_local, orb, orb)

    def call(kernel, out, operands, parts=1, scratch=(), aliases={}):
        return pl.pallas_call(
            kernel,
            out_shape=[jax.ShapeDtypeStruct(shape, jnp.float32) for shape in out],
            in_specs=[SMEM, SMEM] + [VMEM] * (1 + len(operands)),
            out_specs=[VMEM] * len(out),
            scratch_shapes=list(scratch)
            + [
                pltpu.VMEM((parts, a_local, e_local, orb, 2 * orb), jnp.bfloat16),
                pltpu.SMEM((a_local * neighbours.shape[1],), jnp.int32),
            ],
            input_output_aliases=aliases,
            compiler_params=pltpu.CompilerParams(vmem_limit_bytes=24 * 2**20),
            cost_estimate=pl.CostEstimate(flops=10**9, bytes_accessed=2 * 10**6, transcendentals=0),
        )(neighbours, jnp.swapaxes(phonon, 1, 2), coupling, *operands)

    green0, green1 = pl.pallas_call(
        part_kernel,
        out_shape=[jax.ShapeDtypeStruct(green.shape[1:], green.dtype)] * 2,
        in_specs=[HBM],
        out_specs=[VMEM] * 2,
        scratch_shapes=[pltpu.SemaphoreType.DMA((2,))],
        compiler_params=pltpu.CompilerParams(vmem_limit_bytes=24 * 2**20),
    )(green)
    green, green0, green1 = lax.optimization_barrier((green, green0, green1))
    below = shift(green, "energy", True)
    above = shift(green, "energy", False)
    ahead1 = swap(green1, "atom", 0)
    ahead0 = swap(green0, "atom", 0)
    ahead0, green1 = lax.optimization_barrier((ahead0, green1))
    across1 = swap(green1, "atom", 1)
    across0 = forward(ahead0, "atom")

    work = pltpu.VMEM(spread, jnp.float32)
    total0, total1 = call(own_kernel, [spread] * 2, (green,), parts=2)
    (total0,) = call(pair_kernel, [spread], (ahead0, total0), aliases={4: 0})
    own, core, cross, partial, total1, turned = call(
        middle_kernel,
        [green.shape, edge, edge, (a_local, orb, orb), spread, spread],
        (green, below, above, across0, ahead1, total0, total1),
        scratch=(work, work),
        aliases={9: 4},
    )
    own, core, cross, rate = call(
        functools.partial(last_kernel, 1.0 / (4.0 * points)),
        [green.shape, edge, edge, (a_local, orb)],
        (across1, turned, partial, total1, own, core, cross),
        scratch=(work,),
        aliases={7: 0, 8: 1, 9: 2},
    )
    from_core = swap(core, "energy", 0)
    from_cross = swap(cross, "energy", 1)
    return own + from_cross + from_core, lax.psum(rate, "energy")


def solution(mesh):
    return jax.shard_map(
        per_device,
        mesh=mesh,
        in_specs=(
            P(None, "energy", "atom", None, None),
            P("atom", None, None, None),
            P("atom", None, None),
            P("atom", None),
        ),
        out_specs=(P(None, "energy", "atom", None, None), P("atom", None)),
        check_vma=False,
    )
```

```python
import functools

import jax
import jax.numpy as jnp
from jax import lax
from jax.experimental import pallas as pl
from jax.experimental.pallas import tpu as pltpu
from jax.sharding import PartitionSpec as P

SHIFTS = (-2, -1, 1, 2)
REACH = max(SHIFTS)
OWN, PAIR, FAR = 0, 1, 2
VMEM = pl.BlockSpec(memory_space=pltpu.VMEM)
SMEM = pl.BlockSpec(memory_space=pltpu.SMEM)
HBM = pl.BlockSpec(memory_space=pltpu.HBM)


def halves(x):
    high = x.astype(jnp.bfloat16)
    return high, (x - high.astype(jnp.float32)).astype(jnp.bfloat16)


def swap(x, axis, first):
    low = range(first, lax.axis_size(axis) - 1, 2)
    return lax.ppermute(x, axis, [(i, i + 1) for i in low] + [(i + 1, i) for i in low])


def forward(x, axis):
    size = lax.axis_size(axis)
    ups = [(i, i + 2) for i in range(0, size - 2, 2)]
    downs = [(i + 2, i) for i in range(1, size - 2, 2)]
    return lax.ppermute(x, axis, ups + downs)


def shift(x, axis, up):
    pairs = [(i, i + 1) for i in range(lax.axis_size(axis) - 1)]
    return lax.ppermute(x, axis, pairs if up else [(j, i) for i, j in pairs])


def put_blocks(blocks, c, green):
    orb = green.shape[-1]
    for e in range(green.shape[0]):
        for a in range(green.shape[1]):
            high, low = halves(green[e, a])
            blocks[c, a, e, :, :orb] = high
            blocks[c, a, e, :, orb:] = low


def add_pairs(group, neighbours, phonon, coupling, blocks, totals, picked, size):
    atoms, slots, orb = coupling.shape[0], coupling.shape[1], coupling.shape[-1]
    e_local = blocks.shape[2]
    index = lax.axis_index("atom")
    base = index * atoms
    if group != OWN:
        upper = (index & 1) == (0 if group == PAIR else 1)
        base += jnp.where(upper, atoms, -atoms)

    found = jnp.int32(0)
    for a in range(atoms):
        for j in range(slots):
            picked[found] = a * slots + j
            b = neighbours[a, j] - base
            found += ((b >= 0) & (b < atoms)).astype(jnp.int32)

    def batch(step, _):
        pairs = []
        for u in range(size):
            at = step * size + u
            item = picked[jnp.minimum(at, found - 1)]
            a = item // slots
            j = item - a * slots
            high, low = halves(coupling[a, j])
            left = jnp.concatenate([high, low], 1)
            right = jnp.concatenate(
                [jnp.concatenate([high, high], 1), jnp.concatenate([low, low], 1)], 0
            )
            pairs.append((a, j, neighbours[a, j] - base, jnp.where(at < found, 1.0, 0.0), left, right))
        inners = []
        for a, j, b, live, left, right in pairs:
            for c in range(len(totals)):
                near = blocks[c, b].reshape(e_local * orb, 2 * orb)
                inner = lax.dot_general(
                    near, right, (((1,), (1,)), ((), ())), preferred_element_type=jnp.float32
                )
                inners.append(inner[:, :orb] + inner[:, orb:])
        results = []
        for a, j, b, live, left, right in pairs:
            for total in totals:
                inner = inners.pop(0)
                sums = [None] * (e_local + 2 * REACH)
                for e in range(e_local):
                    high, low = halves(inner[e * orb : (e + 1) * orb])
                    both = jnp.concatenate([high, low], 1)
                    outer = jnp.dot(
                        left, jnp.concatenate([both, both], 0), preferred_element_type=jnp.float32
                    )
                    outer = outer[:, :orb] + outer[:, orb:]
                    for k, s in enumerate(SHIFTS):
                        d = e - s + REACH
                        term = (phonon[a, k, j] * live) * outer
                        sums[d] = term if sums[d] is None else sums[d] + term
                results.append((total, a, sums))
        for total, a, sums in results:
            for d, value in enumerate(sums):
                if value is not None:
                    total[d, a] += value

    lax.fori_loop(0, (found + size - 1) // size, batch, None)


def part_kernel(green, first, second, sems):
    copies = [
        pltpu.make_async_copy(green.at[c], part, sems.at[c]) for c, part in enumerate((first, second))
    ]
    for copy in copies:
        copy.start()
    for copy in copies:
        copy.wait()


def own_kernel(neighbours, phonon, coupling, green0, green1, total0, total1, blocks, picked):
    for c, (green, total) in enumerate(((green0, total0), (green1, total1))):
        put_blocks(blocks, c, green)
        total[...] = jnp.zeros_like(total)
    add_pairs(OWN, neighbours, phonon, coupling, blocks, (total0, total1), picked, 2)


def pair_kernel(
    neighbours, phonon, coupling, green0, green1, ahead0, ahead1, before0, before1, every,
    total0, total1, turned, below, above, sems, blocks, picked,
):
    e_local, a_local = green0.shape[0], green0.shape[1]
    me, devices = lax.axis_index("energy"), every.shape[0]
    lower, upper = jnp.maximum(me - 1, 0), jnp.minimum(me + 1, devices - 1)
    fetch_below = pltpu.make_async_copy(
        every.at[lower, :, pl.ds(e_local - REACH, REACH)], below, sems.at[0]
    )
    fetch_above = pltpu.make_async_copy(every.at[upper, :, pl.ds(0, REACH)], above, sems.at[1])
    fetch_below.start()
    fetch_above.start()
    total0[...] = before0[...]
    total1[...] = before1[...]
    put_blocks(blocks, 0, ahead0)
    put_blocks(blocks, 1, ahead1)
    add_pairs(PAIR, neighbours, phonon, coupling, blocks, (total0, total1), picked, 2)
    fetch_below.wait()
    fetch_above.wait()
    has_below, has_above = jnp.where(me > 0, 1.0, 0.0), jnp.where(me < devices - 1, 1.0, 0.0)
    for c, green in enumerate((green0, green1)):
        for a in range(a_local):
            for e in range(e_local):
                turned[c, REACH + e, a] = green[e, a].T
            for e in range(REACH):
                turned[c, e, a] = below[c, e, a].T * has_below
                turned[c, REACH + e_local + e, a] = above[c, e, a].T * has_above


def finish(c, total, own, core, cross):
    e_local = own.shape[1]
    odd = lax.axis_index("energy") & 1
    up = REACH + e_local
    to_core, to_cross = jnp.where(odd == 0, up, 0), jnp.where(odd == 0, 0, up)
    for e in range(REACH):
        core[c, e] = total[to_core + e]
        cross[c, e] = total[to_cross + e]
    for e in range(e_local):
        own[c, e] = total[REACH + e]


def rate_sums(total, turned, c, a):
    sums = total[0, a] * turned[c, 0, a]
    for d in range(1, total.shape[0]):
        sums += total[d, a] * turned[c, d, a]
    return sums


def far_kernel(
    neighbours, phonon, coupling, across0, turned, before0,
    own, core, cross, partial, total0, blocks, picked,
):
    total0[...] = before0[...]
    put_blocks(blocks, 0, across0)
    add_pairs(FAR, neighbours, phonon, coupling, blocks, (total0,), picked, 4)
    finish(0, total0, own, core, cross)
    for a in range(partial.shape[0]):
        partial[a] = rate_sums(total0, turned, 0, a)


def last_kernel(
    scale, neighbours, phonon, coupling, across1, turned, partial, before1, own_in, core_in, cross_in,
    own, core, cross, rate, total1, blocks, picked,
):
    put_blocks(blocks, 0, across1)
    total1[...] = before1[...]
    add_pairs(FAR, neighbours, phonon, coupling, blocks, (total1,), picked, 4)
    own[0] = own_in[0]
    core[0] = core_in[0]
    cross[0] = cross_in[0]
    finish(1, total1, own, core, cross)
    for a in range(partial.shape[0]):
        sums = partial[a] - rate_sums(total1, turned, 1, a)
        rate[a : a + 1, :] = jnp.sum(sums.T, axis=0, keepdims=True) * scale


def per_device(green, coupling, phonon, neighbours):
    _, e_local, a_local, orb, _ = green.shape
    points = e_local * lax.axis_size("energy")
    spread = (e_local + 2 * REACH, a_local, orb, orb)
    edge = (2, REACH, a_local, orb, orb)

    def call(kernel, out, operands, parts=1, scratch=(), far=0):
        return pl.pallas_call(
            kernel,
            out_shape=[jax.ShapeDtypeStruct(shape, jnp.float32) for shape in out],
            in_specs=[SMEM, SMEM] + [VMEM] * (1 + len(operands) - far) + [HBM] * far,
            out_specs=[VMEM] * len(out),
            scratch_shapes=list(scratch)
            + [
                pltpu.VMEM((parts, a_local, e_local, orb, 2 * orb), jnp.bfloat16),
                pltpu.SMEM((a_local * neighbours.shape[1] + 1,), jnp.int32),
            ],
            compiler_params=pltpu.CompilerParams(vmem_limit_bytes=24 * 2**20),
            cost_estimate=pl.CostEstimate(flops=10**9, bytes_accessed=2 * 10**6, transcendentals=0),
        )(neighbours, jnp.swapaxes(phonon, 1, 2), coupling, *operands)

    green0, green1 = pl.pallas_call(
        part_kernel,
        out_shape=[jax.ShapeDtypeStruct(green.shape[1:], green.dtype)] * 2,
        in_specs=[HBM],
        out_specs=[VMEM] * 2,
        scratch_shapes=[pltpu.SemaphoreType.DMA((2,))],
        compiler_params=pltpu.CompilerParams(vmem_limit_bytes=24 * 2**20),
    )(green)
    every = lax.all_gather(green, "energy")
    ahead1 = swap(green1, "atom", 0)
    ahead0 = swap(green0, "atom", 0)
    total0, total1 = call(own_kernel, [spread] * 2, (green0, green1), parts=2)
    ahead0, total0, total1 = lax.optimization_barrier((ahead0, total0, total1))
    across0 = forward(ahead0, "atom")
    across1 = forward(ahead1, "atom")

    work = pltpu.VMEM(spread, jnp.float32)
    total0, total1, turned = call(
        pair_kernel,
        [spread] * 2 + [(2,) + spread],
        (green0, green1, ahead0, ahead1, total0, total1, every),
        parts=2,
        scratch=[pltpu.VMEM(edge, jnp.float32)] * 2 + [pltpu.SemaphoreType.DMA((2,))],
        far=1,
    )
    own, core, cross, partial = call(
        far_kernel,
        [green.shape, edge, edge, (a_local, orb, orb)],
        (across0, turned, total0),
        scratch=(work,),
    )
    own, core, cross, rate = call(
        functools.partial(last_kernel, 1.0 / (4.0 * points)),
        [green.shape, edge, edge, (a_local, orb)],
        (across1, turned, partial, total1, own, core, cross),
        scratch=(work,),
    )
    from_core = swap(core, "energy", 0)
    from_cross = swap(cross, "energy", 1)
    rates = jnp.sum(lax.all_gather(rate, "energy"), axis=0)
    return own + from_cross + from_core, rates


def solution(mesh):
    return jax.shard_map(
        per_device,
        mesh=mesh,
        in_specs=(
            P(None, "energy", "atom", None, None),
            P("atom", None, None, None),
            P("atom", None, None),
            P("atom", None),
        ),
        out_specs=(P(None, "energy", "atom", None, None), P("atom", None)),
        check_vma=False,
    )
```

```python
import functools

import jax
import jax.numpy as jnp
from jax import lax
from jax.experimental import pallas as pl
from jax.experimental.pallas import tpu as pltpu
from jax.sharding import PartitionSpec as P

SHIFTS = (-2, -1, 1, 2)
REACH = max(SHIFTS)
OWN, PAIR, FAR = 0, 1, 2
VMEM = pl.BlockSpec(memory_space=pltpu.VMEM)
SMEM = pl.BlockSpec(memory_space=pltpu.SMEM)
HBM = pl.BlockSpec(memory_space=pltpu.HBM)


def halves(x):
    high = x.astype(jnp.bfloat16)
    return high, (x - high.astype(jnp.float32)).astype(jnp.bfloat16)


def swap(x, axis, first):
    low = range(first, lax.axis_size(axis) - 1, 2)
    return lax.ppermute(x, axis, [(i, i + 1) for i in low] + [(i + 1, i) for i in low])


def forward(x, axis):
    size = lax.axis_size(axis)
    ups = [(i, i + 2) for i in range(0, size - 2, 2)]
    downs = [(i + 2, i) for i in range(1, size - 2, 2)]
    return lax.ppermute(x, axis, ups + downs)


def shift(x, axis, up):
    pairs = [(i, i + 1) for i in range(lax.axis_size(axis) - 1)]
    return lax.ppermute(x, axis, pairs if up else [(j, i) for i, j in pairs])


def put_blocks(blocks, c, green):
    orb = green.shape[-1]
    for e in range(green.shape[0]):
        for a in range(green.shape[1]):
            high, low = halves(green[e, a])
            blocks[c, a, e, :, :orb] = high
            blocks[c, a, e, :, orb:] = low


def add_pairs(group, neighbours, phonon, coupling, blocks, totals, picked, size):
    atoms, slots, orb = coupling.shape[0], coupling.shape[1], coupling.shape[-1]
    e_local = blocks.shape[2]
    index = lax.axis_index("atom")
    base = index * atoms
    if group != OWN:
        upper = (index & 1) == (0 if group == PAIR else 1)
        base += jnp.where(upper, atoms, -atoms)

    found = jnp.int32(0)
    for a in range(atoms):
        for j in range(slots):
            picked[found] = a * slots + j
            b = neighbours[a, j] - base
            found += ((b >= 0) & (b < atoms)).astype(jnp.int32)

    def batch(step, _):
        pairs = []
        for u in range(size):
            at = step * size + u
            item = picked[jnp.minimum(at, found - 1)]
            a = item // slots
            j = item - a * slots
            high, low = halves(coupling[a, j])
            left = jnp.concatenate([high, low], 1)
            right = jnp.concatenate(
                [jnp.concatenate([high, high], 1), jnp.concatenate([low, low], 1)], 0
            )
            pairs.append((a, j, neighbours[a, j] - base, jnp.where(at < found, 1.0, 0.0), left, right))
        inners = []
        for a, j, b, live, left, right in pairs:
            for c in range(len(totals)):
                near = blocks[c, b].reshape(e_local * orb, 2 * orb)
                inner = lax.dot_general(
                    near, right, (((1,), (1,)), ((), ())), preferred_element_type=jnp.float32
                )
                inners.append(inner[:, :orb] + inner[:, orb:])
        results = []
        for a, j, b, live, left, right in pairs:
            for total in totals:
                inner = inners.pop(0)
                sums = [None] * (e_local + 2 * REACH)
                for e in range(e_local):
                    high, low = halves(inner[e * orb : (e + 1) * orb])
                    both = jnp.concatenate([high, low], 1)
                    outer = jnp.dot(
                        left, jnp.concatenate([both, both], 0), preferred_element_type=jnp.float32
                    )
                    outer = outer[:, :orb] + outer[:, orb:]
                    for k, s in enumerate(SHIFTS):
                        d = e - s + REACH
                        term = (phonon[a, k, j] * live) * outer
                        sums[d] = term if sums[d] is None else sums[d] + term
                results.append((total, a, sums))
        for total, a, sums in results:
            for d, value in enumerate(sums):
                if value is not None:
                    total[d, a] += value

    lax.fori_loop(0, (found + size - 1) // size, batch, None)


def part_kernel(green, first, second, sems):
    copies = [
        pltpu.make_async_copy(green.at[c], part, sems.at[c]) for c, part in enumerate((first, second))
    ]
    for copy in copies:
        copy.start()
    for copy in copies:
        copy.wait()


def own_kernel(neighbours, phonon, coupling, green0, green1, total0, total1, blocks, picked):
    for c, (green, total) in enumerate(((green0, total0), (green1, total1))):
        put_blocks(blocks, c, green)
        total[...] = jnp.zeros_like(total)
    add_pairs(OWN, neighbours, phonon, coupling, blocks, (total0, total1), picked, 2)


def pair_kernel(neighbours, phonon, coupling, ahead, before, total, blocks, picked):
    total[...] = before[...]
    put_blocks(blocks, 0, ahead)
    add_pairs(PAIR, neighbours, phonon, coupling, blocks, (total,), picked, 4)


def turn_kernel(
    neighbours, phonon, coupling, ahead, before, green0, green1, by_core, by_cross,
    total, turned, blocks, picked,
):
    e_local, a_local = green0.shape[0], green0.shape[1]
    core, cross = partner_energies(turned.shape[1])
    for c, green in enumerate((green0, green1)):
        for a in range(a_local):
            for e in range(e_local):
                turned[c, REACH + e, a] = green[e, a].T
            for e in range(REACH):
                turned[c, core + e, a] = by_core[c, e, a].T
                turned[c, cross + e, a] = by_cross[c, e, a].T
    pair_kernel(neighbours, phonon, coupling, ahead, before, total, blocks, picked)


def partner_energies(spread):
    odd = lax.axis_index("energy") & 1
    return jnp.where(odd == 0, spread - REACH, 0), jnp.where(odd == 0, 0, spread - REACH)


def finish(total, core, cross):
    to_core, to_cross = partner_energies(total.shape[0])
    for e in range(REACH):
        core[e] = total[to_core + e]
        cross[e] = total[to_cross + e]


def rate_sums(total, turned, c, a):
    sums = total[0, a] * turned[c, 0, a]
    for d in range(1, total.shape[0]):
        sums += total[d, a] * turned[c, d, a]
    return sums


def far_kernel(
    neighbours, phonon, coupling, across, before, turned, total, core, cross, partial, blocks, picked
):
    pair_kernel_far(neighbours, phonon, coupling, across, before, total, blocks, picked)
    finish(total, core, cross)
    for a in range(partial.shape[0]):
        partial[a] = rate_sums(total, turned, 0, a)


def pair_kernel_far(neighbours, phonon, coupling, across, before, total, blocks, picked):
    total[...] = before[...]
    put_blocks(blocks, 0, across)
    add_pairs(FAR, neighbours, phonon, coupling, blocks, (total,), picked, 4)


def last_kernel(
    scale, neighbours, phonon, coupling, across, before, turned, partial,
    total, core, cross, rate, blocks, picked,
):
    pair_kernel_far(neighbours, phonon, coupling, across, before, total, blocks, picked)
    finish(total, core, cross)
    for a in range(partial.shape[0]):
        sums = partial[a] - rate_sums(total, turned, 1, a)
        total_rate = jnp.sum(sums.T, axis=0, keepdims=True) * scale
        for copy in range(rate.shape[0]):
            rate[copy, a : a + 1, :] = total_rate


def end_kernel(total0, total1, cross0, core0, cross1, core1, rates, out, rate):
    e_local = out.shape[1]
    for c, (total, cross, core) in enumerate(((total0, cross0, core0), (total1, cross1, core1))):
        for e in range(e_local):
            out[c, e] = total[REACH + e] + core[e] + cross[e]
    rate[...] = jnp.sum(rates[...], axis=0)


def per_device(green, coupling, phonon, neighbours):
    _, e_local, a_local, orb, _ = green.shape
    points = e_local * lax.axis_size("energy")
    spread = (e_local + 2 * REACH, a_local, orb, orb)
    edge = (REACH, a_local, orb, orb)

    def call(kernel, out, operands, parts=1):
        return pl.pallas_call(
            kernel,
            out_shape=[jax.ShapeDtypeStruct(shape, jnp.float32) for shape in out],
            in_specs=[SMEM, SMEM] + [VMEM] * (1 + len(operands)),
            out_specs=[VMEM] * len(out),
            scratch_shapes=[
                pltpu.VMEM((parts, a_local, e_local, orb, 2 * orb), jnp.bfloat16),
                pltpu.SMEM((a_local * neighbours.shape[1] + 1,), jnp.int32),
            ],
            compiler_params=pltpu.CompilerParams(vmem_limit_bytes=24 * 2**20),
            cost_estimate=pl.CostEstimate(flops=10**6, bytes_accessed=10**4, transcendentals=0),
        )(neighbours, jnp.swapaxes(phonon, 1, 2), coupling, *operands)

    green0, green1 = pl.pallas_call(
        part_kernel,
        out_shape=[jax.ShapeDtypeStruct(green.shape[1:], green.dtype)] * 2,
        in_specs=[HBM],
        out_specs=[VMEM] * 2,
        scratch_shapes=[pltpu.SemaphoreType.DMA((2,))],
        compiler_params=pltpu.CompilerParams(vmem_limit_bytes=24 * 2**20),
    )(green)
    ahead1 = swap(green1, "atom", 0)
    ahead0 = swap(green0, "atom", 0)
    total0, total1 = call(own_kernel, [spread] * 2, (green0, green1), parts=2)
    ahead0, total0 = lax.optimization_barrier((ahead0, total0))
    green, total1 = lax.optimization_barrier((green, total1))
    by_core, by_cross = swap(green, "energy", 0), swap(green, "energy", 1)
    across0 = forward(ahead0, "atom")
    (total0,) = call(pair_kernel, [spread], (ahead0, total0))
    ahead1, total0 = lax.optimization_barrier((ahead1, total0))
    across1 = forward(ahead1, "atom")
    total1, turned = call(
        turn_kernel, [spread, (2,) + spread], (ahead1, total1, green0, green1, by_core, by_cross)
    )
    total0, core0, cross0, partial = call(
        far_kernel, [spread, edge, edge, (a_local, orb, orb)], (across0, total0, turned)
    )
    core0, cross0 = swap(core0, "energy", 0), swap(cross0, "energy", 1)
    total1, core1, cross1, rate = call(
        functools.partial(last_kernel, 1.0 / (4.0 * points)),
        [spread, edge, edge, (lax.axis_size("energy"), a_local, orb)],
        (across1, total1, turned, partial),
    )
    core1, cross1 = swap(core1, "energy", 0), swap(cross1, "energy", 1)
    rates = lax.all_to_all(rate, "energy", 0, 0)
    return pl.pallas_call(
        end_kernel,
        out_shape=[
            jax.ShapeDtypeStruct(green.shape, jnp.float32),
            jax.ShapeDtypeStruct((a_local, orb), jnp.float32),
        ],
        in_specs=[VMEM] * 7,
        out_specs=[VMEM] * 2,
        compiler_params=pltpu.CompilerParams(vmem_limit_bytes=24 * 2**20),
        cost_estimate=pl.CostEstimate(flops=10**6, bytes_accessed=2 * 10**6, transcendentals=0),
    )(total0, total1, cross0, core0, cross1, core1, rates)


def solution(mesh):
    return jax.shard_map(
        per_device,
        mesh=mesh,
        in_specs=(
            P(None, "energy", "atom", None, None),
            P("atom", None, None, None),
            P("atom", None, None),
            P("atom", None),
        ),
        out_specs=(P(None, "energy", "atom", None, None), P("atom", None)),
        check_vma=False,
    )
```

```python
import functools

import jax
import jax.numpy as jnp
from jax import lax
from jax.experimental import pallas as pl
from jax.experimental.pallas import tpu as pltpu
from jax.sharding import PartitionSpec as P

SHIFTS = (-2, -1, 1, 2)
REACH = max(SHIFTS)
OWN, PAIR, FAR = 0, 1, 2
FEW = 4
VMEM = pl.BlockSpec(memory_space=pltpu.VMEM)
SMEM = pl.BlockSpec(memory_space=pltpu.SMEM)
HBM = pl.BlockSpec(memory_space=pltpu.HBM)


def halves(x):
    high = x.astype(jnp.bfloat16)
    return high, (x - high.astype(jnp.float32)).astype(jnp.bfloat16)


def swap(x, axis, first):
    low = range(first, lax.axis_size(axis) - 1, 2)
    return lax.ppermute(x, axis, [(i, i + 1) for i in low] + [(i + 1, i) for i in low])


def forward(x, axis):
    size = lax.axis_size(axis)
    ups = [(i, i + 2) for i in range(0, size - 2, 2)]
    downs = [(i + 2, i) for i in range(1, size - 2, 2)]
    return lax.ppermute(x, axis, ups + downs)


def shift(x, axis, up):
    pairs = [(i, i + 1) for i in range(lax.axis_size(axis) - 1)]
    return lax.ppermute(x, axis, pairs if up else [(j, i) for i, j in pairs])


def put_blocks(blocks, c, green):
    orb = green.shape[-1]
    for e in range(green.shape[0]):
        for a in range(green.shape[1]):
            high, low = halves(green[e, a])
            blocks[c, a, e, :, :orb] = high
            blocks[c, a, e, :, orb:] = low


def add_pairs(group, neighbours, phonon, coupling, blocks, totals, picked, size):
    atoms, slots, orb = coupling.shape[0], coupling.shape[1], coupling.shape[-1]
    e_local = blocks.shape[2]
    index = lax.axis_index("atom")
    base = index * atoms
    if group != OWN:
        upper = (index & 1) == (0 if group == PAIR else 1)
        base += jnp.where(upper, atoms, -atoms)

    found = jnp.int32(0)
    for a in range(atoms):
        for j in range(slots):
            picked[found] = a * slots + j
            b = neighbours[a, j] - base
            found += ((b >= 0) & (b < atoms)).astype(jnp.int32)

    def batch(step, _):
        pairs = []
        for u in range(size):
            at = step * size + u
            item = picked[jnp.minimum(at, found - 1)]
            a = item // slots
            j = item - a * slots
            high, low = halves(coupling[a, j])
            left = jnp.concatenate([high, low], 1)
            right = jnp.concatenate(
                [jnp.concatenate([high, high], 1), jnp.concatenate([low, low], 1)], 0
            )
            pairs.append((a, j, neighbours[a, j] - base, jnp.where(at < found, 1.0, 0.0), left, right))
        inners = []
        for a, j, b, live, left, right in pairs:
            for c in range(len(totals)):
                near = blocks[c, b].reshape(e_local * orb, 2 * orb)
                inner = lax.dot_general(
                    near, right, (((1,), (1,)), ((), ())), preferred_element_type=jnp.float32
                )
                inners.append(inner[:, :orb] + inner[:, orb:])
        results = []
        for a, j, b, live, left, right in pairs:
            for total in totals:
                inner = inners.pop(0)
                sums = [None] * (e_local + 2 * REACH)
                for e in range(e_local):
                    high, low = halves(inner[e * orb : (e + 1) * orb])
                    both = jnp.concatenate([high, low], 1)
                    outer = jnp.dot(
                        left, jnp.concatenate([both, both], 0), preferred_element_type=jnp.float32
                    )
                    outer = outer[:, :orb] + outer[:, orb:]
                    for k, s in enumerate(SHIFTS):
                        d = e - s + REACH
                        term = (phonon[a, k, j] * live) * outer
                        sums[d] = term if sums[d] is None else sums[d] + term
                results.append((total, a, sums))
        for total, a, sums in results:
            for d, value in enumerate(sums):
                if value is not None:
                    total[d, a] += value

    lax.fori_loop(0, (found + size - 1) // size, batch, None)


def part_kernel(green, first, second, sems):
    copies = [
        pltpu.make_async_copy(green.at[c], part, sems.at[c]) for c, part in enumerate((first, second))
    ]
    for copy in copies:
        copy.start()
    for copy in copies:
        copy.wait()


def own_kernel(neighbours, phonon, coupling, green0, green1, total0, total1, blocks, picked):
    for c, (green, total) in enumerate(((green0, total0), (green1, total1))):
        put_blocks(blocks, c, green)
        total[...] = jnp.zeros_like(total)
    add_pairs(OWN, neighbours, phonon, coupling, blocks, (total0, total1), picked, 2)


def pair_kernel(neighbours, phonon, coupling, ahead, before, total, blocks, picked):
    total[...] = before[...]
    put_blocks(blocks, 0, ahead)
    add_pairs(PAIR, neighbours, phonon, coupling, blocks, (total,), picked, 4)


def turn_kernel(
    neighbours, phonon, coupling, ahead, before, green0, green1, by_core, by_cross,
    total, turned, blocks, picked,
):
    e_local, a_local = green0.shape[0], green0.shape[1]
    core, cross = partner_energies(turned.shape[1])
    for c, green in enumerate((green0, green1)):
        for a in range(a_local):
            for e in range(e_local):
                turned[c, REACH + e, a] = green[e, a].T
            for e in range(REACH):
                turned[c, core + e, a] = by_core[c, e, a].T
                turned[c, cross + e, a] = by_cross[c, e, a].T
    pair_kernel(neighbours, phonon, coupling, ahead, before, total, blocks, picked)


def partner_energies(spread):
    odd = lax.axis_index("energy") & 1
    return jnp.where(odd == 0, spread - REACH, 0), jnp.where(odd == 0, 0, spread - REACH)


def finish(total, core, cross):
    to_core, to_cross = partner_energies(total.shape[0])
    for e in range(REACH):
        core[e] = total[to_core + e]
        cross[e] = total[to_cross + e]


def rate_sums(total, turned, c, a):
    sums = total[0, a] * turned[c, 0, a]
    for d in range(1, total.shape[0]):
        sums += total[d, a] * turned[c, d, a]
    return sums


def far_kernel(
    neighbours, phonon, coupling, across, before, turned, total, core, cross, partial, blocks, picked
):
    pair_kernel_far(neighbours, phonon, coupling, across, before, total, blocks, picked)
    finish(total, core, cross)
    for a in range(partial.shape[0]):
        partial[a] = rate_sums(total, turned, 0, a)


def pair_kernel_far(neighbours, phonon, coupling, across, before, total, blocks, picked):
    total[...] = before[...]
    put_blocks(blocks, 0, across)
    add_pairs(FAR, neighbours, phonon, coupling, blocks, (total,), picked, 4)


def last_kernel(
    scale, neighbours, phonon, coupling, across, before, turned, partial,
    total, core, cross, rate, blocks, picked,
):
    pair_kernel_far(neighbours, phonon, coupling, across, before, total, blocks, picked)
    finish(total, core, cross)
    for a in range(partial.shape[0]):
        sums = partial[a] - rate_sums(total, turned, 1, a)
        rate[a : a + 1, :] = jnp.sum(sums.T, axis=0, keepdims=True) * scale


def addends(x, axis):
    size = lax.axis_size(axis)
    if size > FEW:
        return [lax.psum(x, axis)]
    turns = [[(i, (i + k) % size) for i in range(size)] for k in range(1, size)]
    return [x] + [lax.ppermute(x, axis, turn) for turn in turns]


def end_kernel(total0, total1, cross0, core0, cross1, core1, *rest):
    *rates, out, rate = rest
    e_local = out.shape[1]
    for c, (total, cross, core) in enumerate(((total0, cross0, core0), (total1, cross1, core1))):
        for e in range(e_local):
            out[c, e] = total[REACH + e] + core[e] + cross[e]
    rate[...] = sum(r[...] for r in rates)


def per_device(green, coupling, phonon, neighbours):
    _, e_local, a_local, orb, _ = green.shape
    points = e_local * lax.axis_size("energy")
    spread = (e_local + 2 * REACH, a_local, orb, orb)
    edge = (REACH, a_local, orb, orb)

    def call(kernel, out, operands, parts=1):
        return pl.pallas_call(
            kernel,
            out_shape=[jax.ShapeDtypeStruct(shape, jnp.float32) for shape in out],
            in_specs=[SMEM, SMEM] + [VMEM] * (1 + len(operands)),
            out_specs=[VMEM] * len(out),
            scratch_shapes=[
                pltpu.VMEM((parts, a_local, e_local, orb, 2 * orb), jnp.bfloat16),
                pltpu.SMEM((a_local * neighbours.shape[1] + 1,), jnp.int32),
            ],
            compiler_params=pltpu.CompilerParams(vmem_limit_bytes=24 * 2**20),
            cost_estimate=pl.CostEstimate(flops=10**6, bytes_accessed=10**4, transcendentals=0),
        )(neighbours, jnp.swapaxes(phonon, 1, 2), coupling, *operands)

    green0, green1 = pl.pallas_call(
        part_kernel,
        out_shape=[jax.ShapeDtypeStruct(green.shape[1:], green.dtype)] * 2,
        in_specs=[HBM],
        out_specs=[VMEM] * 2,
        scratch_shapes=[pltpu.SemaphoreType.DMA((2,))],
        compiler_params=pltpu.CompilerParams(vmem_limit_bytes=24 * 2**20),
    )(green)
    ahead1 = swap(green1, "atom", 0)
    ahead0 = swap(green0, "atom", 0)
    total0, total1 = call(own_kernel, [spread] * 2, (green0, green1), parts=2)
    ahead0, total0, total1 = lax.optimization_barrier((ahead0, total0, total1))
    across0 = forward(ahead0, "atom")
    (total0,) = call(pair_kernel, [spread], (ahead0, total0))
    ahead1, total0 = lax.optimization_barrier((ahead1, total0))
    across1 = forward(ahead1, "atom")
    by_core, by_cross = swap(green, "energy", 0), swap(green, "energy", 1)
    total1, turned = call(
        turn_kernel, [spread, (2,) + spread], (ahead1, total1, green0, green1, by_core, by_cross)
    )
    total0, core0, cross0, partial = call(
        far_kernel, [spread, edge, edge, (a_local, orb, orb)], (across0, total0, turned)
    )
    core0, cross0 = swap(core0, "energy", 0), swap(cross0, "energy", 1)
    total1, core1, cross1, rate = call(
        functools.partial(last_kernel, 1.0 / (4.0 * points)),
        [spread, edge, edge, (a_local, orb)],
        (across1, total1, turned, partial),
    )
    core1, cross1 = swap(core1, "energy", 0), swap(cross1, "energy", 1)
    cross0, core0, rate = lax.optimization_barrier((cross0, core0, rate))
    rates = addends(rate, "energy")
    return pl.pallas_call(
        end_kernel,
        out_shape=[
            jax.ShapeDtypeStruct(green.shape, jnp.float32),
            jax.ShapeDtypeStruct((a_local, orb), jnp.float32),
        ],
        in_specs=[VMEM] * (6 + len(rates)),
        out_specs=[VMEM] * 2,
        compiler_params=pltpu.CompilerParams(vmem_limit_bytes=24 * 2**20),
        cost_estimate=pl.CostEstimate(flops=10**6, bytes_accessed=2 * 10**6, transcendentals=0),
    )(total0, total1, cross0, core0, cross1, core1, *rates)


def solution(mesh):
    return jax.shard_map(
        per_device,
        mesh=mesh,
        in_specs=(
            P(None, "energy", "atom", None, None),
            P("atom", None, None, None),
            P("atom", None, None),
            P("atom", None),
        ),
        out_specs=(P(None, "energy", "atom", None, None), P("atom", None)),
        check_vma=False,
    )
```

```python
import functools

import jax
import jax.numpy as jnp
from jax import lax
from jax.experimental import pallas as pl
from jax.experimental.pallas import tpu as pltpu
from jax.sharding import PartitionSpec as P

SHIFTS = (-2, -1, 1, 2)
REACH = max(SHIFTS)
OWN, PAIR, FAR = 0, 1, 2
FEW = 4
VMEM = pl.BlockSpec(memory_space=pltpu.VMEM)
SMEM = pl.BlockSpec(memory_space=pltpu.SMEM)
ANY = pl.BlockSpec(memory_space=pl.ANY)


def halves(x):
    high = x.astype(jnp.bfloat16)
    return high, (x - high.astype(jnp.float32)).astype(jnp.bfloat16)


def swap(x, axis, first):
    low = range(first, lax.axis_size(axis) - 1, 2)
    return lax.ppermute(x, axis, [(i, i + 1) for i in low] + [(i + 1, i) for i in low])


def leap(x, axis, first):
    size = lax.axis_size(axis)
    ups = [(i, i + 2) for i in range(first, size - 2, 2)]
    downs = [(i + 2, i) for i in range(1 - first, size - 2, 2)]
    return lax.ppermute(x, axis, ups + downs)


def shift(x, axis, up):
    pairs = [(i, i + 1) for i in range(lax.axis_size(axis) - 1)]
    return lax.ppermute(x, axis, pairs if up else [(j, i) for i, j in pairs])


def put_blocks(blocks, c, green):
    orb = green.shape[-1]
    for e in range(green.shape[0]):
        for a in range(green.shape[1]):
            high, low = halves(green[e, a])
            blocks[c, a, e, :, :orb] = high
            blocks[c, a, e, :, orb:] = low


def add_pairs(group, neighbours, phonon, coupling, blocks, totals, picked, size):
    atoms, slots, orb = coupling.shape[0], coupling.shape[1], coupling.shape[-1]
    e_local = blocks.shape[2]
    index = lax.axis_index("atom")
    base = index * atoms
    if group != OWN:
        upper = (index & 1) == (0 if group == PAIR else 1)
        base += jnp.where(upper, atoms, -atoms)

    found = jnp.int32(0)
    for a in range(atoms):
        for j in range(slots):
            picked[found] = a * slots + j
            b = neighbours[a, j] - base
            found += ((b >= 0) & (b < atoms)).astype(jnp.int32)

    def batch(step, _):
        pairs = []
        for u in range(size):
            at = step * size + u
            item = picked[jnp.minimum(at, found - 1)]
            a = item // slots
            j = item - a * slots
            high, low = halves(coupling[a, j])
            left = jnp.concatenate([high, low], 1)
            right = jnp.concatenate(
                [jnp.concatenate([high, high], 1), jnp.concatenate([low, low], 1)], 0
            )
            pairs.append((a, j, neighbours[a, j] - base, jnp.where(at < found, 1.0, 0.0), left, right))
        inners = []
        for a, j, b, live, left, right in pairs:
            for c in range(len(totals)):
                near = blocks[c, b].reshape(e_local * orb, 2 * orb)
                inner = lax.dot_general(
                    near, right, (((1,), (1,)), ((), ())), preferred_element_type=jnp.float32
                )
                inners.append(inner[:, :orb] + inner[:, orb:])
        results = []
        for a, j, b, live, left, right in pairs:
            for total in totals:
                inner = inners.pop(0)
                sums = [None] * (e_local + 2 * REACH)
                for e in range(e_local):
                    high, low = halves(inner[e * orb : (e + 1) * orb])
                    both = jnp.concatenate([high, low], 1)
                    outer = jnp.dot(
                        left, jnp.concatenate([both, both], 0), preferred_element_type=jnp.float32
                    )
                    outer = outer[:, :orb] + outer[:, orb:]
                    for k, s in enumerate(SHIFTS):
                        d = e - s + REACH
                        term = (phonon[a, k, j] * live) * outer
                        sums[d] = term if sums[d] is None else sums[d] + term
                results.append((total, a, sums))
        for total, a, sums in results:
            for d, value in enumerate(sums):
                if value is not None:
                    total[d, a] += value

    lax.fori_loop(0, (found + size - 1) // size, batch, None)


def part_kernel(c, whole, part, sem):
    copy = pltpu.make_async_copy(whole.at[c], part, sem)
    copy.start()
    copy.wait()


def own_kernel(neighbours, phonon, coupling, green, total0, total1, blocks, picked):
    for c, total in enumerate((total0, total1)):
        put_blocks(blocks, c, green.at[c])
        total[...] = jnp.zeros_like(total)
    add_pairs(OWN, neighbours, phonon, coupling, blocks, (total0, total1), picked, 2)


def pair_kernel(
    neighbours, phonon, coupling, ahead, before0, before1, total0, total1, blocks, picked
):
    for c, (before, total) in enumerate(((before0, total0), (before1, total1))):
        put_blocks(blocks, c, ahead.at[c])
        total[...] = before[...]
    add_pairs(PAIR, neighbours, phonon, coupling, blocks, (total0, total1), picked, 2)


def turn_kernel(green, by_core, by_cross, turned):
    e_local, a_local = green.shape[1], green.shape[2]
    core, cross = partner_energies(turned.shape[1])
    for c in range(2):
        for a in range(a_local):
            for e in range(e_local):
                turned[c, REACH + e, a] = green[c, e, a].T
            for e in range(REACH):
                turned[c, core + e, a] = by_core[c, e, a].T
                turned[c, cross + e, a] = by_cross[c, e, a].T


def partner_energies(spread):
    odd = lax.axis_index("energy") & 1
    return jnp.where(odd == 0, spread - REACH, 0), jnp.where(odd == 0, 0, spread - REACH)


def far_kernel(
    scale, neighbours, phonon, coupling, across0, across1, turned, before0, before1,
    own, core, cross, rate, total0, total1, blocks, picked,
):
    e_local, a_local = own.shape[1], own.shape[2]
    total0[...] = before0[...]
    total1[...] = before1[...]
    put_blocks(blocks, 0, across0)
    put_blocks(blocks, 1, across1)
    add_pairs(FAR, neighbours, phonon, coupling, blocks, (total0, total1), picked, 2)
    to_core, to_cross = partner_energies(total0.shape[0])
    for c, total in enumerate((total0, total1)):
        for e in range(REACH):
            core[c, e] = total[to_core + e]
            cross[c, e] = total[to_cross + e]
        for e in range(e_local):
            own[c, e] = total[REACH + e]
    for a in range(a_local):
        sums = total0[0, a] * turned[0, 0, a] - total1[0, a] * turned[1, 0, a]
        for d in range(1, total0.shape[0]):
            sums += total0[d, a] * turned[0, d, a] - total1[d, a] * turned[1, d, a]
        rate[a : a + 1, :] = jnp.sum(sums.T, axis=0, keepdims=True) * scale


def addends(x, axis):
    size = lax.axis_size(axis)
    if size > FEW:
        return [lax.psum(x, axis)]
    turns = [[(i, (i + k) % size) for i in range(size)] for k in range(1, size)]
    return [x] + [lax.ppermute(x, axis, turn) for turn in turns]


def end_kernel(own, cross, core, *rest):
    *rates, out, rate = rest
    out[...] = own[...] + core[...] + cross[...]
    rate[...] = sum(r[...] for r in rates)


def per_device(green, coupling, phonon, neighbours):
    _, e_local, a_local, orb, _ = green.shape
    points = e_local * lax.axis_size("energy")
    spread = (e_local + 2 * REACH, a_local, orb, orb)
    edge = (2, REACH, a_local, orb, orb)

    def call(kernel, out, operands, parts=1, scratch=()):
        return pl.pallas_call(
            kernel,
            out_shape=[jax.ShapeDtypeStruct(shape, jnp.float32) for shape in out],
            in_specs=[SMEM, SMEM] + [VMEM] * (1 + len(operands)),
            out_specs=[VMEM] * len(out),
            scratch_shapes=list(scratch)
            + [
                pltpu.VMEM((parts, a_local, e_local, orb, 2 * orb), jnp.bfloat16),
                pltpu.SMEM((a_local * neighbours.shape[1] + 1,), jnp.int32),
            ],
            compiler_params=pltpu.CompilerParams(vmem_limit_bytes=24 * 2**20),
            cost_estimate=pl.CostEstimate(flops=10**6, bytes_accessed=10**4, transcendentals=0),
        )(neighbours, jnp.swapaxes(phonon, 1, 2), coupling, *operands)

    def part(x, c):
        return pl.pallas_call(
            functools.partial(part_kernel, c),
            out_shape=jax.ShapeDtypeStruct(x.shape[1:], x.dtype),
            in_specs=[ANY],
            out_specs=VMEM,
            scratch_shapes=[pltpu.SemaphoreType.DMA(())],
            compiler_params=pltpu.CompilerParams(vmem_limit_bytes=24 * 2**20),
        )(x)

    ahead = swap(green, "atom", 0)
    straight1 = leap(part(green, 1), "atom", 1)
    by_core, by_cross = swap(green, "energy", 0), swap(green, "energy", 1)
    total0, total1 = call(own_kernel, [spread] * 2, (green,), parts=2)
    ahead, straight1, total0, total1 = lax.optimization_barrier((ahead, straight1, total0, total1))
    across0 = leap(part(ahead, 0), "atom", 0)
    across1 = swap(straight1, "atom", 0)
    total0, total1 = call(
        pair_kernel, [spread] * 2, (ahead, total0, total1), parts=2
    )
    by_core, by_cross, total0 = lax.optimization_barrier((by_core, by_cross, total0))
    turned = pl.pallas_call(
        turn_kernel,
        out_shape=jax.ShapeDtypeStruct((2,) + spread, jnp.float32),
        in_specs=[VMEM] * 3,
        out_specs=VMEM,
        compiler_params=pltpu.CompilerParams(vmem_limit_bytes=24 * 2**20),
        cost_estimate=pl.CostEstimate(flops=10**6, bytes_accessed=10**4, transcendentals=0),
    )(green, by_core, by_cross)
    own, core, cross, rate = call(
        functools.partial(far_kernel, 1.0 / (4.0 * points)),
        [green.shape, edge, edge, (a_local, orb)],
        (across0, across1, turned, total0, total1),
        parts=2,
        scratch=[pltpu.VMEM(spread, jnp.float32)] * 2,
    )
    core, cross = swap(core, "energy", 0), swap(cross, "energy", 1)
    rates = addends(rate, "energy")
    return pl.pallas_call(
        end_kernel,
        out_shape=[
            jax.ShapeDtypeStruct(green.shape, jnp.float32),
            jax.ShapeDtypeStruct((a_local, orb), jnp.float32),
        ],
        in_specs=[VMEM] * (3 + len(rates)),
        out_specs=[VMEM] * 2,
        compiler_params=pltpu.CompilerParams(vmem_limit_bytes=24 * 2**20),
        cost_estimate=pl.CostEstimate(flops=10**6, bytes_accessed=2 * 10**6, transcendentals=0),
    )(own, cross, core, *rates)


def solution(mesh):
    return jax.shard_map(
        per_device,
        mesh=mesh,
        in_specs=(
            P(None, "energy", "atom", None, None),
            P("atom", None, None, None),
            P("atom", None, None),
            P("atom", None),
        ),
        out_specs=(P(None, "energy", "atom", None, None), P("atom", None)),
        check_vma=False,
    )
```

```python
import functools

import jax
import jax.numpy as jnp
from jax import lax
from jax.experimental import pallas as pl
from jax.experimental.pallas import tpu as pltpu
from jax.sharding import PartitionSpec as P

SHIFTS = (-2, -1, 1, 2)
REACH = max(SHIFTS)
OWN, PAIR, FAR = 0, 1, 2
FEW = 4
VMEM = pl.BlockSpec(memory_space=pltpu.VMEM)
SMEM = pl.BlockSpec(memory_space=pltpu.SMEM)
HBM = pl.BlockSpec(memory_space=pltpu.HBM)


def halves(x):
    high = x.astype(jnp.bfloat16)
    return high, (x - high.astype(jnp.float32)).astype(jnp.bfloat16)


def swap(x, axis, first):
    low = range(first, lax.axis_size(axis) - 1, 2)
    return lax.ppermute(x, axis, [(i, i + 1) for i in low] + [(i + 1, i) for i in low])


def leap(x, axis, first):
    size = lax.axis_size(axis)
    ups = [(i, i + 2) for i in range(first, size - 2, 2)]
    downs = [(i + 2, i) for i in range(1 - first, size - 2, 2)]
    return lax.ppermute(x, axis, ups + downs)


def put_blocks(blocks, c, green):
    orb = green.shape[-1]
    for e in range(green.shape[0]):
        for a in range(green.shape[1]):
            high, low = halves(green[e, a])
            blocks[c, a, e, :, :orb] = high
            blocks[c, a, e, :, orb:] = low


def add_pairs(group, neighbours, phonon, coupling, blocks, totals, picked, size):
    atoms, slots, orb = coupling.shape[0], coupling.shape[1], coupling.shape[-1]
    e_local = blocks.shape[2]
    index = lax.axis_index("atom")
    base = index * atoms
    if group != OWN:
        upper = (index & 1) == (0 if group == PAIR else 1)
        base += jnp.where(upper, atoms, -atoms)

    found = jnp.int32(0)
    for a in range(atoms):
        for j in range(slots):
            picked[found] = a * slots + j
            b = neighbours[a, j] - base
            found += ((b >= 0) & (b < atoms)).astype(jnp.int32)

    def batch(step, _):
        pairs = []
        for u in range(size):
            at = step * size + u
            item = picked[jnp.minimum(at, found - 1)]
            a = item // slots
            j = item - a * slots
            high, low = halves(coupling[a, j])
            left = jnp.concatenate([high, low], 1)
            right = jnp.concatenate(
                [jnp.concatenate([high, high], 1), jnp.concatenate([low, low], 1)], 0
            )
            pairs.append((a, j, neighbours[a, j] - base, jnp.where(at < found, 1.0, 0.0), left, right))
        inners = []
        for a, j, b, live, left, right in pairs:
            for c in range(len(totals)):
                near = blocks[c, b].reshape(e_local * orb, 2 * orb)
                inner = lax.dot_general(
                    near, right, (((1,), (1,)), ((), ())), preferred_element_type=jnp.float32
                )
                inners.append(inner[:, :orb] + inner[:, orb:])
        results = []
        for a, j, b, live, left, right in pairs:
            for total in totals:
                inner = inners.pop(0)
                sums = [None] * (e_local + 2 * REACH)
                for e in range(e_local):
                    high, low = halves(inner[e * orb : (e + 1) * orb])
                    both = jnp.concatenate([high, low], 1)
                    outer = jnp.dot(
                        left, jnp.concatenate([both, both], 0), preferred_element_type=jnp.float32
                    )
                    outer = outer[:, :orb] + outer[:, orb:]
                    for k, s in enumerate(SHIFTS):
                        d = e - s + REACH
                        term = (phonon[a, k, j] * live) * outer
                        sums[d] = term if sums[d] is None else sums[d] + term
                results.append((total, a, sums))
        for total, a, sums in results:
            for d, value in enumerate(sums):
                if value is not None:
                    total[d, a] += value

    lax.fori_loop(0, (found + size - 1) // size, batch, None)


def part_kernel(green, first, second, sems):
    copies = [
        pltpu.make_async_copy(green.at[c], part, sems.at[c]) for c, part in enumerate((first, second))
    ]
    for copy in copies:
        copy.start()
    for copy in copies:
        copy.wait()


def own_kernel(neighbours, phonon, coupling, green0, green1, total0, total1, blocks, picked):
    for c, (green, total) in enumerate(((green0, total0), (green1, total1))):
        put_blocks(blocks, c, green)
        total[...] = jnp.zeros_like(total)
    add_pairs(OWN, neighbours, phonon, coupling, blocks, (total0, total1), picked, 2)


def pair_kernel(neighbours, phonon, coupling, ahead, before, total, blocks, picked):
    total[...] = before[...]
    put_blocks(blocks, 0, ahead)
    add_pairs(PAIR, neighbours, phonon, coupling, blocks, (total,), picked, 4)


def turn_kernel(
    neighbours, phonon, coupling, ahead, before, green0, green1, by_core, by_cross,
    total, turned, blocks, picked,
):
    e_local, a_local = green0.shape[0], green0.shape[1]
    core, cross = partner_energies(turned.shape[1])
    for c, green in enumerate((green0, green1)):
        for a in range(a_local):
            for e in range(e_local):
                turned[c, REACH + e, a] = green[e, a].T
            for e in range(REACH):
                turned[c, core + e, a] = by_core[c, e, a].T
                turned[c, cross + e, a] = by_cross[c, e, a].T
    pair_kernel(neighbours, phonon, coupling, ahead, before, total, blocks, picked)


def partner_energies(spread):
    odd = lax.axis_index("energy") & 1
    return jnp.where(odd == 0, spread - REACH, 0), jnp.where(odd == 0, 0, spread - REACH)


def finish(total, core, cross):
    to_core, to_cross = partner_energies(total.shape[0])
    for e in range(REACH):
        core[e] = total[to_core + e]
        cross[e] = total[to_cross + e]


def rate_sums(total, turned, c, a):
    sums = total[0, a] * turned[c, 0, a]
    for d in range(1, total.shape[0]):
        sums += total[d, a] * turned[c, d, a]
    return sums


def far_kernel(
    neighbours, phonon, coupling, across, before, turned, total, core, cross, partial, blocks, picked
):
    pair_kernel_far(neighbours, phonon, coupling, across, before, total, blocks, picked)
    finish(total, core, cross)
    for a in range(partial.shape[0]):
        partial[a] = rate_sums(total, turned, 0, a)


def pair_kernel_far(neighbours, phonon, coupling, across, before, total, blocks, picked):
    total[...] = before[...]
    put_blocks(blocks, 0, across)
    add_pairs(FAR, neighbours, phonon, coupling, blocks, (total,), picked, 4)


def last_kernel(
    scale, neighbours, phonon, coupling, across, before, turned, partial,
    total, core, cross, rate, blocks, picked,
):
    pair_kernel_far(neighbours, phonon, coupling, across, before, total, blocks, picked)
    finish(total, core, cross)
    for a in range(partial.shape[0]):
        sums = partial[a] - rate_sums(total, turned, 1, a)
        rate[a : a + 1, :] = jnp.sum(sums.T, axis=0, keepdims=True) * scale


def addends(x, axis):
    size = lax.axis_size(axis)
    if size > FEW:
        return [lax.psum(x, axis)]
    turns = [[(i, (i + k) % size) for i in range(size)] for k in range(1, size)]
    return [x] + [lax.ppermute(x, axis, turn) for turn in turns]


def end_kernel(total0, total1, cross0, core0, cross1, core1, *rest):
    *rates, out, rate = rest
    e_local = out.shape[1]
    for c, (total, cross, core) in enumerate(((total0, cross0, core0), (total1, cross1, core1))):
        for e in range(e_local):
            out[c, e] = total[REACH + e] + core[e] + cross[e]
    rate[...] = sum(r[...] for r in rates)


def per_device(green, coupling, phonon, neighbours):
    _, e_local, a_local, orb, _ = green.shape
    points = e_local * lax.axis_size("energy")
    spread = (e_local + 2 * REACH, a_local, orb, orb)
    edge = (REACH, a_local, orb, orb)

    def call(kernel, out, operands, parts=1):
        return pl.pallas_call(
            kernel,
            out_shape=[jax.ShapeDtypeStruct(shape, jnp.float32) for shape in out],
            in_specs=[SMEM, SMEM] + [VMEM] * (1 + len(operands)),
            out_specs=[VMEM] * len(out),
            scratch_shapes=[
                pltpu.VMEM((parts, a_local, e_local, orb, 2 * orb), jnp.bfloat16),
                pltpu.SMEM((a_local * neighbours.shape[1] + 1,), jnp.int32),
            ],
            compiler_params=pltpu.CompilerParams(vmem_limit_bytes=24 * 2**20),
            cost_estimate=pl.CostEstimate(flops=10**6, bytes_accessed=10**4, transcendentals=0),
        )(neighbours, jnp.swapaxes(phonon, 1, 2), coupling, *operands)

    green0, green1 = pl.pallas_call(
        part_kernel,
        out_shape=[jax.ShapeDtypeStruct(green.shape[1:], green.dtype)] * 2,
        in_specs=[HBM],
        out_specs=[VMEM] * 2,
        scratch_shapes=[pltpu.SemaphoreType.DMA((2,))],
        compiler_params=pltpu.CompilerParams(vmem_limit_bytes=24 * 2**20),
    )(green)
    ahead0 = swap(green0, "atom", 0)
    straight1 = leap(green1, "atom", 1)
    by_core, by_cross = swap(green, "energy", 0), swap(green, "energy", 1)
    ahead1 = swap(green1, "atom", 0)
    total0, total1 = call(own_kernel, [spread] * 2, (green0, green1), parts=2)
    ahead0, total0, total1 = lax.optimization_barrier((ahead0, total0, total1))
    across0 = leap(ahead0, "atom", 0)
    across1 = swap(straight1, "atom", 0)
    (total0,) = call(pair_kernel, [spread], (ahead0, total0))
    ahead1, total0 = lax.optimization_barrier((ahead1, total0))
    total1, turned = call(
        turn_kernel, [spread, (2,) + spread], (ahead1, total1, green0, green1, by_core, by_cross)
    )
    total0, core0, cross0, partial = call(
        far_kernel, [spread, edge, edge, (a_local, orb, orb)], (across0, total0, turned)
    )
    core0, cross0 = swap(core0, "energy", 0), swap(cross0, "energy", 1)
    total1, core1, cross1, rate = call(
        functools.partial(last_kernel, 1.0 / (4.0 * points)),
        [spread, edge, edge, (a_local, orb)],
        (across1, total1, turned, partial),
    )
    core1, cross1 = swap(core1, "energy", 0), swap(cross1, "energy", 1)
    cross0, core0, rate = lax.optimization_barrier((cross0, core0, rate))
    rates = addends(rate, "energy")
    return pl.pallas_call(
        end_kernel,
        out_shape=[
            jax.ShapeDtypeStruct(green.shape, jnp.float32),
            jax.ShapeDtypeStruct((a_local, orb), jnp.float32),
        ],
        in_specs=[VMEM] * (6 + len(rates)),
        out_specs=[VMEM] * 2,
        compiler_params=pltpu.CompilerParams(vmem_limit_bytes=24 * 2**20),
        cost_estimate=pl.CostEstimate(flops=10**6, bytes_accessed=2 * 10**6, transcendentals=0),
    )(total0, total1, cross0, core0, cross1, core1, *rates)


def solution(mesh):
    return jax.shard_map(
        per_device,
        mesh=mesh,
        in_specs=(
            P(None, "energy", "atom", None, None),
            P("atom", None, None, None),
            P("atom", None, None),
            P("atom", None),
        ),
        out_specs=(P(None, "energy", "atom", None, None), P("atom", None)),
        check_vma=False,
    )
```

```python
import functools

import jax
import jax.numpy as jnp
from jax import lax
from jax.experimental import pallas as pl
from jax.experimental.pallas import tpu as pltpu
from jax.sharding import PartitionSpec as P

SHIFTS = (-2, -1, 1, 2)
REACH = max(SHIFTS)
OWN, PAIR, FAR = 0, 1, 2
FEW = 4
VMEM = pl.BlockSpec(memory_space=pltpu.VMEM)
SMEM = pl.BlockSpec(memory_space=pltpu.SMEM)
ANY = pl.BlockSpec(memory_space=pl.ANY)


def halves(x):
    high = x.astype(jnp.bfloat16)
    return high, (x - high.astype(jnp.float32)).astype(jnp.bfloat16)


def swap(x, axis, first):
    low = range(first, lax.axis_size(axis) - 1, 2)
    return lax.ppermute(x, axis, [(i, i + 1) for i in low] + [(i + 1, i) for i in low])


def forward(x, axis):
    size = lax.axis_size(axis)
    ups = [(i, i + 2) for i in range(0, size - 2, 2)]
    downs = [(i + 2, i) for i in range(1, size - 2, 2)]
    return lax.ppermute(x, axis, ups + downs)


def shift(x, axis, up):
    pairs = [(i, i + 1) for i in range(lax.axis_size(axis) - 1)]
    return lax.ppermute(x, axis, pairs if up else [(j, i) for i, j in pairs])


def put_blocks(blocks, c, green):
    orb = green.shape[-1]
    for e in range(green.shape[0]):
        for a in range(green.shape[1]):
            high, low = halves(green[e, a])
            blocks[c, a, e, :, :orb] = high
            blocks[c, a, e, :, orb:] = low


def add_pairs(group, neighbours, phonon, coupling, blocks, totals, picked, size):
    atoms, slots, orb = coupling.shape[0], coupling.shape[1], coupling.shape[-1]
    e_local = blocks.shape[2]
    index = lax.axis_index("atom")
    base = index * atoms
    if group != OWN:
        upper = (index & 1) == (0 if group == PAIR else 1)
        base += jnp.where(upper, atoms, -atoms)

    found = jnp.int32(0)
    for a in range(atoms):
        for j in range(slots):
            picked[found] = a * slots + j
            b = neighbours[a, j] - base
            found += ((b >= 0) & (b < atoms)).astype(jnp.int32)

    def batch(step, _):
        pairs = []
        for u in range(size):
            at = step * size + u
            item = picked[jnp.minimum(at, found - 1)]
            a = item // slots
            j = item - a * slots
            high, low = halves(coupling[a, j])
            left = jnp.concatenate([high, low], 1)
            right = jnp.concatenate(
                [jnp.concatenate([high, high], 1), jnp.concatenate([low, low], 1)], 0
            )
            pairs.append((a, j, neighbours[a, j] - base, jnp.where(at < found, 1.0, 0.0), left, right))
        inners = []
        for a, j, b, live, left, right in pairs:
            for c in range(len(totals)):
                near = blocks[c, b].reshape(e_local * orb, 2 * orb)
                inner = lax.dot_general(
                    near, right, (((1,), (1,)), ((), ())), preferred_element_type=jnp.float32
                )
                inners.append(inner[:, :orb] + inner[:, orb:])
        results = []
        for a, j, b, live, left, right in pairs:
            for total in totals:
                inner = inners.pop(0)
                sums = [None] * (e_local + 2 * REACH)
                for e in range(e_local):
                    high, low = halves(inner[e * orb : (e + 1) * orb])
                    both = jnp.concatenate([high, low], 1)
                    outer = jnp.dot(
                        left, jnp.concatenate([both, both], 0), preferred_element_type=jnp.float32
                    )
                    outer = outer[:, :orb] + outer[:, orb:]
                    for k, s in enumerate(SHIFTS):
                        d = e - s + REACH
                        term = (phonon[a, k, j] * live) * outer
                        sums[d] = term if sums[d] is None else sums[d] + term
                results.append((total, a, sums))
        for total, a, sums in results:
            for d, value in enumerate(sums):
                if value is not None:
                    total[d, a] += value

    lax.fori_loop(0, (found + size - 1) // size, batch, None)


def fetch_kernel(green, coupling, phonon, neighbours, *rest):
    *results, sems = rest
    sources = [green.at[0], green.at[1], green, coupling, phonon, neighbours]
    copies = [
        pltpu.make_async_copy(source, result, sems.at[i])
        for i, (source, result) in enumerate(zip(sources, results))
    ]
    for copy in copies:
        copy.start()
    for copy in copies:
        copy.wait()


def own_kernel(neighbours, phonon, coupling, green0, green1, total0, total1, blocks, picked):
    for c, (green, total) in enumerate(((green0, total0), (green1, total1))):
        put_blocks(blocks, c, green)
        total[...] = jnp.zeros_like(total)
    add_pairs(OWN, neighbours, phonon, coupling, blocks, (total0, total1), picked, 2)


def pair_kernel(neighbours, phonon, coupling, ahead, before, total, blocks, picked):
    total[...] = before[...]
    put_blocks(blocks, 0, ahead)
    add_pairs(PAIR, neighbours, phonon, coupling, blocks, (total,), picked, 4)


def turn_kernel(
    neighbours, phonon, coupling, ahead, before, green0, green1, by_core, by_cross,
    total, turned, blocks, picked,
):
    e_local, a_local = green0.shape[0], green0.shape[1]
    core, cross = partner_energies(turned.shape[1])
    for c, green in enumerate((green0, green1)):
        for a in range(a_local):
            for e in range(e_local):
                turned[c, REACH + e, a] = green[e, a].T
            for e in range(REACH):
                turned[c, core + e, a] = by_core[c, e, a].T
                turned[c, cross + e, a] = by_cross[c, e, a].T
    pair_kernel(neighbours, phonon, coupling, ahead, before, total, blocks, picked)


def partner_energies(spread):
    odd = lax.axis_index("energy") & 1
    return jnp.where(odd == 0, spread - REACH, 0), jnp.where(odd == 0, 0, spread - REACH)


def finish(total, core, cross):
    to_core, to_cross = partner_energies(total.shape[0])
    for e in range(REACH):
        core[e] = total[to_core + e]
        cross[e] = total[to_cross + e]


def rate_sums(total, turned, c, a):
    sums = total[0, a] * turned[c, 0, a]
    for d in range(1, total.shape[0]):
        sums += total[d, a] * turned[c, d, a]
    return sums


def far_kernel(
    neighbours, phonon, coupling, across, before, turned, total, core, cross, partial, blocks, picked
):
    pair_kernel_far(neighbours, phonon, coupling, across, before, total, blocks, picked)
    finish(total, core, cross)
    for a in range(partial.shape[0]):
        partial[a] = rate_sums(total, turned, 0, a)


def pair_kernel_far(neighbours, phonon, coupling, across, before, total, blocks, picked):
    total[...] = before[...]
    put_blocks(blocks, 0, across)
    add_pairs(FAR, neighbours, phonon, coupling, blocks, (total,), picked, 4)


def last_kernel(
    scale, neighbours, phonon, coupling, across, before, turned, partial,
    total, core, cross, rate, blocks, picked,
):
    pair_kernel_far(neighbours, phonon, coupling, across, before, total, blocks, picked)
    finish(total, core, cross)
    for a in range(partial.shape[0]):
        sums = partial[a] - rate_sums(total, turned, 1, a)
        rate[a : a + 1, :] = jnp.sum(sums.T, axis=0, keepdims=True) * scale


def addends(x, axis):
    size = lax.axis_size(axis)
    if size > FEW:
        return [lax.psum(x, axis)]
    turns = [[(i, (i + k) % size) for i in range(size)] for k in range(1, size)]
    return [x] + [lax.ppermute(x, axis, turn) for turn in turns]


def end_kernel(total0, total1, cross0, core0, cross1, core1, *rest):
    *rates, out, rate = rest
    e_local = out.shape[1]
    for c, (total, cross, core) in enumerate(((total0, cross0, core0), (total1, cross1, core1))):
        for e in range(e_local):
            out[c, e] = total[REACH + e] + core[e] + cross[e]
    rate[...] = sum(r[...] for r in rates)


def per_device(green, coupling, phonon, neighbours):
    _, e_local, a_local, orb, _ = green.shape
    points = e_local * lax.axis_size("energy")
    spread = (e_local + 2 * REACH, a_local, orb, orb)
    edge = (REACH, a_local, orb, orb)

    def call(kernel, out, operands, parts=1):
        return pl.pallas_call(
            kernel,
            out_shape=[jax.ShapeDtypeStruct(shape, jnp.float32) for shape in out],
            in_specs=[SMEM, SMEM] + [VMEM] * (1 + len(operands)),
            out_specs=[VMEM] * len(out),
            scratch_shapes=[
                pltpu.VMEM((parts, a_local, e_local, orb, 2 * orb), jnp.bfloat16),
                pltpu.SMEM((a_local * neighbours.shape[1] + 1,), jnp.int32),
            ],
            compiler_params=pltpu.CompilerParams(vmem_limit_bytes=24 * 2**20),
            cost_estimate=pl.CostEstimate(flops=10**6, bytes_accessed=10**4, transcendentals=0),
        )(neighbours, phonon, coupling, *operands)

    sources = (green, coupling, jnp.swapaxes(phonon, 1, 2), neighbours)
    green0, green1, green, coupling, phonon, neighbours = pl.pallas_call(
        fetch_kernel,
        out_shape=[jax.ShapeDtypeStruct(green.shape[1:], green.dtype)] * 2
        + [jax.ShapeDtypeStruct(x.shape, x.dtype) for x in sources],
        in_specs=[ANY] * 4,
        out_specs=[VMEM] * 6,
        scratch_shapes=[pltpu.SemaphoreType.DMA((6,))],
        compiler_params=pltpu.CompilerParams(vmem_limit_bytes=24 * 2**20),
    )(*(pltpu.with_memory_space_constraint(x, pltpu.HBM) for x in sources))
    ahead1 = swap(green1, "atom", 0)
    ahead0 = swap(green0, "atom", 0)
    total0, total1 = call(own_kernel, [spread] * 2, (green0, green1), parts=2)
    ahead0, total0, total1 = lax.optimization_barrier((ahead0, total0, total1))
    across0 = forward(ahead0, "atom")
    (total0,) = call(pair_kernel, [spread], (ahead0, total0))
    ahead1, total0 = lax.optimization_barrier((ahead1, total0))
    across1 = forward(ahead1, "atom")
    by_core, by_cross = swap(green, "energy", 0), swap(green, "energy", 1)
    total1, turned = call(
        turn_kernel, [spread, (2,) + spread], (ahead1, total1, green0, green1, by_core, by_cross)
    )
    total0, core0, cross0, partial = call(
        far_kernel, [spread, edge, edge, (a_local, orb, orb)], (across0, total0, turned)
    )
    core0, cross0 = swap(core0, "energy", 0), swap(cross0, "energy", 1)
    total1, core1, cross1, rate = call(
        functools.partial(last_kernel, 1.0 / (4.0 * points)),
        [spread, edge, edge, (a_local, orb)],
        (across1, total1, turned, partial),
    )
    core1, cross1 = swap(core1, "energy", 0), swap(cross1, "energy", 1)
    cross0, core0, rate = lax.optimization_barrier((cross0, core0, rate))
    rates = addends(rate, "energy")
    return pl.pallas_call(
        end_kernel,
        out_shape=[
            jax.ShapeDtypeStruct(green.shape, jnp.float32),
            jax.ShapeDtypeStruct((a_local, orb), jnp.float32),
        ],
        in_specs=[VMEM] * (6 + len(rates)),
        out_specs=[VMEM] * 2,
        compiler_params=pltpu.CompilerParams(vmem_limit_bytes=24 * 2**20),
        cost_estimate=pl.CostEstimate(flops=10**6, bytes_accessed=2 * 10**6, transcendentals=0),
    )(total0, total1, cross0, core0, cross1, core1, *rates)


def solution(mesh):
    return jax.shard_map(
        per_device,
        mesh=mesh,
        in_specs=(
            P(None, "energy", "atom", None, None),
            P("atom", None, None, None),
            P("atom", None, None),
            P("atom", None),
        ),
        out_specs=(P(None, "energy", "atom", None, None), P("atom", None)),
        check_vma=False,
    )
```

```python
import functools

import jax
import jax.numpy as jnp
from jax import lax
from jax.experimental import pallas as pl
from jax.experimental.pallas import tpu as pltpu
from jax.sharding import PartitionSpec as P

SHIFTS = (-2, -1, 1, 2)
REACH = max(SHIFTS)
OWN, PAIR, FAR = 0, 1, 2
FEW = 4
VMEM = pl.BlockSpec(memory_space=pltpu.VMEM)
SMEM = pl.BlockSpec(memory_space=pltpu.SMEM)
ANY = pl.BlockSpec(memory_space=pl.ANY)


def halves(x):
    high = x.astype(jnp.bfloat16)
    return high, (x - high.astype(jnp.float32)).astype(jnp.bfloat16)


def swap(x, axis, first):
    low = range(first, lax.axis_size(axis) - 1, 2)
    return lax.ppermute(x, axis, [(i, i + 1) for i in low] + [(i + 1, i) for i in low])


def forward(x, axis):
    size = lax.axis_size(axis)
    ups = [(i, i + 2) for i in range(0, size - 2, 2)]
    downs = [(i + 2, i) for i in range(1, size - 2, 2)]
    return lax.ppermute(x, axis, ups + downs)


def put_blocks(blocks, c, green):
    orb = green.shape[-1]
    for e in range(green.shape[0]):
        for a in range(green.shape[1]):
            high, low = halves(green[e, a])
            blocks[c, a, e, :, :orb] = high
            blocks[c, a, e, :, orb:] = low


def add_pairs(group, neighbours, phonon, coupling, blocks, totals, picked, size):
    atoms, slots, orb = coupling.shape[0], coupling.shape[1], coupling.shape[-1]
    e_local = blocks.shape[2]
    index = lax.axis_index("atom")
    base = index * atoms
    if group != OWN:
        upper = (index & 1) == (0 if group == PAIR else 1)
        base += jnp.where(upper, atoms, -atoms)

    found = jnp.int32(0)
    for a in range(atoms):
        for j in range(slots):
            picked[found] = a * slots + j
            b = neighbours[a, j] - base
            found += ((b >= 0) & (b < atoms)).astype(jnp.int32)

    def batch(step, _):
        pairs = []
        for u in range(size):
            at = step * size + u
            item = picked[jnp.minimum(at, found - 1)]
            a = item // slots
            j = item - a * slots
            high, low = halves(coupling[a, j])
            left = jnp.concatenate([high, low], 1)
            right = jnp.concatenate(
                [jnp.concatenate([high, high], 1), jnp.concatenate([low, low], 1)], 0
            )
            pairs.append((a, j, neighbours[a, j] - base, jnp.where(at < found, 1.0, 0.0), left, right))
        inners = []
        for a, j, b, live, left, right in pairs:
            for c in range(len(totals)):
                near = blocks[c, b].reshape(e_local * orb, 2 * orb)
                inner = lax.dot_general(
                    near, right, (((1,), (1,)), ((), ())), preferred_element_type=jnp.float32
                )
                inners.append(inner[:, :orb] + inner[:, orb:])
        results = []
        for a, j, b, live, left, right in pairs:
            for total in totals:
                inner = inners.pop(0)
                sums = [None] * (e_local + 2 * REACH)
                for e in range(e_local):
                    high, low = halves(inner[e * orb : (e + 1) * orb])
                    both = jnp.concatenate([high, low], 1)
                    outer = jnp.dot(
                        left, jnp.concatenate([both, both], 0), preferred_element_type=jnp.float32
                    )
                    outer = outer[:, :orb] + outer[:, orb:]
                    for k, s in enumerate(SHIFTS):
                        d = e - s + REACH
                        term = (phonon[a, k, j] * live) * outer
                        sums[d] = term if sums[d] is None else sums[d] + term
                results.append((total, a, sums))
        for total, a, sums in results:
            for d, value in enumerate(sums):
                if value is not None:
                    total[d, a] += value

    lax.fori_loop(0, (found + size - 1) // size, batch, None)


def fetch_kernel(green, coupling, phonon, neighbours, *rest):
    *results, sems = rest
    sources = [green.at[0], green.at[1], green, coupling, phonon, neighbours]
    copies = [
        pltpu.make_async_copy(source, result, sems.at[i])
        for i, (source, result) in enumerate(zip(sources, results))
    ]
    for copy in copies:
        copy.start()
    for copy in copies:
        copy.wait()


def own_kernel(neighbours, phonon, coupling, green0, green1, total0, total1, blocks, picked):
    for c, (green, total) in enumerate(((green0, total0), (green1, total1))):
        put_blocks(blocks, c, green)
        total[...] = jnp.zeros_like(total)
    add_pairs(OWN, neighbours, phonon, coupling, blocks, (total0, total1), picked, 2)


def pair_kernel(
    neighbours, phonon, coupling, ahead0, ahead1, before0, before1, green, by_core, by_cross,
    total0, total1, turned, blocks, picked,
):
    e_local, a_local = green.shape[1], green.shape[2]
    core, cross = partner_energies(turned.shape[1])
    for c in range(2):
        for a in range(a_local):
            for e in range(e_local):
                turned[c, REACH + e, a] = green[c, e, a].T
            for e in range(REACH):
                turned[c, core + e, a] = by_core[c, e, a].T
                turned[c, cross + e, a] = by_cross[c, e, a].T
    total0[...] = before0[...]
    total1[...] = before1[...]
    put_blocks(blocks, 0, ahead0)
    put_blocks(blocks, 1, ahead1)
    add_pairs(PAIR, neighbours, phonon, coupling, blocks, (total0, total1), picked, 2)


def partner_energies(spread):
    odd = lax.axis_index("energy") & 1
    return jnp.where(odd == 0, spread - REACH, 0), jnp.where(odd == 0, 0, spread - REACH)


def finish(total, core, cross):
    to_core, to_cross = partner_energies(total.shape[0])
    for e in range(REACH):
        core[e] = total[to_core + e]
        cross[e] = total[to_cross + e]


def rate_sums(total, turned, c, a):
    sums = total[0, a] * turned[c, 0, a]
    for d in range(1, total.shape[0]):
        sums += total[d, a] * turned[c, d, a]
    return sums


def far_kernel(
    neighbours, phonon, coupling, across, before, turned, total, core, cross, partial, blocks, picked
):
    add_far(neighbours, phonon, coupling, across, before, total, blocks, picked)
    finish(total, core, cross)
    for a in range(partial.shape[0]):
        partial[a] = rate_sums(total, turned, 0, a)


def add_far(neighbours, phonon, coupling, across, before, total, blocks, picked):
    total[...] = before[...]
    put_blocks(blocks, 0, across)
    add_pairs(FAR, neighbours, phonon, coupling, blocks, (total,), picked, 4)


def last_kernel(
    scale, neighbours, phonon, coupling, across, before, turned, partial,
    total, core, cross, rate, blocks, picked,
):
    add_far(neighbours, phonon, coupling, across, before, total, blocks, picked)
    finish(total, core, cross)
    for a in range(partial.shape[0]):
        sums = partial[a] - rate_sums(total, turned, 1, a)
        rate[a : a + 1, :] = jnp.sum(sums.T, axis=0, keepdims=True) * scale


def addends(x, axis):
    size = lax.axis_size(axis)
    if size > FEW:
        return [lax.psum(x, axis)]
    turns = [[(i, (i + k) % size) for i in range(size)] for k in range(1, size)]
    return [x] + [lax.ppermute(x, axis, turn) for turn in turns]


def end_kernel(total0, total1, cross0, core0, cross1, core1, *rest):
    *rates, out, rate = rest
    e_local = out.shape[1]
    for c, (total, cross, core) in enumerate(((total0, cross0, core0), (total1, cross1, core1))):
        for e in range(e_local):
            out[c, e] = total[REACH + e] + core[e] + cross[e]
    rate[...] = sum(r[...] for r in rates)


def per_device(green, coupling, phonon, neighbours):
    _, e_local, a_local, orb, _ = green.shape
    points = e_local * lax.axis_size("energy")
    spread = (e_local + 2 * REACH, a_local, orb, orb)
    edge = (REACH, a_local, orb, orb)

    def call(kernel, out, operands, parts=1):
        return pl.pallas_call(
            kernel,
            out_shape=[jax.ShapeDtypeStruct(shape, jnp.float32) for shape in out],
            in_specs=[SMEM, SMEM] + [VMEM] * (1 + len(operands)),
            out_specs=[VMEM] * len(out),
            scratch_shapes=[
                pltpu.VMEM((parts, a_local, e_local, orb, 2 * orb), jnp.bfloat16),
                pltpu.SMEM((a_local * neighbours.shape[1] + 1,), jnp.int32),
            ],
            compiler_params=pltpu.CompilerParams(vmem_limit_bytes=24 * 2**20),
            cost_estimate=pl.CostEstimate(flops=10**6, bytes_accessed=10**4, transcendentals=0),
        )(neighbours, phonon, coupling, *operands)

    sources = (green, coupling, jnp.swapaxes(phonon, 1, 2), neighbours)
    green0, green1, green, coupling, phonon, neighbours = pl.pallas_call(
        fetch_kernel,
        out_shape=[jax.ShapeDtypeStruct(green.shape[1:], green.dtype)] * 2
        + [jax.ShapeDtypeStruct(x.shape, x.dtype) for x in sources],
        in_specs=[ANY] * 4,
        out_specs=[VMEM] * 6,
        scratch_shapes=[pltpu.SemaphoreType.DMA((6,))],
        compiler_params=pltpu.CompilerParams(vmem_limit_bytes=24 * 2**20),
    )(*(pltpu.with_memory_space_constraint(x, pltpu.HBM) for x in sources))
    ahead1 = swap(green1, "atom", 0)
    ahead0 = swap(green0, "atom", 0)
    by_core, by_cross = swap(green, "energy", 0), swap(green, "energy", 1)
    total0, total1 = call(own_kernel, [spread] * 2, (green0, green1), parts=2)
    ahead0, total0, total1 = lax.optimization_barrier((ahead0, total0, total1))
    across0 = forward(ahead0, "atom")
    green1, ahead0 = lax.optimization_barrier((green1, ahead0))
    across1 = swap(green1, "atom", 1)
    total0, total1, turned = call(
        pair_kernel,
        [spread, spread, (2,) + spread],
        (ahead0, ahead1, total0, total1, green, by_core, by_cross),
        parts=2,
    )
    total0, core0, cross0, partial = call(
        far_kernel, [spread, edge, edge, (a_local, orb, orb)], (across0, total0, turned)
    )
    core0, cross0 = swap(core0, "energy", 0), swap(cross0, "energy", 1)
    total1, core1, cross1, rate = call(
        functools.partial(last_kernel, 1.0 / (4.0 * points)),
        [spread, edge, edge, (a_local, orb)],
        (across1, total1, turned, partial),
    )
    core1, cross1 = swap(core1, "energy", 0), swap(cross1, "energy", 1)
    cross0, core0, rate = lax.optimization_barrier((cross0, core0, rate))
    rates = addends(rate, "energy")
    return pl.pallas_call(
        end_kernel,
        out_shape=[
            jax.ShapeDtypeStruct(green.shape, jnp.float32),
            jax.ShapeDtypeStruct((a_local, orb), jnp.float32),
        ],
        in_specs=[VMEM] * (6 + len(rates)),
        out_specs=[VMEM] * 2,
        compiler_params=pltpu.CompilerParams(vmem_limit_bytes=24 * 2**20),
        cost_estimate=pl.CostEstimate(flops=10**6, bytes_accessed=2 * 10**6, transcendentals=0),
    )(total0, total1, cross0, core0, cross1, core1, *rates)


def solution(mesh):
    return jax.shard_map(
        per_device,
        mesh=mesh,
        in_specs=(
            P(None, "energy", "atom", None, None),
            P("atom", None, None, None),
            P("atom", None, None),
            P("atom", None),
        ),
        out_specs=(P(None, "energy", "atom", None, None), P("atom", None)),
        check_vma=False,
    )
```

```python
import functools

import jax
import jax.numpy as jnp
from jax import lax
from jax.experimental import pallas as pl
from jax.experimental.pallas import tpu as pltpu
from jax.sharding import PartitionSpec as P

SHIFTS = (-2, -1, 1, 2)
REACH = max(SHIFTS)
OWN, PAIR, FAR = 0, 1, 2
FEW = 4
VMEM = pl.BlockSpec(memory_space=pltpu.VMEM)
SMEM = pl.BlockSpec(memory_space=pltpu.SMEM)
ANY = pl.BlockSpec(memory_space=pl.ANY)


def halves(x):
    high = x.astype(jnp.bfloat16)
    return high, (x - high.astype(jnp.float32)).astype(jnp.bfloat16)


def partner_of(i, first, size):
    other = i + 1 if (i - first) % 2 == 0 else i - 1
    return other if 0 <= other < size else i


def swap(x, axis, first):
    partner = [partner_of(i, first, lax.axis_size(axis)) for i in range(lax.axis_size(axis))]
    return lax.ppermute(x, axis, list(enumerate(partner)))


def forward(x, axis):
    size = lax.axis_size(axis)
    ups = [(i, i + 2) for i in range(0, size - 2, 2)]
    downs = [(i + 2, i) for i in range(1, size - 2, 2)]
    return lax.ppermute(x, axis, ups + downs)


def put_blocks(blocks, c, green):
    orb = green.shape[-1]
    for e in range(green.shape[0]):
        for a in range(green.shape[1]):
            high, low = halves(green[e, a])
            blocks[c, a, e, :, :orb] = high
            blocks[c, a, e, :, orb:] = low


def add_pairs(group, neighbours, phonon, coupling, blocks, totals, picked, size):
    atoms, slots, orb = coupling.shape[0], coupling.shape[1], coupling.shape[-1]
    e_local = blocks.shape[2]
    index = lax.axis_index("atom")
    base = index * atoms
    if group != OWN:
        upper = (index & 1) == (0 if group == PAIR else 1)
        base += jnp.where(upper, atoms, -atoms)

    found = jnp.int32(0)
    for a in range(atoms):
        for j in range(slots):
            picked[found] = a * slots + j
            b = neighbours[a, j] - base
            found += ((b >= 0) & (b < atoms)).astype(jnp.int32)

    def batch(step, _):
        pairs = []
        for u in range(size):
            at = step * size + u
            item = picked[jnp.minimum(at, found - 1)]
            a = item // slots
            j = item - a * slots
            high, low = halves(coupling[a, j])
            left = jnp.concatenate([high, low], 1)
            right = jnp.concatenate(
                [jnp.concatenate([high, high], 1), jnp.concatenate([low, low], 1)], 0
            )
            pairs.append((a, j, neighbours[a, j] - base, jnp.where(at < found, 1.0, 0.0), left, right))
        inners = []
        for a, j, b, live, left, right in pairs:
            for c in range(len(totals)):
                near = blocks[c, b].reshape(e_local * orb, 2 * orb)
                inner = lax.dot_general(
                    near, right, (((1,), (1,)), ((), ())), preferred_element_type=jnp.float32
                )
                inners.append(inner[:, :orb] + inner[:, orb:])
        results = []
        for a, j, b, live, left, right in pairs:
            for total in totals:
                inner = inners.pop(0)
                sums = [None] * (e_local + 2 * REACH)
                for e in range(e_local):
                    high, low = halves(inner[e * orb : (e + 1) * orb])
                    both = jnp.concatenate([high, low], 1)
                    outer = jnp.dot(
                        left, jnp.concatenate([both, both], 0), preferred_element_type=jnp.float32
                    )
                    outer = outer[:, :orb] + outer[:, orb:]
                    for k, s in enumerate(SHIFTS):
                        d = e - s + REACH
                        term = (phonon[a, k, j] * live) * outer
                        sums[d] = term if sums[d] is None else sums[d] + term
                results.append((total, a, sums))
        for total, a, sums in results:
            for d, value in enumerate(sums):
                if value is not None:
                    total[d, a] += value

    lax.fori_loop(0, (found + size - 1) // size, batch, None)


def fetch_kernel(green, coupling, phonon, neighbours, *rest):
    *results, sems = rest
    sources = [green.at[0], green.at[1], green, coupling, phonon, neighbours]
    copies = [
        pltpu.make_async_copy(source, result, sems.at[i])
        for i, (source, result) in enumerate(zip(sources, results))
    ]
    for copy in copies:
        copy.start()
    for copy in copies:
        copy.wait()


def own_kernel(neighbours, phonon, coupling, green0, green1, total0, total1, blocks, picked):
    for c, (green, total) in enumerate(((green0, total0), (green1, total1))):
        put_blocks(blocks, c, green)
        total[...] = jnp.zeros_like(total)
    add_pairs(OWN, neighbours, phonon, coupling, blocks, (total0, total1), picked, 2)


def pair_kernel(
    size, neighbours, phonon, coupling, ahead0, ahead1, before0, before1, green, by_core, by_cross,
    total0, total1, turned, blocks, picked,
):
    e_local, a_local = green.shape[1], green.shape[2]
    core, cross = partner_energies(turned.shape[1])
    has_core, has_cross = has_partners(size)
    for c in range(2):
        for a in range(a_local):
            for e in range(e_local):
                turned[c, REACH + e, a] = green[c, e, a].T
            for e in range(REACH):
                turned[c, core + e, a] = by_core[c, e, a].T * has_core
                turned[c, cross + e, a] = by_cross[c, e, a].T * has_cross
    total0[...] = before0[...]
    total1[...] = before1[...]
    put_blocks(blocks, 0, ahead0)
    put_blocks(blocks, 1, ahead1)
    add_pairs(PAIR, neighbours, phonon, coupling, blocks, (total0, total1), picked, 2)


def partner_energies(spread):
    odd = lax.axis_index("energy") & 1
    return jnp.where(odd == 0, spread - REACH, 0), jnp.where(odd == 0, 0, spread - REACH)


def has_partners(size):
    me = lax.axis_index("energy")
    above, below = jnp.where(me < size - 1, 1.0, 0.0), jnp.where(me > 0, 1.0, 0.0)
    odd = me & 1
    return jnp.where(odd == 0, above, below), jnp.where(odd == 0, below, above)


def finish(total, core, cross):
    to_core, to_cross = partner_energies(total.shape[0])
    for e in range(REACH):
        core[e] = total[to_core + e]
        cross[e] = total[to_cross + e]


def rate_sums(total, turned, c, a):
    sums = total[0, a] * turned[c, 0, a]
    for d in range(1, total.shape[0]):
        sums += total[d, a] * turned[c, d, a]
    return sums


def far_kernel(
    neighbours, phonon, coupling, across, before, turned, total, core, cross, partial, blocks, picked
):
    add_far(neighbours, phonon, coupling, across, before, total, blocks, picked)
    finish(total, core, cross)
    for a in range(partial.shape[0]):
        partial[a] = rate_sums(total, turned, 0, a)


def add_far(neighbours, phonon, coupling, across, before, total, blocks, picked):
    total[...] = before[...]
    put_blocks(blocks, 0, across)
    add_pairs(FAR, neighbours, phonon, coupling, blocks, (total,), picked, 4)


def last_kernel(
    scale, neighbours, phonon, coupling, across, before, turned, partial,
    total, core, cross, rate, blocks, picked,
):
    add_far(neighbours, phonon, coupling, across, before, total, blocks, picked)
    finish(total, core, cross)
    for a in range(partial.shape[0]):
        sums = partial[a] - rate_sums(total, turned, 1, a)
        rate[a : a + 1, :] = jnp.sum(sums.T, axis=0, keepdims=True) * scale


def addends(x, axis):
    size = lax.axis_size(axis)
    if size > FEW:
        return [lax.psum(x, axis)]
    turns = [[(i, (i + k) % size) for i in range(size)] for k in range(1, size)]
    return [x] + [lax.ppermute(x, axis, turn) for turn in turns]


def end_kernel(size, total0, total1, cross0, core0, cross1, core1, *rest):
    *rates, out, rate = rest
    e_local = out.shape[1]
    has_core, has_cross = has_partners(size)
    for c, (total, cross, core) in enumerate(((total0, cross0, core0), (total1, cross1, core1))):
        for e in range(e_local):
            out[c, e] = total[REACH + e] + core[e] * has_core + cross[e] * has_cross
    rate[...] = sum(r[...] for r in rates)


def per_device(green, coupling, phonon, neighbours):
    _, e_local, a_local, orb, _ = green.shape
    energies = lax.axis_size("energy")
    points = e_local * energies
    spread = (e_local + 2 * REACH, a_local, orb, orb)
    edge = (REACH, a_local, orb, orb)

    def call(kernel, out, operands, parts=1):
        return pl.pallas_call(
            kernel,
            out_shape=[jax.ShapeDtypeStruct(shape, jnp.float32) for shape in out],
            in_specs=[SMEM, SMEM] + [VMEM] * (1 + len(operands)),
            out_specs=[VMEM] * len(out),
            scratch_shapes=[
                pltpu.VMEM((parts, a_local, e_local, orb, 2 * orb), jnp.bfloat16),
                pltpu.SMEM((a_local * neighbours.shape[1] + 1,), jnp.int32),
            ],
            compiler_params=pltpu.CompilerParams(vmem_limit_bytes=24 * 2**20),
            cost_estimate=pl.CostEstimate(flops=10**6, bytes_accessed=10**4, transcendentals=0),
        )(neighbours, phonon, coupling, *operands)

    sources = (green, coupling, jnp.swapaxes(phonon, 1, 2), neighbours)
    green0, green1, green, coupling, phonon, neighbours = pl.pallas_call(
        fetch_kernel,
        out_shape=[jax.ShapeDtypeStruct(green.shape[1:], green.dtype)] * 2
        + [jax.ShapeDtypeStruct(x.shape, x.dtype) for x in sources],
        in_specs=[ANY] * 4,
        out_specs=[VMEM] * 6,
        scratch_shapes=[pltpu.SemaphoreType.DMA((6,))],
        compiler_params=pltpu.CompilerParams(vmem_limit_bytes=24 * 2**20),
    )(*(pltpu.with_memory_space_constraint(x, pltpu.HBM) for x in sources))
    ahead1 = swap(green1, "atom", 0)
    ahead0 = swap(green0, "atom", 0)
    by_core, by_cross = swap(green, "energy", 0), swap(green, "energy", 1)
    total0, total1 = call(own_kernel, [spread] * 2, (green0, green1), parts=2)
    ahead0, total0, total1 = lax.optimization_barrier((ahead0, total0, total1))
    across0 = forward(ahead0, "atom")
    green1, ahead0 = lax.optimization_barrier((green1, ahead0))
    across1 = swap(green1, "atom", 1)
    total0, total1, turned = call(
        functools.partial(pair_kernel, energies),
        [spread, spread, (2,) + spread],
        (ahead0, ahead1, total0, total1, green, by_core, by_cross),
        parts=2,
    )
    total0, core0, cross0, partial = call(
        far_kernel, [spread, edge, edge, (a_local, orb, orb)], (across0, total0, turned)
    )
    core0, cross0 = swap(core0, "energy", 0), swap(cross0, "energy", 1)
    total1, core1, cross1, rate = call(
        functools.partial(last_kernel, 1.0 / (4.0 * points)),
        [spread, edge, edge, (a_local, orb)],
        (across1, total1, turned, partial),
    )
    core1, cross1 = swap(core1, "energy", 0), swap(cross1, "energy", 1)
    cross0, core0, rate = lax.optimization_barrier((cross0, core0, rate))
    rates = addends(rate, "energy")
    return pl.pallas_call(
        functools.partial(end_kernel, energies),
        out_shape=[
            jax.ShapeDtypeStruct(green.shape, jnp.float32),
            jax.ShapeDtypeStruct((a_local, orb), jnp.float32),
        ],
        in_specs=[VMEM] * (6 + len(rates)),
        out_specs=[VMEM] * 2,
        compiler_params=pltpu.CompilerParams(vmem_limit_bytes=24 * 2**20),
        cost_estimate=pl.CostEstimate(flops=10**6, bytes_accessed=2 * 10**6, transcendentals=0),
    )(total0, total1, cross0, core0, cross1, core1, *rates)


def solution(mesh):
    return jax.shard_map(
        per_device,
        mesh=mesh,
        in_specs=(
            P(None, "energy", "atom", None, None),
            P("atom", None, None, None),
            P("atom", None, None),
            P("atom", None),
        ),
        out_specs=(P(None, "energy", "atom", None, None), P("atom", None)),
        check_vma=False,
    )
```

```python
import functools

import jax
import jax.numpy as jnp
from jax import lax
from jax.experimental import pallas as pl
from jax.experimental.pallas import tpu as pltpu
from jax.sharding import PartitionSpec as P

SHIFTS = (-2, -1, 1, 2)
REACH = max(SHIFTS)
OWN, PAIR, FAR = 0, 1, 2
FEW = 4
VMEM = pl.BlockSpec(memory_space=pltpu.VMEM)
SMEM = pl.BlockSpec(memory_space=pltpu.SMEM)
ANY = pl.BlockSpec(memory_space=pl.ANY)


def halves(x):
    high = x.astype(jnp.bfloat16)
    return high, (x - high.astype(jnp.float32)).astype(jnp.bfloat16)


def swap(x, axis, first):
    low = range(first, lax.axis_size(axis) - 1, 2)
    return lax.ppermute(x, axis, [(i, i + 1) for i in low] + [(i + 1, i) for i in low])


def forward(x, axis):
    size = lax.axis_size(axis)
    ups = [(i, i + 2) for i in range(0, size - 2, 2)]
    downs = [(i + 2, i) for i in range(1, size - 2, 2)]
    return lax.ppermute(x, axis, ups + downs)


def put_blocks(blocks, c, green):
    orb = green.shape[-1]
    for e in range(green.shape[0]):
        for a in range(green.shape[1]):
            high, low = halves(green[e, a])
            blocks[a, c, e, :, :orb] = high
            blocks[a, c, e, :, orb:] = low


def add_pairs(group, neighbours, phonon, coupling, blocks, totals, picked, size):
    atoms, slots, orb = coupling.shape[0], coupling.shape[1], coupling.shape[-1]
    _, parts, e_local, _, _ = blocks.shape
    index = lax.axis_index("atom")
    base = index * atoms
    if group != OWN:
        upper = (index & 1) == (0 if group == PAIR else 1)
        base += jnp.where(upper, atoms, -atoms)

    found = jnp.int32(0)
    for a in range(atoms):
        for j in range(slots):
            picked[found] = a * slots + j
            b = neighbours[a, j] - base
            found += ((b >= 0) & (b < atoms)).astype(jnp.int32)

    def batch(step, _):
        pairs = []
        for u in range(size):
            at = step * size + u
            item = picked[jnp.minimum(at, found - 1)]
            a = item // slots
            j = item - a * slots
            high, low = halves(coupling[a, j])
            left = jnp.concatenate([high, low], 1)
            right = jnp.concatenate(
                [jnp.concatenate([high, high], 1), jnp.concatenate([low, low], 1)], 0
            )
            near = blocks[neighbours[a, j] - base].reshape(parts * e_local * orb, 2 * orb)
            inner = lax.dot_general(
                near, right, (((1,), (1,)), ((), ())), preferred_element_type=jnp.float32
            )
            pairs.append((a, j, jnp.where(at < found, 1.0, 0.0), left, inner[:, :orb] + inner[:, orb:]))
        results = []
        for a, j, live, left, inner in pairs:
            for c, total in enumerate(totals):
                sums = [None] * (e_local + 2 * REACH)
                for e in range(e_local):
                    start = (c * e_local + e) * orb
                    high, low = halves(inner[start : start + orb])
                    both = jnp.concatenate([high, low], 1)
                    outer = jnp.dot(
                        left, jnp.concatenate([both, both], 0), preferred_element_type=jnp.float32
                    )
                    outer = outer[:, :orb] + outer[:, orb:]
                    for k, s in enumerate(SHIFTS):
                        d = e - s + REACH
                        term = (phonon[a, k, j] * live) * outer
                        sums[d] = term if sums[d] is None else sums[d] + term
                results.append((total, a, sums))
        for total, a, sums in results:
            for d, value in enumerate(sums):
                if value is not None:
                    total[d, a] += value

    lax.fori_loop(0, (found + size - 1) // size, batch, None)


def fetch_kernel(green, coupling, phonon, neighbours, *rest):
    *results, sems = rest
    sources = [green.at[0], green.at[1], green, coupling, phonon, neighbours]
    copies = [
        pltpu.make_async_copy(source, result, sems.at[i])
        for i, (source, result) in enumerate(zip(sources, results))
    ]
    for copy in copies:
        copy.start()
    for copy in copies:
        copy.wait()


def own_kernel(neighbours, phonon, coupling, green0, green1, total0, total1, blocks, picked):
    for c, (green, total) in enumerate(((green0, total0), (green1, total1))):
        put_blocks(blocks, c, green)
        total[...] = jnp.zeros_like(total)
    add_pairs(OWN, neighbours, phonon, coupling, blocks, (total0, total1), picked, 2)


def pair_kernel(neighbours, phonon, coupling, ahead, before, total, blocks, picked):
    total[...] = before[...]
    put_blocks(blocks, 0, ahead)
    add_pairs(PAIR, neighbours, phonon, coupling, blocks, (total,), picked, 4)


def turn_kernel(
    neighbours, phonon, coupling, ahead, before, green, by_core, by_cross, total, turned, blocks, picked
):
    e_local, a_local = green.shape[1], green.shape[2]
    core, cross = partner_energies(turned.shape[1])
    for c in range(2):
        for a in range(a_local):
            for e in range(e_local):
                turned[c, REACH + e, a] = green[c, e, a].T
            for e in range(REACH):
                turned[c, core + e, a] = by_core[c, e, a].T
                turned[c, cross + e, a] = by_cross[c, e, a].T
    pair_kernel(neighbours, phonon, coupling, ahead, before, total, blocks, picked)


def partner_energies(spread):
    odd = lax.axis_index("energy") & 1
    return jnp.where(odd == 0, spread - REACH, 0), jnp.where(odd == 0, 0, spread - REACH)


def far_kernel(
    scale, neighbours, phonon, coupling, across0, across1, turned, before0, before1,
    own, core, cross, rate, total0, total1, blocks, picked,
):
    e_local, a_local = own.shape[1], own.shape[2]
    total0[...] = before0[...]
    total1[...] = before1[...]
    put_blocks(blocks, 0, across0)
    put_blocks(blocks, 1, across1)
    add_pairs(FAR, neighbours, phonon, coupling, blocks, (total0, total1), picked, 2)
    to_core, to_cross = partner_energies(total0.shape[0])
    for c, total in enumerate((total0, total1)):
        for e in range(REACH):
            core[c, e] = total[to_core + e]
            cross[c, e] = total[to_cross + e]
        for e in range(e_local):
            own[c, e] = total[REACH + e]
    for a in range(a_local):
        sums = total0[0, a] * turned[0, 0, a] - total1[0, a] * turned[1, 0, a]
        for d in range(1, total0.shape[0]):
            sums += total0[d, a] * turned[0, d, a] - total1[d, a] * turned[1, d, a]
        rate[a : a + 1, :] = jnp.sum(sums.T, axis=0, keepdims=True) * scale


def addends(x, axis):
    size = lax.axis_size(axis)
    if size > FEW:
        return [lax.psum(x, axis)]
    turns = [[(i, (i + k) % size) for i in range(size)] for k in range(1, size)]
    return [x] + [lax.ppermute(x, axis, turn) for turn in turns]


def end_kernel(own, cross, core, *rest):
    *rates, out, rate = rest
    out[...] = own[...] + core[...] + cross[...]
    rate[...] = sum(r[...] for r in rates)


def per_device(green, coupling, phonon, neighbours):
    _, e_local, a_local, orb, _ = green.shape
    points = e_local * lax.axis_size("energy")
    spread = (e_local + 2 * REACH, a_local, orb, orb)
    edge = (2, REACH, a_local, orb, orb)

    def call(kernel, out, operands, parts=1, scratch=()):
        return pl.pallas_call(
            kernel,
            out_shape=[jax.ShapeDtypeStruct(shape, jnp.float32) for shape in out],
            in_specs=[SMEM, SMEM] + [VMEM] * (1 + len(operands)),
            out_specs=[VMEM] * len(out),
            scratch_shapes=list(scratch)
            + [
                pltpu.VMEM((a_local, parts, e_local, orb, 2 * orb), jnp.bfloat16),
                pltpu.SMEM((a_local * neighbours.shape[1] + 1,), jnp.int32),
            ],
            compiler_params=pltpu.CompilerParams(vmem_limit_bytes=24 * 2**20),
            cost_estimate=pl.CostEstimate(flops=10**6, bytes_accessed=10**4, transcendentals=0),
        )(neighbours, phonon, coupling, *operands)

    sources = (green, coupling, jnp.swapaxes(phonon, 1, 2), neighbours)
    green0, green1, green, coupling, phonon, neighbours = pl.pallas_call(
        fetch_kernel,
        out_shape=[jax.ShapeDtypeStruct(green.shape[1:], green.dtype)] * 2
        + [jax.ShapeDtypeStruct(x.shape, x.dtype) for x in sources],
        in_specs=[ANY] * 4,
        out_specs=[VMEM] * 6,
        scratch_shapes=[pltpu.SemaphoreType.DMA((6,))],
        compiler_params=pltpu.CompilerParams(vmem_limit_bytes=24 * 2**20),
    )(*(pltpu.with_memory_space_constraint(x, pltpu.HBM) for x in sources))
    ahead1 = swap(green1, "atom", 0)
    ahead0 = swap(green0, "atom", 0)
    by_core, by_cross = swap(green, "energy", 0), swap(green, "energy", 1)
    total0, total1 = call(own_kernel, [spread] * 2, (green0, green1), parts=2)
    ahead0, total0, total1 = lax.optimization_barrier((ahead0, total0, total1))
    across0 = forward(ahead0, "atom")
    (total0,) = call(pair_kernel, [spread], (ahead0, total0))
    green1, total0 = lax.optimization_barrier((green1, total0))
    across1 = swap(green1, "atom", 1)
    total1, turned = call(
        turn_kernel, [spread, (2,) + spread], (ahead1, total1, green, by_core, by_cross)
    )
    across0, turned = lax.optimization_barrier((across0, turned))
    across1, across0 = lax.optimization_barrier((across1, across0))
    own, core, cross, rate = call(
        functools.partial(far_kernel, 1.0 / (4.0 * points)),
        [green.shape, edge, edge, (a_local, orb)],
        (across0, across1, turned, total0, total1),
        parts=2,
        scratch=[pltpu.VMEM(spread, jnp.float32)] * 2,
    )
    core, cross = swap(core, "energy", 0), swap(cross, "energy", 1)
    rates = addends(rate, "energy")
    return pl.pallas_call(
        end_kernel,
        out_shape=[
            jax.ShapeDtypeStruct(green.shape, jnp.float32),
            jax.ShapeDtypeStruct((a_local, orb), jnp.float32),
        ],
        in_specs=[VMEM] * (3 + len(rates)),
        out_specs=[VMEM] * 2,
        compiler_params=pltpu.CompilerParams(vmem_limit_bytes=24 * 2**20),
        cost_estimate=pl.CostEstimate(flops=10**6, bytes_accessed=2 * 10**6, transcendentals=0),
    )(own, cross, core, *rates)


def solution(mesh):
    return jax.shard_map(
        per_device,
        mesh=mesh,
        in_specs=(
            P(None, "energy", "atom", None, None),
            P("atom", None, None, None),
            P("atom", None, None),
            P("atom", None),
        ),
        out_specs=(P(None, "energy", "atom", None, None), P("atom", None)),
        check_vma=False,
    )
```

```python
import functools

import jax
import jax.numpy as jnp
from jax import lax
from jax.experimental import pallas as pl
from jax.experimental.pallas import tpu as pltpu
from jax.sharding import PartitionSpec as P

SHIFTS = (-2, -1, 1, 2)
REACH = max(SHIFTS)
OWN, PAIR, FAR = 0, 1, 2
FEW = 4
VMEM = pl.BlockSpec(memory_space=pltpu.VMEM)
SMEM = pl.BlockSpec(memory_space=pltpu.SMEM)
ANY = pl.BlockSpec(memory_space=pl.ANY)


def halves(x):
    high = x.astype(jnp.bfloat16)
    return high, (x - high.astype(jnp.float32)).astype(jnp.bfloat16)


def swap(x, axis, first):
    low = range(first, lax.axis_size(axis) - 1, 2)
    return lax.ppermute(x, axis, [(i, i + 1) for i in low] + [(i + 1, i) for i in low])


def forward(x, axis):
    size = lax.axis_size(axis)
    ups = [(i, i + 2) for i in range(0, size - 2, 2)]
    downs = [(i + 2, i) for i in range(1, size - 2, 2)]
    return lax.ppermute(x, axis, ups + downs)


def put_blocks(blocks, c, green):
    orb = green.shape[-1]
    for e in range(green.shape[0]):
        for a in range(green.shape[1]):
            high, low = halves(green[e, a])
            blocks[c, a, e, :, :orb] = high
            blocks[c, a, e, :, orb:] = low


def add_pairs(group, neighbours, phonon, coupling, blocks, totals, picked, size):
    atoms, slots, orb = coupling.shape[0], coupling.shape[1], coupling.shape[-1]
    e_local = blocks.shape[2]
    index = lax.axis_index("atom")
    base = index * atoms
    if group != OWN:
        upper = (index & 1) == (0 if group == PAIR else 1)
        base += jnp.where(upper, atoms, -atoms)

    found = jnp.int32(0)
    for a in range(atoms):
        for j in range(slots):
            picked[found] = a * slots + j
            b = neighbours[a, j] - base
            found += ((b >= 0) & (b < atoms)).astype(jnp.int32)

    def batch(step, _):
        pairs = []
        for u in range(size):
            at = step * size + u
            item = picked[jnp.minimum(at, found - 1)]
            a = item // slots
            j = item - a * slots
            high, low = halves(coupling[a, j])
            left = jnp.concatenate([high, low], 1)
            right = jnp.concatenate(
                [jnp.concatenate([high, high], 1), jnp.concatenate([low, low], 1)], 0
            )
            pairs.append((a, j, neighbours[a, j] - base, jnp.where(at < found, 1.0, 0.0), left, right))
        inners = []
        for a, j, b, live, left, right in pairs:
            for c in range(len(totals)):
                near = blocks[c, b].reshape(e_local * orb, 2 * orb)
                inner = lax.dot_general(
                    near, right, (((1,), (1,)), ((), ())), preferred_element_type=jnp.float32
                )
                inners.append(inner[:, :orb] + inner[:, orb:])
        results = []
        for a, j, b, live, left, right in pairs:
            for total in totals:
                inner = inners.pop(0)
                sums = [None] * (e_local + 2 * REACH)
                for e in range(e_local):
                    high, low = halves(inner[e * orb : (e + 1) * orb])
                    both = jnp.concatenate([high, low], 1)
                    outer = jnp.dot(
                        left, jnp.concatenate([both, both], 0), preferred_element_type=jnp.float32
                    )
                    outer = outer[:, :orb] + outer[:, orb:]
                    for k, s in enumerate(SHIFTS):
                        d = e - s + REACH
                        term = (phonon[a, k, j] * live) * outer
                        sums[d] = term if sums[d] is None else sums[d] + term
                results.append((total, a, sums))
        for total, a, sums in results:
            for d, value in enumerate(sums):
                if value is not None:
                    total[d, a] += value

    lax.fori_loop(0, (found + size - 1) // size, batch, None)


def copy_all(sources, results, sems):
    copies = [
        pltpu.make_async_copy(source, result, sems.at[i])
        for i, (source, result) in enumerate(zip(sources, results))
    ]
    for copy in copies:
        copy.start()
    for copy in copies:
        copy.wait()


def part_kernel(green, part, sems):
    copy_all([green.at[0]], [part], sems)


def fetch_kernel(green, coupling, phonon, neighbours, *rest):
    copy_all([green.at[1], green, coupling, phonon, neighbours], rest[:-1], rest[-1])


def own_kernel(neighbours, phonon, coupling, green0, green1, total0, total1, blocks, picked):
    for c, (green, total) in enumerate(((green0, total0), (green1, total1))):
        put_blocks(blocks, c, green)
        total[...] = jnp.zeros_like(total)
    add_pairs(OWN, neighbours, phonon, coupling, blocks, (total0, total1), picked, 2)


def pair_kernel(neighbours, phonon, coupling, ahead, before, total, blocks, picked):
    total[...] = before[...]
    put_blocks(blocks, 0, ahead)
    add_pairs(PAIR, neighbours, phonon, coupling, blocks, (total,), picked, 4)


def turn_kernel(
    neighbours, phonon, coupling, ahead, before, total0, green, by_core, by_cross,
    total, turned, partial, blocks, picked,
):
    e_local, a_local = green.shape[1], green.shape[2]
    core, cross = partner_energies(turned.shape[1])
    for c in range(2):
        for a in range(a_local):
            for e in range(e_local):
                turned[c, REACH + e, a] = green[c, e, a].T
            for e in range(REACH):
                turned[c, core + e, a] = by_core[c, e, a].T
                turned[c, cross + e, a] = by_cross[c, e, a].T
    for a in range(a_local):
        partial[a] = rate_sums(total0, turned, 0, a)
    pair_kernel(neighbours, phonon, coupling, ahead, before, total, blocks, picked)


def partner_energies(spread):
    odd = lax.axis_index("energy") & 1
    return jnp.where(odd == 0, spread - REACH, 0), jnp.where(odd == 0, 0, spread - REACH)


def finish(total, core, cross):
    to_core, to_cross = partner_energies(total.shape[0])
    for e in range(REACH):
        core[e] = total[to_core + e]
        cross[e] = total[to_cross + e]


def rate_sums(total, turned, c, a):
    sums = total[0, a] * turned[c, 0, a]
    for d in range(1, total.shape[0]):
        sums += total[d, a] * turned[c, d, a]
    return sums


def far_kernel(neighbours, phonon, coupling, across, before, total, core, cross, blocks, picked):
    add_far(neighbours, phonon, coupling, across, before, total, blocks, picked)
    finish(total, core, cross)


def add_far(neighbours, phonon, coupling, across, before, total, blocks, picked):
    total[...] = before[...]
    put_blocks(blocks, 0, across)
    add_pairs(FAR, neighbours, phonon, coupling, blocks, (total,), picked, 4)


def last_kernel(
    scale, neighbours, phonon, coupling, across, before, turned, partial,
    total, core, cross, rate, blocks, picked,
):
    add_far(neighbours, phonon, coupling, across, before, total, blocks, picked)
    finish(total, core, cross)
    for a in range(partial.shape[0]):
        sums = partial[a] - rate_sums(total, turned, 1, a)
        rate[a : a + 1, :] = jnp.sum(sums.T, axis=0, keepdims=True) * scale


def addends(x, axis):
    size = lax.axis_size(axis)
    if size > FEW:
        return [lax.psum(x, axis)]
    turns = [[(i, (i + k) % size) for i in range(size)] for k in range(1, size)]
    return [x] + [lax.ppermute(x, axis, turn) for turn in turns]


def end_kernel(total0, total1, cross0, core0, cross1, core1, *rest):
    *rates, out, rate = rest
    e_local = out.shape[1]
    for c, (total, cross, core) in enumerate(((total0, cross0, core0), (total1, cross1, core1))):
        for e in range(e_local):
            out[c, e] = total[REACH + e] + core[e] + cross[e]
    rate[...] = sum(r[...] for r in rates)


def per_device(green, coupling, phonon, neighbours):
    _, e_local, a_local, orb, _ = green.shape
    points = e_local * lax.axis_size("energy")
    spread = (e_local + 2 * REACH, a_local, orb, orb)
    edge = (REACH, a_local, orb, orb)

    def call(kernel, out, operands, parts=1):
        return pl.pallas_call(
            kernel,
            out_shape=[jax.ShapeDtypeStruct(shape, jnp.float32) for shape in out],
            in_specs=[SMEM, SMEM] + [VMEM] * (1 + len(operands)),
            out_specs=[VMEM] * len(out),
            scratch_shapes=[
                pltpu.VMEM((parts, a_local, e_local, orb, 2 * orb), jnp.bfloat16),
                pltpu.SMEM((a_local * neighbours.shape[1] + 1,), jnp.int32),
            ],
            compiler_params=pltpu.CompilerParams(vmem_limit_bytes=24 * 2**20),
            cost_estimate=pl.CostEstimate(flops=10**6, bytes_accessed=10**4, transcendentals=0),
        )(neighbours, phonon, coupling, *operands)

    def fetch(kernel, out, sources):
        return pl.pallas_call(
            kernel,
            out_shape=[jax.ShapeDtypeStruct(x.shape, x.dtype) for x in out],
            in_specs=[ANY] * len(sources),
            out_specs=[VMEM] * len(out),
            scratch_shapes=[pltpu.SemaphoreType.DMA((len(out),))],
            compiler_params=pltpu.CompilerParams(vmem_limit_bytes=24 * 2**20),
        )(*(pltpu.with_memory_space_constraint(x, pltpu.HBM) for x in sources))

    sources = (green, coupling, jnp.swapaxes(phonon, 1, 2), neighbours)
    part = jax.ShapeDtypeStruct(green.shape[1:], green.dtype)
    (green0,) = fetch(part_kernel, [part], [green])
    green0, *sources = lax.optimization_barrier((green0, *sources))
    green1, green, coupling, phonon, neighbours = fetch(fetch_kernel, [part, *sources], sources)
    ahead0 = swap(green0, "atom", 0)
    by_core, by_cross = swap(green, "energy", 0), swap(green, "energy", 1)
    total0, total1 = call(own_kernel, [spread] * 2, (green0, green1), parts=2)
    green1, total0, total1 = lax.optimization_barrier((green1, total0, total1))
    ahead1 = swap(green1, "atom", 0)
    ahead0, total0 = lax.optimization_barrier((ahead0, total0))
    across0 = forward(ahead0, "atom")
    green1, ahead0 = lax.optimization_barrier((green1, ahead0))
    across1 = swap(green1, "atom", 1)
    (total0,) = call(pair_kernel, [spread], (ahead0, total0))
    ahead1, total0 = lax.optimization_barrier((ahead1, total0))
    total0, core0, cross0 = call(far_kernel, [spread, edge, edge], (across0, total0))
    core0, cross0 = swap(core0, "energy", 0), swap(cross0, "energy", 1)
    total1, turned, partial = call(
        turn_kernel,
        [spread, (2,) + spread, (a_local, orb, orb)],
        (ahead1, total1, total0, green, by_core, by_cross),
    )
    total1, core1, cross1, rate = call(
        functools.partial(last_kernel, 1.0 / (4.0 * points)),
        [spread, edge, edge, (a_local, orb)],
        (across1, total1, turned, partial),
    )
    cross0, core0, rate = lax.optimization_barrier((cross0, core0, rate))
    rates = addends(rate, "energy")
    core1, cross1, rates = lax.optimization_barrier((core1, cross1, rates))
    core1, cross1 = swap(core1, "energy", 0), swap(cross1, "energy", 1)
    return pl.pallas_call(
        end_kernel,
        out_shape=[
            jax.ShapeDtypeStruct(green.shape, jnp.float32),
            jax.ShapeDtypeStruct((a_local, orb), jnp.float32),
        ],
        in_specs=[VMEM] * (6 + len(rates)),
        out_specs=[VMEM] * 2,
        compiler_params=pltpu.CompilerParams(vmem_limit_bytes=24 * 2**20),
        cost_estimate=pl.CostEstimate(flops=10**6, bytes_accessed=2 * 10**6, transcendentals=0),
    )(total0, total1, cross0, core0, cross1, core1, *rates)


def solution(mesh):
    return jax.shard_map(
        per_device,
        mesh=mesh,
        in_specs=(
            P(None, "energy", "atom", None, None),
            P("atom", None, None, None),
            P("atom", None, None),
            P("atom", None),
        ),
        out_specs=(P(None, "energy", "atom", None, None), P("atom", None)),
        check_vma=False,
    )
```

```python
import functools

import jax
import jax.numpy as jnp
from jax import lax
from jax.experimental import pallas as pl
from jax.experimental.pallas import tpu as pltpu
from jax.sharding import PartitionSpec as P

SHIFTS = (-2, -1, 1, 2)
REACH = max(SHIFTS)
OWN, PAIR, FAR = 0, 1, 2
FEW = 4
VMEM = pl.BlockSpec(memory_space=pltpu.VMEM)
SMEM = pl.BlockSpec(memory_space=pltpu.SMEM)
ANY = pl.BlockSpec(memory_space=pl.ANY)


def halves(x):
    high = x.astype(jnp.bfloat16)
    return high, (x - high.astype(jnp.float32)).astype(jnp.bfloat16)


def swap(x, axis, first):
    low = range(first, lax.axis_size(axis) - 1, 2)
    return lax.ppermute(x, axis, [(i, i + 1) for i in low] + [(i + 1, i) for i in low])


def forward(x, axis):
    size = lax.axis_size(axis)
    ups = [(i, i + 2) for i in range(0, size - 2, 2)]
    downs = [(i + 2, i) for i in range(1, size - 2, 2)]
    return lax.ppermute(x, axis, ups + downs)


def put_blocks(blocks, c, green):
    orb = green.shape[-1]
    for e in range(green.shape[0]):
        for a in range(green.shape[1]):
            high, low = halves(green[e, a])
            blocks[c, a, e, :, :orb] = high
            blocks[c, a, e, :, orb:] = low


def add_pairs(group, neighbours, phonon, coupling, blocks, totals, picked, size):
    atoms, slots, orb = coupling.shape[0], coupling.shape[1], coupling.shape[-1]
    e_local = blocks.shape[2]
    index = lax.axis_index("atom")
    base = index * atoms
    if group != OWN:
        upper = (index & 1) == (0 if group == PAIR else 1)
        base += jnp.where(upper, atoms, -atoms)

    found = jnp.int32(0)
    for a in range(atoms):
        for j in range(slots):
            picked[found] = a * slots + j
            b = neighbours[a, j] - base
            found += ((b >= 0) & (b < atoms)).astype(jnp.int32)

    def batch(step, _):
        pairs = []
        for u in range(size):
            at = step * size + u
            item = picked[jnp.minimum(at, found - 1)]
            a = item // slots
            j = item - a * slots
            high, low = halves(coupling[a, j])
            left = jnp.concatenate([high, low], 1)
            right = jnp.concatenate(
                [jnp.concatenate([high, high], 1), jnp.concatenate([low, low], 1)], 0
            )
            pairs.append((a, j, neighbours[a, j] - base, jnp.where(at < found, 1.0, 0.0), left, right))
        inners = []
        for a, j, b, live, left, right in pairs:
            for c in range(len(totals)):
                near = blocks[c, b].reshape(e_local * orb, 2 * orb)
                inner = lax.dot_general(
                    near, right, (((1,), (1,)), ((), ())), preferred_element_type=jnp.float32
                )
                inners.append(inner[:, :orb] + inner[:, orb:])
        results = []
        for a, j, b, live, left, right in pairs:
            for total in totals:
                inner = inners.pop(0)
                sums = [None] * (e_local + 2 * REACH)
                for e in range(e_local):
                    high, low = halves(inner[e * orb : (e + 1) * orb])
                    both = jnp.concatenate([high, low], 1)
                    outer = jnp.dot(
                        left, jnp.concatenate([both, both], 0), preferred_element_type=jnp.float32
                    )
                    outer = outer[:, :orb] + outer[:, orb:]
                    for k, s in enumerate(SHIFTS):
                        d = e - s + REACH
                        term = (phonon[a, k, j] * live) * outer
                        sums[d] = term if sums[d] is None else sums[d] + term
                results.append((total, a, sums))
        for total, a, sums in results:
            for d, value in enumerate(sums):
                if value is not None:
                    total[d, a] += value

    lax.fori_loop(0, (found + size - 1) // size, batch, None)


def fetch_kernel(green, coupling, phonon, neighbours, *rest):
    *results, sems = rest
    sources = [green.at[0], green.at[1], green, coupling, phonon, neighbours]
    copies = [
        pltpu.make_async_copy(source, result, sems.at[i])
        for i, (source, result) in enumerate(zip(sources, results))
    ]
    for copy in copies:
        copy.start()
    for copy in copies:
        copy.wait()


def own_kernel(neighbours, phonon, coupling, green0, green1, total0, total1, blocks, picked):
    for c, (green, total) in enumerate(((green0, total0), (green1, total1))):
        put_blocks(blocks, c, green)
        total[...] = jnp.zeros_like(total)
    add_pairs(OWN, neighbours, phonon, coupling, blocks, (total0, total1), picked, 2)


def pair_kernel(neighbours, phonon, coupling, ahead, before, total, blocks, picked):
    total[...] = before[...]
    put_blocks(blocks, 0, ahead)
    add_pairs(PAIR, neighbours, phonon, coupling, blocks, (total,), picked, 4)


def turn_kernel(
    neighbours, phonon, coupling, ahead, before, total0, green, by_core, by_cross,
    total, turned, partial, blocks, picked,
):
    e_local, a_local = green.shape[1], green.shape[2]
    core, cross = partner_energies(turned.shape[1])
    for c in range(2):
        for a in range(a_local):
            for e in range(e_local):
                turned[c, REACH + e, a] = green[c, e, a].T
            for e in range(REACH):
                turned[c, core + e, a] = by_core[c, e, a].T
                turned[c, cross + e, a] = by_cross[c, e, a].T
    for a in range(a_local):
        partial[a] = rate_sums(total0, turned, 0, a)
    pair_kernel(neighbours, phonon, coupling, ahead, before, total, blocks, picked)


def partner_energies(spread):
    odd = lax.axis_index("energy") & 1
    return jnp.where(odd == 0, spread - REACH, 0), jnp.where(odd == 0, 0, spread - REACH)


def finish(total, core, cross):
    to_core, to_cross = partner_energies(total.shape[0])
    for e in range(REACH):
        core[e] = total[to_core + e]
        cross[e] = total[to_cross + e]


def rate_sums(total, turned, c, a):
    sums = total[0, a] * turned[c, 0, a]
    for d in range(1, total.shape[0]):
        sums += total[d, a] * turned[c, d, a]
    return sums


def far_kernel(neighbours, phonon, coupling, across, before, total, core, cross, blocks, picked):
    add_far(neighbours, phonon, coupling, across, before, total, blocks, picked)
    finish(total, core, cross)


def add_far(neighbours, phonon, coupling, across, before, total, blocks, picked):
    total[...] = before[...]
    put_blocks(blocks, 0, across)
    add_pairs(FAR, neighbours, phonon, coupling, blocks, (total,), picked, 4)


def last_kernel(
    scale, neighbours, phonon, coupling, across, before, turned, partial,
    total, core, cross, rate, blocks, picked,
):
    add_far(neighbours, phonon, coupling, across, before, total, blocks, picked)
    finish(total, core, cross)
    for a in range(partial.shape[0]):
        sums = partial[a] - rate_sums(total, turned, 1, a)
        rate[a : a + 1, :] = jnp.sum(sums.T, axis=0, keepdims=True) * scale


def addends(x, axis):
    size = lax.axis_size(axis)
    if size > FEW:
        return [lax.psum(x, axis)]
    turns = [[(i, (i + k) % size) for i in range(size)] for k in range(1, size)]
    return [x] + [lax.ppermute(x, axis, turn) for turn in turns]


def end_kernel(total0, total1, cross0, core0, cross1, core1, *rest):
    *rates, out, rate = rest
    e_local = out.shape[1]
    for c, (total, cross, core) in enumerate(((total0, cross0, core0), (total1, cross1, core1))):
        for e in range(e_local):
            out[c, e] = total[REACH + e] + core[e] + cross[e]
    rate[...] = sum(r[...] for r in rates)


def per_device(green, coupling, phonon, neighbours):
    _, e_local, a_local, orb, _ = green.shape
    points = e_local * lax.axis_size("energy")
    spread = (e_local + 2 * REACH, a_local, orb, orb)
    edge = (REACH, a_local, orb, orb)

    def call(kernel, out, operands, parts=1):
        return pl.pallas_call(
            kernel,
            out_shape=[jax.ShapeDtypeStruct(shape, jnp.float32) for shape in out],
            in_specs=[SMEM, SMEM] + [VMEM] * (1 + len(operands)),
            out_specs=[VMEM] * len(out),
            scratch_shapes=[
                pltpu.VMEM((parts, a_local, e_local, orb, 2 * orb), jnp.bfloat16),
                pltpu.SMEM((a_local * neighbours.shape[1] + 1,), jnp.int32),
            ],
            compiler_params=pltpu.CompilerParams(vmem_limit_bytes=24 * 2**20),
            cost_estimate=pl.CostEstimate(flops=10**6, bytes_accessed=10**4, transcendentals=0),
        )(neighbours, phonon, coupling, *operands)

    sources = (green, coupling, jnp.swapaxes(phonon, 1, 2), neighbours)
    green0, green1, green, coupling, phonon, neighbours = pl.pallas_call(
        fetch_kernel,
        out_shape=[jax.ShapeDtypeStruct(green.shape[1:], green.dtype)] * 2
        + [jax.ShapeDtypeStruct(x.shape, x.dtype) for x in sources],
        in_specs=[ANY] * 4,
        out_specs=[VMEM] * 6,
        scratch_shapes=[pltpu.SemaphoreType.DMA((6,))],
        compiler_params=pltpu.CompilerParams(vmem_limit_bytes=24 * 2**20),
    )(*(pltpu.with_memory_space_constraint(x, pltpu.HBM) for x in sources))
    ahead1 = swap(green1, "atom", 0)
    ahead0 = swap(green0, "atom", 0)
    by_core, by_cross = swap(green, "energy", 0), swap(green, "energy", 1)
    total0, total1 = call(own_kernel, [spread] * 2, (green0, green1), parts=2)
    ahead0, total0, total1 = lax.optimization_barrier((ahead0, total0, total1))
    across0 = forward(ahead0, "atom")
    green1, ahead0 = lax.optimization_barrier((green1, ahead0))
    across1 = swap(green1, "atom", 1)
    (total0,) = call(pair_kernel, [spread], (ahead0, total0))
    ahead1, total0 = lax.optimization_barrier((ahead1, total0))
    total0, core0, cross0 = call(far_kernel, [spread, edge, edge], (across0, total0))
    core0, cross0 = swap(core0, "energy", 0), swap(cross0, "energy", 1)
    total1, turned, partial = call(
        turn_kernel,
        [spread, (2,) + spread, (a_local, orb, orb)],
        (ahead1, total1, total0, green, by_core, by_cross),
    )
    total1, core1, cross1, rate = call(
        functools.partial(last_kernel, 1.0 / (4.0 * points)),
        [spread, edge, edge, (a_local, orb)],
        (across1, total1, turned, partial),
    )
    core1, cross1 = swap(core1, "energy", 0), swap(cross1, "energy", 1)
    cross0, core0, rate = lax.optimization_barrier((cross0, core0, rate))
    rates = addends(rate, "energy")
    return pl.pallas_call(
        end_kernel,
        out_shape=[
            jax.ShapeDtypeStruct(green.shape, jnp.float32),
            jax.ShapeDtypeStruct((a_local, orb), jnp.float32),
        ],
        in_specs=[VMEM] * (6 + len(rates)),
        out_specs=[VMEM] * 2,
        compiler_params=pltpu.CompilerParams(vmem_limit_bytes=24 * 2**20),
        cost_estimate=pl.CostEstimate(flops=10**6, bytes_accessed=2 * 10**6, transcendentals=0),
    )(total0, total1, cross0, core0, cross1, core1, *rates)


def solution(mesh):
    return jax.shard_map(
        per_device,
        mesh=mesh,
        in_specs=(
            P(None, "energy", "atom", None, None),
            P("atom", None, None, None),
            P("atom", None, None),
            P("atom", None),
        ),
        out_specs=(P(None, "energy", "atom", None, None), P("atom", None)),
        check_vma=False,
    )
```

```python
import functools

import jax
import jax.numpy as jnp
from jax import lax
from jax.experimental import pallas as pl
from jax.experimental.pallas import tpu as pltpu
from jax.sharding import PartitionSpec as P

SHIFTS = (-2, -1, 1, 2)
REACH = max(SHIFTS)
OWN, PAIR, FAR = 0, 1, 2
FEW = 4
VMEM = pl.BlockSpec(memory_space=pltpu.VMEM)
SMEM = pl.BlockSpec(memory_space=pltpu.SMEM)
ANY = pl.BlockSpec(memory_space=pl.ANY)


def halves(x):
    high = x.astype(jnp.bfloat16)
    return high, (x - high.astype(jnp.float32)).astype(jnp.bfloat16)


def swap(x, axis, first, close=False):
    size = lax.axis_size(axis)
    pairs = [(i, i + 1) for i in range(first, size - 1, 2)]
    if close and first == 1 and size % 2 == 0:
        pairs.append((0, size - 1))
    return lax.ppermute(x, axis, pairs + [(j, i) for i, j in pairs])


def forward(x, axis):
    size = lax.axis_size(axis)
    ups = [(i, i + 2) for i in range(0, size - 2, 2)]
    downs = [(i + 2, i) for i in range(1, size - 2, 2)]
    return lax.ppermute(x, axis, ups + downs)


def put_blocks(blocks, c, green):
    orb = green.shape[-1]
    for e in range(green.shape[0]):
        for a in range(green.shape[1]):
            high, low = halves(green[e, a])
            blocks[c, a, e, :, :orb] = high
            blocks[c, a, e, :, orb:] = low


def add_pairs(group, neighbours, phonon, coupling, blocks, totals, picked, size):
    atoms, slots, orb = coupling.shape[0], coupling.shape[1], coupling.shape[-1]
    e_local = blocks.shape[2]
    index = lax.axis_index("atom")
    base = index * atoms
    if group != OWN:
        upper = (index & 1) == (0 if group == PAIR else 1)
        base += jnp.where(upper, atoms, -atoms)

    found = jnp.int32(0)
    for a in range(atoms):
        for j in range(slots):
            picked[found] = a * slots + j
            b = neighbours[a, j] - base
            found += ((b >= 0) & (b < atoms)).astype(jnp.int32)

    def batch(step, _):
        pairs = []
        for u in range(size):
            at = step * size + u
            item = picked[jnp.minimum(at, found - 1)]
            a = item // slots
            j = item - a * slots
            high, low = halves(coupling[a, j])
            left = jnp.concatenate([high, low], 1)
            right = jnp.concatenate(
                [jnp.concatenate([high, high], 1), jnp.concatenate([low, low], 1)], 0
            )
            pairs.append((a, j, neighbours[a, j] - base, jnp.where(at < found, 1.0, 0.0), left, right))
        inners = []
        for a, j, b, live, left, right in pairs:
            for c in range(len(totals)):
                near = blocks[c, b].reshape(e_local * orb, 2 * orb)
                inner = lax.dot_general(
                    near, right, (((1,), (1,)), ((), ())), preferred_element_type=jnp.float32
                )
                inners.append(inner[:, :orb] + inner[:, orb:])
        results = []
        for a, j, b, live, left, right in pairs:
            for total in totals:
                inner = inners.pop(0)
                sums = [None] * (e_local + 2 * REACH)
                for e in range(e_local):
                    high, low = halves(inner[e * orb : (e + 1) * orb])
                    both = jnp.concatenate([high, low], 1)
                    outer = jnp.dot(
                        left, jnp.concatenate([both, both], 0), preferred_element_type=jnp.float32
                    )
                    outer = outer[:, :orb] + outer[:, orb:]
                    for k, s in enumerate(SHIFTS):
                        d = e - s + REACH
                        term = (phonon[a, k, j] * live) * outer
                        sums[d] = term if sums[d] is None else sums[d] + term
                results.append((total, a, sums))
        for total, a, sums in results:
            for d, value in enumerate(sums):
                if value is not None:
                    total[d, a] += value

    lax.fori_loop(0, (found + size - 1) // size, batch, None)


def fetch_kernel(green, coupling, phonon, neighbours, *rest):
    *results, sems = rest
    sources = [green.at[0], green.at[1], green, coupling, phonon, neighbours]
    copies = [
        pltpu.make_async_copy(source, result, sems.at[i])
        for i, (source, result) in enumerate(zip(sources, results))
    ]
    for copy in copies:
        copy.start()
    for copy in copies:
        copy.wait()


def own_kernel(neighbours, phonon, coupling, green0, green1, total0, total1, blocks, picked):
    for c, (green, total) in enumerate(((green0, total0), (green1, total1))):
        put_blocks(blocks, c, green)
        total[...] = jnp.zeros_like(total)
    add_pairs(OWN, neighbours, phonon, coupling, blocks, (total0, total1), picked, 2)


def pair_kernel(
    size, neighbours, phonon, coupling, ahead0, ahead1, before0, before1, green, by_core, by_cross,
    total0, total1, turned, blocks, picked,
):
    e_local, a_local = green.shape[1], green.shape[2]
    core, cross = partner_energies(turned.shape[1])
    has_core, has_cross = has_partners(size)
    for c in range(2):
        for a in range(a_local):
            for e in range(e_local):
                turned[c, REACH + e, a] = green[c, e, a].T
            for e in range(REACH):
                turned[c, core + e, a] = by_core[c, e, a].T * has_core
                turned[c, cross + e, a] = by_cross[c, e, a].T * has_cross
    total0[...] = before0[...]
    total1[...] = before1[...]
    put_blocks(blocks, 0, ahead0)
    put_blocks(blocks, 1, ahead1)
    add_pairs(PAIR, neighbours, phonon, coupling, blocks, (total0, total1), picked, 2)


def partner_energies(spread):
    odd = lax.axis_index("energy") & 1
    return jnp.where(odd == 0, spread - REACH, 0), jnp.where(odd == 0, 0, spread - REACH)


def has_partners(size):
    me = lax.axis_index("energy")
    above, below = jnp.where(me < size - 1, 1.0, 0.0), jnp.where(me > 0, 1.0, 0.0)
    odd = me & 1
    return jnp.where(odd == 0, above, below), jnp.where(odd == 0, below, above)


def finish(total, core, cross):
    to_core, to_cross = partner_energies(total.shape[0])
    for e in range(REACH):
        core[e] = total[to_core + e]
        cross[e] = total[to_cross + e]


def rate_sums(total, turned, c, a):
    sums = total[0, a] * turned[c, 0, a]
    for d in range(1, total.shape[0]):
        sums += total[d, a] * turned[c, d, a]
    return sums


def far_kernel(
    neighbours, phonon, coupling, across, before, turned, total, core, cross, partial, blocks, picked
):
    add_far(neighbours, phonon, coupling, across, before, total, blocks, picked)
    finish(total, core, cross)
    for a in range(partial.shape[0]):
        partial[a] = rate_sums(total, turned, 0, a)


def add_far(neighbours, phonon, coupling, across, before, total, blocks, picked):
    total[...] = before[...]
    put_blocks(blocks, 0, across)
    add_pairs(FAR, neighbours, phonon, coupling, blocks, (total,), picked, 4)


def last_kernel(
    scale, neighbours, phonon, coupling, across, before, turned, partial,
    total, core, cross, rate, blocks, picked,
):
    add_far(neighbours, phonon, coupling, across, before, total, blocks, picked)
    finish(total, core, cross)
    for a in range(partial.shape[0]):
        sums = partial[a] - rate_sums(total, turned, 1, a)
        rate[a : a + 1, :] = jnp.sum(sums.T, axis=0, keepdims=True) * scale


def addends(x, axis):
    size = lax.axis_size(axis)
    if size > FEW:
        return [lax.psum(x, axis)]
    turns = [[(i, (i + k) % size) for i in range(size)] for k in range(1, size)]
    return [x] + [lax.ppermute(x, axis, turn) for turn in turns]


def end_kernel(size, total0, total1, cross0, core0, cross1, core1, *rest):
    *rates, out, rate = rest
    e_local = out.shape[1]
    has_core, has_cross = has_partners(size)
    for c, (total, cross, core) in enumerate(((total0, cross0, core0), (total1, cross1, core1))):
        for e in range(e_local):
            out[c, e] = total[REACH + e] + core[e] * has_core + cross[e] * has_cross
    rate[...] = sum(r[...] for r in rates)


def per_device(green, coupling, phonon, neighbours):
    _, e_local, a_local, orb, _ = green.shape
    energies = lax.axis_size("energy")
    points = e_local * energies
    spread = (e_local + 2 * REACH, a_local, orb, orb)
    edge = (REACH, a_local, orb, orb)

    def call(kernel, out, operands, parts=1):
        return pl.pallas_call(
            kernel,
            out_shape=[jax.ShapeDtypeStruct(shape, jnp.float32) for shape in out],
            in_specs=[SMEM, SMEM] + [VMEM] * (1 + len(operands)),
            out_specs=[VMEM] * len(out),
            scratch_shapes=[
                pltpu.VMEM((parts, a_local, e_local, orb, 2 * orb), jnp.bfloat16),
                pltpu.SMEM((a_local * neighbours.shape[1] + 1,), jnp.int32),
            ],
            compiler_params=pltpu.CompilerParams(vmem_limit_bytes=24 * 2**20),
            cost_estimate=pl.CostEstimate(flops=10**6, bytes_accessed=10**4, transcendentals=0),
        )(neighbours, phonon, coupling, *operands)

    sources = (green, coupling, jnp.swapaxes(phonon, 1, 2), neighbours)
    green0, green1, green, coupling, phonon, neighbours = pl.pallas_call(
        fetch_kernel,
        out_shape=[jax.ShapeDtypeStruct(green.shape[1:], green.dtype)] * 2
        + [jax.ShapeDtypeStruct(x.shape, x.dtype) for x in sources],
        in_specs=[ANY] * 4,
        out_specs=[VMEM] * 6,
        scratch_shapes=[pltpu.SemaphoreType.DMA((6,))],
        compiler_params=pltpu.CompilerParams(vmem_limit_bytes=24 * 2**20),
    )(*(pltpu.with_memory_space_constraint(x, pltpu.HBM) for x in sources))
    ahead1 = swap(green1, "atom", 0)
    ahead0 = swap(green0, "atom", 0)
    by_core, by_cross = swap(green, "energy", 0), swap(green, "energy", 1, close=True)
    total0, total1 = call(own_kernel, [spread] * 2, (green0, green1), parts=2)
    ahead0, total0, total1 = lax.optimization_barrier((ahead0, total0, total1))
    across0 = forward(ahead0, "atom")
    green1, ahead0 = lax.optimization_barrier((green1, ahead0))
    across1 = swap(green1, "atom", 1)
    total0, total1, turned = call(
        functools.partial(pair_kernel, energies),
        [spread, spread, (2,) + spread],
        (ahead0, ahead1, total0, total1, green, by_core, by_cross),
        parts=2,
    )
    total0, core0, cross0, partial = call(
        far_kernel, [spread, edge, edge, (a_local, orb, orb)], (across0, total0, turned)
    )
    core0, cross0 = swap(core0, "energy", 0), swap(cross0, "energy", 1, close=True)
    total1, core1, cross1, rate = call(
        functools.partial(last_kernel, 1.0 / (4.0 * points)),
        [spread, edge, edge, (a_local, orb)],
        (across1, total1, turned, partial),
    )
    core1, cross1 = swap(core1, "energy", 0), swap(cross1, "energy", 1)
    cross0, core0, rate = lax.optimization_barrier((cross0, core0, rate))
    rates = addends(rate, "energy")
    return pl.pallas_call(
        functools.partial(end_kernel, energies),
        out_shape=[
            jax.ShapeDtypeStruct(green.shape, jnp.float32),
            jax.ShapeDtypeStruct((a_local, orb), jnp.float32),
        ],
        in_specs=[VMEM] * (6 + len(rates)),
        out_specs=[VMEM] * 2,
        compiler_params=pltpu.CompilerParams(vmem_limit_bytes=24 * 2**20),
        cost_estimate=pl.CostEstimate(flops=10**6, bytes_accessed=2 * 10**6, transcendentals=0),
    )(total0, total1, cross0, core0, cross1, core1, *rates)


def solution(mesh):
    return jax.shard_map(
        per_device,
        mesh=mesh,
        in_specs=(
            P(None, "energy", "atom", None, None),
            P("atom", None, None, None),
            P("atom", None, None),
            P("atom", None),
        ),
        out_specs=(P(None, "energy", "atom", None, None), P("atom", None)),
        check_vma=False,
    )
```

```python
import functools

import jax
import jax.numpy as jnp
from jax import lax
from jax.experimental import pallas as pl
from jax.experimental.pallas import tpu as pltpu
from jax.sharding import PartitionSpec as P

SHIFTS = (-2, -1, 1, 2)
REACH = max(SHIFTS)
OWN, PAIR, FAR = 0, 1, 2
FEW = 4
VMEM = pl.BlockSpec(memory_space=pltpu.VMEM)
SMEM = pl.BlockSpec(memory_space=pltpu.SMEM)
ANY = pl.BlockSpec(memory_space=pl.ANY)


def halves(x):
    high = x.astype(jnp.bfloat16)
    return high, (x - high.astype(jnp.float32)).astype(jnp.bfloat16)


def swap(x, axis, first, close=False):
    size = lax.axis_size(axis)
    pairs = [(i, i + 1) for i in range(first, size - 1, 2)]
    if close and first == 1 and size % 2 == 0:
        pairs.append((0, size - 1))
    return lax.ppermute(x, axis, pairs + [(j, i) for i, j in pairs])


def forward(x, axis):
    size = lax.axis_size(axis)
    ups = [(i, i + 2) for i in range(0, size - 2, 2)]
    downs = [(i + 2, i) for i in range(1, size - 2, 2)]
    return lax.ppermute(x, axis, ups + downs)


def put_blocks(blocks, c, green):
    orb = green.shape[-1]
    for e in range(green.shape[0]):
        for a in range(green.shape[1]):
            high, low = halves(green[e, a])
            blocks[c, a, e, :, :orb] = high
            blocks[c, a, e, :, orb:] = low


def add_pairs(group, neighbours, phonon, coupling, blocks, totals, picked, size):
    atoms, slots, orb = coupling.shape[0], coupling.shape[1], coupling.shape[-1]
    e_local = blocks.shape[2]
    index = lax.axis_index("atom")
    base = index * atoms
    if group != OWN:
        upper = (index & 1) == (0 if group == PAIR else 1)
        base += jnp.where(upper, atoms, -atoms)

    found = jnp.int32(0)
    for a in range(atoms):
        for j in range(slots):
            picked[found] = a * slots + j
            b = neighbours[a, j] - base
            found += ((b >= 0) & (b < atoms)).astype(jnp.int32)

    def batch(step, _):
        pairs = []
        for u in range(size):
            at = step * size + u
            item = picked[jnp.minimum(at, found - 1)]
            a = item // slots
            j = item - a * slots
            high, low = halves(coupling[a, j])
            left = jnp.concatenate([high, low], 1)
            right = jnp.concatenate(
                [jnp.concatenate([high, high], 1), jnp.concatenate([low, low], 1)], 0
            )
            pairs.append((a, j, neighbours[a, j] - base, jnp.where(at < found, 1.0, 0.0), left, right))
        inners = []
        for a, j, b, live, left, right in pairs:
            for c in range(len(totals)):
                near = blocks[c, b].reshape(e_local * orb, 2 * orb)
                inner = lax.dot_general(
                    near, right, (((1,), (1,)), ((), ())), preferred_element_type=jnp.float32
                )
                inners.append(inner[:, :orb] + inner[:, orb:])
        results = []
        for a, j, b, live, left, right in pairs:
            for total in totals:
                inner = inners.pop(0)
                sums = [None] * (e_local + 2 * REACH)
                for e in range(e_local):
                    high, low = halves(inner[e * orb : (e + 1) * orb])
                    both = jnp.concatenate([high, low], 1)
                    outer = jnp.dot(
                        left, jnp.concatenate([both, both], 0), preferred_element_type=jnp.float32
                    )
                    outer = outer[:, :orb] + outer[:, orb:]
                    for k, s in enumerate(SHIFTS):
                        d = e - s + REACH
                        term = (phonon[a, k, j] * live) * outer
                        sums[d] = term if sums[d] is None else sums[d] + term
                results.append((total, a, sums))
        for total, a, sums in results:
            for d, value in enumerate(sums):
                if value is not None:
                    total[d, a] += value

    lax.fori_loop(0, (found + size - 1) // size, batch, None)


def fetch_kernel(green, coupling, phonon, neighbours, *rest):
    *results, sems = rest
    sources = [green.at[0], green.at[1], green, coupling, phonon, neighbours]
    copies = [
        pltpu.make_async_copy(source, result, sems.at[i])
        for i, (source, result) in enumerate(zip(sources, results))
    ]
    for copy in copies:
        copy.start()
    for copy in copies:
        copy.wait()


def own_kernel(neighbours, phonon, coupling, green0, green1, total0, total1, blocks, picked):
    for c, (green, total) in enumerate(((green0, total0), (green1, total1))):
        put_blocks(blocks, c, green)
        total[...] = jnp.zeros_like(total)
    add_pairs(OWN, neighbours, phonon, coupling, blocks, (total0, total1), picked, 2)


def pair_kernel(
    size, neighbours, phonon, coupling, ahead0, ahead1, before0, before1, green, by_core, by_cross,
    total0, total1, turned, blocks, picked,
):
    e_local, a_local = green.shape[1], green.shape[2]
    core, cross = partner_energies(turned.shape[1])
    has_core, has_cross = has_partners(size)
    for c in range(2):
        for a in range(a_local):
            for e in range(e_local):
                turned[c, REACH + e, a] = green[c, e, a].T
            for e in range(REACH):
                turned[c, core + e, a] = by_core[c, e, a].T * has_core
                turned[c, cross + e, a] = by_cross[c, e, a].T * has_cross
    total0[...] = before0[...]
    total1[...] = before1[...]
    put_blocks(blocks, 0, ahead0)
    put_blocks(blocks, 1, ahead1)
    add_pairs(PAIR, neighbours, phonon, coupling, blocks, (total0, total1), picked, 2)


def partner_energies(spread):
    odd = lax.axis_index("energy") & 1
    return jnp.where(odd == 0, spread - REACH, 0), jnp.where(odd == 0, 0, spread - REACH)


def has_partners(size):
    me = lax.axis_index("energy")
    above, below = jnp.where(me < size - 1, 1.0, 0.0), jnp.where(me > 0, 1.0, 0.0)
    odd = me & 1
    return jnp.where(odd == 0, above, below), jnp.where(odd == 0, below, above)


def finish(total, core, cross):
    to_core, to_cross = partner_energies(total.shape[0])
    for e in range(REACH):
        core[e] = total[to_core + e]
        cross[e] = total[to_cross + e]


def rate_sums(total, turned, c, a):
    sums = total[0, a] * turned[c, 0, a]
    for d in range(1, total.shape[0]):
        sums += total[d, a] * turned[c, d, a]
    return sums


def far_kernel(
    neighbours, phonon, coupling, across, before, turned, total, core, cross, partial, blocks, picked
):
    add_far(neighbours, phonon, coupling, across, before, total, blocks, picked)
    finish(total, core, cross)
    for a in range(partial.shape[0]):
        partial[a] = rate_sums(total, turned, 0, a)


def add_far(neighbours, phonon, coupling, across, before, total, blocks, picked):
    total[...] = before[...]
    put_blocks(blocks, 0, across)
    add_pairs(FAR, neighbours, phonon, coupling, blocks, (total,), picked, 4)


def last_kernel(
    scale, neighbours, phonon, coupling, across, before, turned, partial,
    total, core, cross, rate, blocks, picked,
):
    add_far(neighbours, phonon, coupling, across, before, total, blocks, picked)
    finish(total, core, cross)
    for a in range(partial.shape[0]):
        sums = partial[a] - rate_sums(total, turned, 1, a)
        rate[a : a + 1, :] = jnp.sum(sums.T, axis=0, keepdims=True) * scale


def addends(x, axis):
    size = lax.axis_size(axis)
    if size > FEW:
        return [lax.psum(x, axis)]
    turns = [[(i, (i + k) % size) for i in range(size)] for k in range(1, size)]
    return [x] + [lax.ppermute(x, axis, turn) for turn in turns]


def end_kernel(size, total0, total1, cross0, core0, cross1, core1, *rest):
    *rates, out, rate = rest
    e_local = out.shape[1]
    has_core, has_cross = has_partners(size)
    for c, (total, cross, core) in enumerate(((total0, cross0, core0), (total1, cross1, core1))):
        for e in range(e_local):
            out[c, e] = total[REACH + e] + core[e] * has_core + cross[e] * has_cross
    rate[...] = sum(r[...] for r in rates)


def per_device(green, coupling, phonon, neighbours):
    _, e_local, a_local, orb, _ = green.shape
    energies = lax.axis_size("energy")
    points = e_local * energies
    spread = (e_local + 2 * REACH, a_local, orb, orb)
    edge = (REACH, a_local, orb, orb)

    def call(kernel, out, operands, parts=1):
        return pl.pallas_call(
            kernel,
            out_shape=[jax.ShapeDtypeStruct(shape, jnp.float32) for shape in out],
            in_specs=[SMEM, SMEM] + [VMEM] * (1 + len(operands)),
            out_specs=[VMEM] * len(out),
            scratch_shapes=[
                pltpu.VMEM((parts, a_local, e_local, orb, 2 * orb), jnp.bfloat16),
                pltpu.SMEM((a_local * neighbours.shape[1] + 1,), jnp.int32),
            ],
            compiler_params=pltpu.CompilerParams(vmem_limit_bytes=24 * 2**20),
            cost_estimate=pl.CostEstimate(flops=10**6, bytes_accessed=10**4, transcendentals=0),
        )(neighbours, phonon, coupling, *operands)

    sources = (green, coupling, jnp.swapaxes(phonon, 1, 2), neighbours)
    green0, green1, green, coupling, phonon, neighbours = pl.pallas_call(
        fetch_kernel,
        out_shape=[jax.ShapeDtypeStruct(green.shape[1:], green.dtype)] * 2
        + [jax.ShapeDtypeStruct(x.shape, x.dtype) for x in sources],
        in_specs=[ANY] * 4,
        out_specs=[VMEM] * 6,
        scratch_shapes=[pltpu.SemaphoreType.DMA((6,))],
        compiler_params=pltpu.CompilerParams(vmem_limit_bytes=24 * 2**20),
    )(*(pltpu.with_memory_space_constraint(x, pltpu.HBM) for x in sources))
    ahead1 = swap(green1, "atom", 0)
    ahead0 = swap(green0, "atom", 0)
    by_core, by_cross = swap(green, "energy", 0), swap(green, "energy", 1, close=True)
    total0, total1 = call(own_kernel, [spread] * 2, (green0, green1), parts=2)
    ahead0, total0, total1 = lax.optimization_barrier((ahead0, total0, total1))
    across0 = forward(ahead0, "atom")
    green1, ahead0 = lax.optimization_barrier((green1, ahead0))
    across1 = swap(green1, "atom", 1)
    total0, total1, turned = call(
        functools.partial(pair_kernel, energies),
        [spread, spread, (2,) + spread],
        (ahead0, ahead1, total0, total1, green, by_core, by_cross),
        parts=2,
    )
    total0, core0, cross0, partial = call(
        far_kernel, [spread, edge, edge, (a_local, orb, orb)], (across0, total0, turned)
    )
    core0, cross0 = swap(core0, "energy", 0), swap(cross0, "energy", 1, close=True)
    total1, core1, cross1, rate = call(
        functools.partial(last_kernel, 1.0 / (4.0 * points)),
        [spread, edge, edge, (a_local, orb)],
        (across1, total1, turned, partial),
    )
    cross1 = swap(cross1, "energy", 1)
    core0, rate = lax.optimization_barrier((core0, rate))
    rates = addends(rate, "energy")
    cross0, core1, rates = lax.optimization_barrier((cross0, core1, rates))
    core1 = swap(core1, "energy", 0)
    return pl.pallas_call(
        functools.partial(end_kernel, energies),
        out_shape=[
            jax.ShapeDtypeStruct(green.shape, jnp.float32),
            jax.ShapeDtypeStruct((a_local, orb), jnp.float32),
        ],
        in_specs=[VMEM] * (6 + len(rates)),
        out_specs=[VMEM] * 2,
        compiler_params=pltpu.CompilerParams(vmem_limit_bytes=24 * 2**20),
        cost_estimate=pl.CostEstimate(flops=10**6, bytes_accessed=2 * 10**6, transcendentals=0),
    )(total0, total1, cross0, core0, cross1, core1, *rates)


def solution(mesh):
    return jax.shard_map(
        per_device,
        mesh=mesh,
        in_specs=(
            P(None, "energy", "atom", None, None),
            P("atom", None, None, None),
            P("atom", None, None),
            P("atom", None),
        ),
        out_specs=(P(None, "energy", "atom", None, None), P("atom", None)),
        check_vma=False,
    )
```

```python
import functools

import jax
import jax.numpy as jnp
from jax import lax
from jax.experimental import pallas as pl
from jax.experimental.pallas import tpu as pltpu
from jax.sharding import PartitionSpec as P

SHIFTS = (-2, -1, 1, 2)
REACH = max(SHIFTS)
OWN, PAIR, FAR = 0, 1, 2
FEW = 4
VMEM = pl.BlockSpec(memory_space=pltpu.VMEM)
SMEM = pl.BlockSpec(memory_space=pltpu.SMEM)
ANY = pl.BlockSpec(memory_space=pl.ANY)


def halves(x):
    high = x.astype(jnp.bfloat16)
    return high, (x - high.astype(jnp.float32)).astype(jnp.bfloat16)


def swap(x, axis, first, close=False):
    size = lax.axis_size(axis)
    pairs = [(i, i + 1) for i in range(first, size - 1, 2)]
    if close and first == 1 and size % 2 == 0:
        pairs.append((0, size - 1))
    return lax.ppermute(x, axis, pairs + [(j, i) for i, j in pairs])


def forward(x, axis):
    size = lax.axis_size(axis)
    ups = [(i, i + 2) for i in range(0, size - 2, 2)]
    downs = [(i + 2, i) for i in range(1, size - 2, 2)]
    return lax.ppermute(x, axis, ups + downs)


def put_blocks(blocks, c, green):
    orb = green.shape[-1]
    for e in range(green.shape[0]):
        for a in range(green.shape[1]):
            high, low = halves(green[e, a])
            blocks[c, a, e, :, :orb] = high
            blocks[c, a, e, :, orb:] = low


def add_pairs(group, neighbours, phonon, coupling, blocks, totals, picked, size):
    atoms, slots, orb = coupling.shape[0], coupling.shape[1], coupling.shape[-1]
    e_local = blocks.shape[2]
    index = lax.axis_index("atom")
    base = index * atoms
    if group != OWN:
        upper = (index & 1) == (0 if group == PAIR else 1)
        base += jnp.where(upper, atoms, -atoms)

    found = jnp.int32(0)
    for a in range(atoms):
        for j in range(slots):
            picked[found] = a * slots + j
            b = neighbours[a, j] - base
            found += ((b >= 0) & (b < atoms)).astype(jnp.int32)

    def batch(step, _):
        pairs = []
        for u in range(size):
            at = step * size + u
            item = picked[jnp.minimum(at, found - 1)]
            a = item // slots
            j = item - a * slots
            high, low = halves(coupling[a, j])
            left = jnp.concatenate([high, low], 1)
            right = jnp.concatenate(
                [jnp.concatenate([high, high], 1), jnp.concatenate([low, low], 1)], 0
            )
            pairs.append((a, j, neighbours[a, j] - base, jnp.where(at < found, 1.0, 0.0), left, right))
        inners = []
        for a, j, b, live, left, right in pairs:
            for c in range(len(totals)):
                near = blocks[c, b].reshape(e_local * orb, 2 * orb)
                inner = lax.dot_general(
                    near, right, (((1,), (1,)), ((), ())), preferred_element_type=jnp.float32
                )
                inners.append(inner[:, :orb] + inner[:, orb:])
        results = []
        for a, j, b, live, left, right in pairs:
            for total in totals:
                inner = inners.pop(0)
                sums = [None] * (e_local + 2 * REACH)
                for e in range(e_local):
                    high, low = halves(inner[e * orb : (e + 1) * orb])
                    both = jnp.concatenate([high, low], 1)
                    outer = jnp.dot(
                        left, jnp.concatenate([both, both], 0), preferred_element_type=jnp.float32
                    )
                    outer = outer[:, :orb] + outer[:, orb:]
                    for k, s in enumerate(SHIFTS):
                        d = e - s + REACH
                        term = (phonon[a, k, j] * live) * outer
                        sums[d] = term if sums[d] is None else sums[d] + term
                results.append((total, a, sums))
        for total, a, sums in results:
            for d, value in enumerate(sums):
                if value is not None:
                    total[d, a] += value

    lax.fori_loop(0, (found + size - 1) // size, batch, None)


def fetch_kernel(green, coupling, phonon, neighbours, *rest):
    *results, sems = rest
    sources = [green.at[0], green.at[1], green, coupling, phonon, neighbours]
    copies = [
        pltpu.make_async_copy(source, result, sems.at[i])
        for i, (source, result) in enumerate(zip(sources, results))
    ]
    for copy in copies:
        copy.start()
    for copy in copies:
        copy.wait()


def own_kernel(neighbours, phonon, coupling, green0, green1, total0, total1, blocks, picked):
    for c, (green, total) in enumerate(((green0, total0), (green1, total1))):
        put_blocks(blocks, c, green)
        total[...] = jnp.zeros_like(total)
    add_pairs(OWN, neighbours, phonon, coupling, blocks, (total0, total1), picked, 2)


def pair_kernel(
    size, neighbours, phonon, coupling, ahead0, ahead1, before0, before1, green, by_core, by_cross,
    total0, total1, turned, blocks, picked,
):
    e_local, a_local = green.shape[1], green.shape[2]
    core, cross = partner_energies(turned.shape[1])
    has_core, has_cross = has_partners(size)
    for c in range(2):
        for a in range(a_local):
            for e in range(e_local):
                turned[c, REACH + e, a] = green[c, e, a].T
            for e in range(REACH):
                turned[c, core + e, a] = by_core[c, e, a].T * has_core
                turned[c, cross + e, a] = by_cross[c, e, a].T * has_cross
    total0[...] = before0[...]
    total1[...] = before1[...]
    put_blocks(blocks, 0, ahead0)
    put_blocks(blocks, 1, ahead1)
    add_pairs(PAIR, neighbours, phonon, coupling, blocks, (total0, total1), picked, 2)


def partner_energies(spread):
    odd = lax.axis_index("energy") & 1
    return jnp.where(odd == 0, spread - REACH, 0), jnp.where(odd == 0, 0, spread - REACH)


def has_partners(size):
    me = lax.axis_index("energy")
    above, below = jnp.where(me < size - 1, 1.0, 0.0), jnp.where(me > 0, 1.0, 0.0)
    odd = me & 1
    return jnp.where(odd == 0, above, below), jnp.where(odd == 0, below, above)


def finish(total, core, cross):
    to_core, to_cross = partner_energies(total.shape[0])
    for e in range(REACH):
        core[e] = total[to_core + e]
        cross[e] = total[to_cross + e]


def rate_sums(total, turned, c, a):
    sums = total[0, a] * turned[c, 0, a]
    for d in range(1, total.shape[0]):
        sums += total[d, a] * turned[c, d, a]
    return sums


def far_kernel(
    neighbours, phonon, coupling, across, before, turned, total, core, cross, partial, blocks, picked
):
    add_far(neighbours, phonon, coupling, across, before, total, blocks, picked)
    finish(total, core, cross)
    for a in range(partial.shape[0]):
        partial[a] = rate_sums(total, turned, 0, a)


def add_far(neighbours, phonon, coupling, across, before, total, blocks, picked):
    total[...] = before[...]
    put_blocks(blocks, 0, across)
    add_pairs(FAR, neighbours, phonon, coupling, blocks, (total,), picked, 4)


def last_kernel(
    scale, neighbours, phonon, coupling, across, before, turned, partial,
    total, core, cross, rate, blocks, picked,
):
    add_far(neighbours, phonon, coupling, across, before, total, blocks, picked)
    finish(total, core, cross)
    for a in range(partial.shape[0]):
        sums = partial[a] - rate_sums(total, turned, 1, a)
        rate[a : a + 1, :] = jnp.sum(sums.T, axis=0, keepdims=True) * scale


def addends(x, axis):
    size = lax.axis_size(axis)
    if size > FEW:
        return [lax.psum(x, axis)]
    turns = [[(i, (i + k) % size) for i in range(size)] for k in range(1, size)]
    return [x] + [lax.ppermute(x, axis, turn) for turn in turns]


def end_kernel(size, total0, total1, cross0, core0, cross1, core1, *rest):
    *rates, out, rate = rest
    e_local = out.shape[1]
    has_core, has_cross = has_partners(size)
    for c, (total, cross, core) in enumerate(((total0, cross0, core0), (total1, cross1, core1))):
        for e in range(e_local):
            out[c, e] = total[REACH + e] + core[e] * has_core + cross[e] * has_cross
    rate[...] = sum(r[...] for r in rates)


def per_device(green, coupling, phonon, neighbours):
    _, e_local, a_local, orb, _ = green.shape
    energies = lax.axis_size("energy")
    points = e_local * energies
    spread = (e_local + 2 * REACH, a_local, orb, orb)
    edge = (REACH, a_local, orb, orb)

    def call(kernel, out, operands, parts=1):
        return pl.pallas_call(
            kernel,
            out_shape=[jax.ShapeDtypeStruct(shape, jnp.float32) for shape in out],
            in_specs=[SMEM, SMEM] + [VMEM] * (1 + len(operands)),
            out_specs=[VMEM] * len(out),
            scratch_shapes=[
                pltpu.VMEM((parts, a_local, e_local, orb, 2 * orb), jnp.bfloat16),
                pltpu.SMEM((a_local * neighbours.shape[1] + 1,), jnp.int32),
            ],
            compiler_params=pltpu.CompilerParams(vmem_limit_bytes=24 * 2**20),
            cost_estimate=pl.CostEstimate(flops=10**6, bytes_accessed=10**4, transcendentals=0),
        )(neighbours, phonon, coupling, *operands)

    sources = (green, coupling, jnp.swapaxes(phonon, 1, 2), neighbours)
    green0, green1, green, coupling, phonon, neighbours = pl.pallas_call(
        fetch_kernel,
        out_shape=[jax.ShapeDtypeStruct(green.shape[1:], green.dtype)] * 2
        + [jax.ShapeDtypeStruct(x.shape, x.dtype) for x in sources],
        in_specs=[ANY] * 4,
        out_specs=[VMEM] * 6,
        scratch_shapes=[pltpu.SemaphoreType.DMA((6,))],
        compiler_params=pltpu.CompilerParams(vmem_limit_bytes=24 * 2**20),
    )(*(pltpu.with_memory_space_constraint(x, pltpu.HBM) for x in sources))
    ahead1 = swap(green1, "atom", 0)
    ahead0 = swap(green0, "atom", 0)
    by_core, by_cross = swap(green, "energy", 0), swap(green, "energy", 1, close=True)
    total0, total1 = call(own_kernel, [spread] * 2, (green0, green1), parts=2)
    ahead0, total0, total1 = lax.optimization_barrier((ahead0, total0, total1))
    across0 = forward(ahead0, "atom")
    green1, ahead0 = lax.optimization_barrier((green1, ahead0))
    across1 = swap(green1, "atom", 1, close=True)
    total0, total1, turned = call(
        functools.partial(pair_kernel, energies),
        [spread, spread, (2,) + spread],
        (ahead0, ahead1, total0, total1, green, by_core, by_cross),
        parts=2,
    )
    total0, core0, cross0, partial = call(
        far_kernel, [spread, edge, edge, (a_local, orb, orb)], (across0, total0, turned)
    )
    core0, cross0 = swap(core0, "energy", 0), swap(cross0, "energy", 1, close=True)
    total1, core1, cross1, rate = call(
        functools.partial(last_kernel, 1.0 / (4.0 * points)),
        [spread, edge, edge, (a_local, orb)],
        (across1, total1, turned, partial),
    )
    core1, cross1 = swap(core1, "energy", 0), swap(cross1, "energy", 1)
    cross0, core0, rate = lax.optimization_barrier((cross0, core0, rate))
    rates = addends(rate, "energy")
    return pl.pallas_call(
        functools.partial(end_kernel, energies),
        out_shape=[
            jax.ShapeDtypeStruct(green.shape, jnp.float32),
            jax.ShapeDtypeStruct((a_local, orb), jnp.float32),
        ],
        in_specs=[VMEM] * (6 + len(rates)),
        out_specs=[VMEM] * 2,
        compiler_params=pltpu.CompilerParams(vmem_limit_bytes=24 * 2**20),
        cost_estimate=pl.CostEstimate(flops=10**6, bytes_accessed=2 * 10**6, transcendentals=0),
    )(total0, total1, cross0, core0, cross1, core1, *rates)


def solution(mesh):
    return jax.shard_map(
        per_device,
        mesh=mesh,
        in_specs=(
            P(None, "energy", "atom", None, None),
            P("atom", None, None, None),
            P("atom", None, None),
            P("atom", None),
        ),
        out_specs=(P(None, "energy", "atom", None, None), P("atom", None)),
        check_vma=False,
    )
```

```python
import functools

import jax
import jax.numpy as jnp
from jax import lax
from jax.experimental import pallas as pl
from jax.experimental.pallas import tpu as pltpu
from jax.sharding import PartitionSpec as P

SHIFTS = (-2, -1, 1, 2)
REACH = max(SHIFTS)
OWN, PAIR, FAR = 0, 1, 2
FEW = 4
VMEM = pl.BlockSpec(memory_space=pltpu.VMEM)
SMEM = pl.BlockSpec(memory_space=pltpu.SMEM)
ANY = pl.BlockSpec(memory_space=pl.ANY)


def halves(x):
    high = x.astype(jnp.bfloat16)
    return high, (x - high.astype(jnp.float32)).astype(jnp.bfloat16)


def swap(x, axis, first, close=False):
    size = lax.axis_size(axis)
    pairs = [(i, i + 1) for i in range(first, size - 1, 2)]
    if close and first == 1 and size % 2 == 0:
        pairs.append((0, size - 1))
    return lax.ppermute(x, axis, pairs + [(j, i) for i, j in pairs])


def cross_swap(x):
    energies, atoms = lax.axis_size("energy"), lax.axis_size("atom")
    perm = []
    for e in range(energies):
        other = e + 1 if e % 2 else e - 1
        for a in range(atoms):
            if 0 <= other < energies:
                perm.append((e * atoms + a, other * atoms + a))
            elif atoms % 2 == 0:
                perm.append((e * atoms + a, e * atoms + (a ^ 1)))
    return lax.ppermute(x, ("energy", "atom"), perm)


def forward(x, axis):
    size = lax.axis_size(axis)
    steps = [(i, i + 2 if i % 2 == 0 else i - 2) for i in range(size)]
    if size % 2 == 0 and size > 2:
        return lax.ppermute(x, axis, [(i, j % size) for i, j in steps])
    return lax.ppermute(x, axis, [(i, j) for i, j in steps if 0 <= j < size])


def put_blocks(blocks, c, green):
    orb = green.shape[-1]
    for e in range(green.shape[0]):
        for a in range(green.shape[1]):
            high, low = halves(green[e, a])
            blocks[c, a, e, :, :orb] = high
            blocks[c, a, e, :, orb:] = low


def add_pairs(group, neighbours, phonon, coupling, blocks, totals, picked, size):
    atoms, slots, orb = coupling.shape[0], coupling.shape[1], coupling.shape[-1]
    e_local = blocks.shape[2]
    index = lax.axis_index("atom")
    base = index * atoms
    if group != OWN:
        upper = (index & 1) == (0 if group == PAIR else 1)
        base += jnp.where(upper, atoms, -atoms)

    found = jnp.int32(0)
    for a in range(atoms):
        for j in range(slots):
            picked[found] = a * slots + j
            b = neighbours[a, j] - base
            found += ((b >= 0) & (b < atoms)).astype(jnp.int32)

    def batch(step, _):
        pairs = []
        for u in range(size):
            at = step * size + u
            item = picked[jnp.minimum(at, found - 1)]
            a = item // slots
            j = item - a * slots
            high, low = halves(coupling[a, j])
            left = jnp.concatenate([high, low], 1)
            right = jnp.concatenate(
                [jnp.concatenate([high, high], 1), jnp.concatenate([low, low], 1)], 0
            )
            pairs.append((a, j, neighbours[a, j] - base, jnp.where(at < found, 1.0, 0.0), left, right))
        inners = []
        for a, j, b, live, left, right in pairs:
            for c in range(len(totals)):
                near = blocks[c, b].reshape(e_local * orb, 2 * orb)
                inner = lax.dot_general(
                    near, right, (((1,), (1,)), ((), ())), preferred_element_type=jnp.float32
                )
                inners.append(inner[:, :orb] + inner[:, orb:])
        results = []
        for a, j, b, live, left, right in pairs:
            for total in totals:
                inner = inners.pop(0)
                sums = [None] * (e_local + 2 * REACH)
                for e in range(e_local):
                    high, low = halves(inner[e * orb : (e + 1) * orb])
                    both = jnp.concatenate([high, low], 1)
                    outer = jnp.dot(
                        left, jnp.concatenate([both, both], 0), preferred_element_type=jnp.float32
                    )
                    outer = outer[:, :orb] + outer[:, orb:]
                    for k, s in enumerate(SHIFTS):
                        d = e - s + REACH
                        term = (phonon[a, k, j] * live) * outer
                        sums[d] = term if sums[d] is None else sums[d] + term
                results.append((total, a, sums))
        for total, a, sums in results:
            for d, value in enumerate(sums):
                if value is not None:
                    total[d, a] += value

    lax.fori_loop(0, (found + size - 1) // size, batch, None)


def fetch_kernel(green, coupling, phonon, neighbours, *rest):
    *results, sems = rest
    sources = [green.at[0], green.at[1], green, coupling, phonon, neighbours]
    copies = [
        pltpu.make_async_copy(source, result, sems.at[i])
        for i, (source, result) in enumerate(zip(sources, results))
    ]
    for copy in copies:
        copy.start()
    for copy in copies:
        copy.wait()


def own_kernel(neighbours, phonon, coupling, green0, green1, total0, total1, blocks, picked):
    for c, (green, total) in enumerate(((green0, total0), (green1, total1))):
        put_blocks(blocks, c, green)
        total[...] = jnp.zeros_like(total)
    add_pairs(OWN, neighbours, phonon, coupling, blocks, (total0, total1), picked, 2)


def pair_kernel(
    size, neighbours, phonon, coupling, ahead0, ahead1, before0, before1, green, by_core, by_cross,
    total0, total1, turned, blocks, picked,
):
    e_local, a_local = green.shape[1], green.shape[2]
    core, cross = partner_energies(turned.shape[1])
    has_core, has_cross = has_partners(size)
    for c in range(2):
        for a in range(a_local):
            for e in range(e_local):
                turned[c, REACH + e, a] = green[c, e, a].T
            for e in range(REACH):
                turned[c, core + e, a] = by_core[c, e, a].T * has_core
                turned[c, cross + e, a] = by_cross[c, e, a].T * has_cross
    total0[...] = before0[...]
    total1[...] = before1[...]
    put_blocks(blocks, 0, ahead0)
    put_blocks(blocks, 1, ahead1)
    add_pairs(PAIR, neighbours, phonon, coupling, blocks, (total0, total1), picked, 2)


def partner_energies(spread):
    odd = lax.axis_index("energy") & 1
    return jnp.where(odd == 0, spread - REACH, 0), jnp.where(odd == 0, 0, spread - REACH)


def has_partners(size):
    me = lax.axis_index("energy")
    above, below = jnp.where(me < size - 1, 1.0, 0.0), jnp.where(me > 0, 1.0, 0.0)
    odd = me & 1
    return jnp.where(odd == 0, above, below), jnp.where(odd == 0, below, above)


def finish(total, core, cross):
    to_core, to_cross = partner_energies(total.shape[0])
    for e in range(REACH):
        core[e] = total[to_core + e]
        cross[e] = total[to_cross + e]


def rate_sums(total, turned, c, a):
    sums = total[0, a] * turned[c, 0, a]
    for d in range(1, total.shape[0]):
        sums += total[d, a] * turned[c, d, a]
    return sums


def far_kernel(
    neighbours, phonon, coupling, across, before, turned, total, core, cross, partial, blocks, picked
):
    add_far(neighbours, phonon, coupling, across, before, total, blocks, picked)
    finish(total, core, cross)
    for a in range(partial.shape[0]):
        partial[a] = rate_sums(total, turned, 0, a)


def add_far(neighbours, phonon, coupling, across, before, total, blocks, picked):
    total[...] = before[...]
    put_blocks(blocks, 0, across)
    add_pairs(FAR, neighbours, phonon, coupling, blocks, (total,), picked, 4)


def last_kernel(
    scale, neighbours, phonon, coupling, across, before, turned, partial,
    total, core, cross, rate, blocks, picked,
):
    add_far(neighbours, phonon, coupling, across, before, total, blocks, picked)
    finish(total, core, cross)
    for a in range(partial.shape[0]):
        sums = partial[a] - rate_sums(total, turned, 1, a)
        rate[a : a + 1, :] = jnp.sum(sums.T, axis=0, keepdims=True) * scale


def addends(x, axis):
    size = lax.axis_size(axis)
    if size > FEW:
        return [lax.psum(x, axis)]
    turns = [[(i, (i + k) % size) for i in range(size)] for k in range(1, size)]
    return [x] + [lax.ppermute(x, axis, turn) for turn in turns]


def end_kernel(size, total0, total1, cross0, core0, cross1, core1, *rest):
    *rates, out, rate = rest
    e_local = out.shape[1]
    has_core, has_cross = has_partners(size)
    for c, (total, cross, core) in enumerate(((total0, cross0, core0), (total1, cross1, core1))):
        for e in range(e_local):
            out[c, e] = total[REACH + e] + core[e] * has_core + cross[e] * has_cross
    rate[...] = sum(r[...] for r in rates)


def per_device(green, coupling, phonon, neighbours):
    _, e_local, a_local, orb, _ = green.shape
    energies = lax.axis_size("energy")
    points = e_local * energies
    spread = (e_local + 2 * REACH, a_local, orb, orb)
    edge = (REACH, a_local, orb, orb)

    def call(kernel, out, operands, parts=1):
        return pl.pallas_call(
            kernel,
            out_shape=[jax.ShapeDtypeStruct(shape, jnp.float32) for shape in out],
            in_specs=[SMEM, SMEM] + [VMEM] * (1 + len(operands)),
            out_specs=[VMEM] * len(out),
            scratch_shapes=[
                pltpu.VMEM((parts, a_local, e_local, orb, 2 * orb), jnp.bfloat16),
                pltpu.SMEM((a_local * neighbours.shape[1] + 1,), jnp.int32),
            ],
            compiler_params=pltpu.CompilerParams(vmem_limit_bytes=24 * 2**20),
            cost_estimate=pl.CostEstimate(flops=10**6, bytes_accessed=10**4, transcendentals=0),
        )(neighbours, phonon, coupling, *operands)

    sources = (green, coupling, jnp.swapaxes(phonon, 1, 2), neighbours)
    green0, green1, green, coupling, phonon, neighbours = pl.pallas_call(
        fetch_kernel,
        out_shape=[jax.ShapeDtypeStruct(green.shape[1:], green.dtype)] * 2
        + [jax.ShapeDtypeStruct(x.shape, x.dtype) for x in sources],
        in_specs=[ANY] * 4,
        out_specs=[VMEM] * 6,
        scratch_shapes=[pltpu.SemaphoreType.DMA((6,))],
        compiler_params=pltpu.CompilerParams(vmem_limit_bytes=24 * 2**20),
    )(*(pltpu.with_memory_space_constraint(x, pltpu.HBM) for x in sources))
    ahead1 = swap(green1, "atom", 0)
    ahead0 = swap(green0, "atom", 0)
    by_core, by_cross = swap(green, "energy", 0), swap(green, "energy", 1, close=True)
    total0, total1 = call(own_kernel, [spread] * 2, (green0, green1), parts=2)
    ahead0, total0, total1 = lax.optimization_barrier((ahead0, total0, total1))
    across0 = forward(ahead0, "atom")
    green1, ahead0 = lax.optimization_barrier((green1, ahead0))
    across1 = swap(green1, "atom", 1)
    total0, total1, turned = call(
        functools.partial(pair_kernel, energies),
        [spread, spread, (2,) + spread],
        (ahead0, ahead1, total0, total1, green, by_core, by_cross),
        parts=2,
    )
    total0, core0, cross0, partial = call(
        far_kernel, [spread, edge, edge, (a_local, orb, orb)], (across0, total0, turned)
    )
    core0, cross0 = swap(core0, "energy", 0), cross_swap(cross0)
    total1, core1, cross1, rate = call(
        functools.partial(last_kernel, 1.0 / (4.0 * points)),
        [spread, edge, edge, (a_local, orb)],
        (across1, total1, turned, partial),
    )
    core1, cross1 = swap(core1, "energy", 0), cross_swap(cross1)
    cross0, core0, rate = lax.optimization_barrier((cross0, core0, rate))
    rates = addends(rate, "energy")
    return pl.pallas_call(
        functools.partial(end_kernel, energies),
        out_shape=[
            jax.ShapeDtypeStruct(green.shape, jnp.float32),
            jax.ShapeDtypeStruct((a_local, orb), jnp.float32),
        ],
        in_specs=[VMEM] * (6 + len(rates)),
        out_specs=[VMEM] * 2,
        compiler_params=pltpu.CompilerParams(vmem_limit_bytes=24 * 2**20),
        cost_estimate=pl.CostEstimate(flops=10**6, bytes_accessed=2 * 10**6, transcendentals=0),
    )(total0, total1, cross0, core0, cross1, core1, *rates)


def solution(mesh):
    return jax.shard_map(
        per_device,
        mesh=mesh,
        in_specs=(
            P(None, "energy", "atom", None, None),
            P("atom", None, None, None),
            P("atom", None, None),
            P("atom", None),
        ),
        out_specs=(P(None, "energy", "atom", None, None), P("atom", None)),
        check_vma=False,
    )
```

```python
import functools

import jax
import jax.numpy as jnp
from jax import lax
from jax.experimental import pallas as pl
from jax.experimental.pallas import tpu as pltpu
from jax.sharding import PartitionSpec as P

SHIFTS = (-2, -1, 1, 2)
REACH = max(SHIFTS)
OWN, PAIR, FAR = 0, 1, 2
FEW = 4
VMEM = pl.BlockSpec(memory_space=pltpu.VMEM)
SMEM = pl.BlockSpec(memory_space=pltpu.SMEM)
ANY = pl.BlockSpec(memory_space=pl.ANY)


def halves(x):
    high = x.astype(jnp.bfloat16)
    return high, (x - high.astype(jnp.float32)).astype(jnp.bfloat16)


def swap(x, axis, first, close=False):
    size = lax.axis_size(axis)
    pairs = [(i, i + 1) for i in range(first, size - 1, 2)]
    if close and first == 1 and size % 2 == 0:
        pairs.append((0, size - 1))
    return lax.ppermute(x, axis, pairs + [(j, i) for i, j in pairs])


def exchange(x, partner, spare):
    energies, atoms = lax.axis_size("energy"), lax.axis_size("atom")
    perm = []
    for e in range(energies):
        for a in range(atoms):
            to_e, to_a = partner(e, a)
            if not (0 <= to_e < energies and 0 <= to_a < atoms):
                to_e, to_a = spare(e, a)
            if 0 <= to_e < energies and 0 <= to_a < atoms:
                perm.append((e * atoms + a, to_e * atoms + to_a))
    return lax.ppermute(x, ("energy", "atom"), perm)


def cross_swap(x):
    step = 2 if lax.axis_size("atom") % 4 == 0 else 1
    return exchange(x, lambda e, a: (e + 1 if e % 2 else e - 1, a), lambda e, a: (e, a ^ step))


def diagonal_swap(x):
    return exchange(x, lambda e, a: (e, a + 1 if a % 2 else a - 1), lambda e, a: (e ^ 1, a))


def forward(x, axis):
    size = lax.axis_size(axis)
    ups = [(i, min(i + 2, size - 1)) for i in range(0, size, 2)]
    downs = [(i, max(i - 2, 0)) for i in range(1, size, 2)]
    return lax.ppermute(x, axis, [(i, j) for i, j in ups + downs if i != j])


def put_blocks(blocks, c, green):
    orb = green.shape[-1]
    for e in range(green.shape[0]):
        for a in range(green.shape[1]):
            high, low = halves(green[e, a])
            blocks[c, a, e, :, :orb] = high
            blocks[c, a, e, :, orb:] = low


def add_pairs(group, neighbours, phonon, coupling, blocks, totals, picked, size):
    atoms, slots, orb = coupling.shape[0], coupling.shape[1], coupling.shape[-1]
    e_local = blocks.shape[2]
    index = lax.axis_index("atom")
    base = index * atoms
    if group != OWN:
        upper = (index & 1) == (0 if group == PAIR else 1)
        base += jnp.where(upper, atoms, -atoms)

    found = jnp.int32(0)
    for a in range(atoms):
        for j in range(slots):
            picked[found] = a * slots + j
            b = neighbours[a, j] - base
            found += ((b >= 0) & (b < atoms)).astype(jnp.int32)

    def batch(step, _):
        pairs = []
        for u in range(size):
            at = step * size + u
            item = picked[jnp.minimum(at, found - 1)]
            a = item // slots
            j = item - a * slots
            high, low = halves(coupling[a, j])
            left = jnp.concatenate([high, low], 1)
            right = jnp.concatenate(
                [jnp.concatenate([high, high], 1), jnp.concatenate([low, low], 1)], 0
            )
            pairs.append((a, j, neighbours[a, j] - base, jnp.where(at < found, 1.0, 0.0), left, right))
        inners = []
        for a, j, b, live, left, right in pairs:
            for c in range(len(totals)):
                near = blocks[c, b].reshape(e_local * orb, 2 * orb)
                inner = lax.dot_general(
                    near, right, (((1,), (1,)), ((), ())), preferred_element_type=jnp.float32
                )
                inners.append(inner[:, :orb] + inner[:, orb:])
        results = []
        for a, j, b, live, left, right in pairs:
            for total in totals:
                inner = inners.pop(0)
                sums = [None] * (e_local + 2 * REACH)
                for e in range(e_local):
                    high, low = halves(inner[e * orb : (e + 1) * orb])
                    both = jnp.concatenate([high, low], 1)
                    outer = jnp.dot(
                        left, jnp.concatenate([both, both], 0), preferred_element_type=jnp.float32
                    )
                    outer = outer[:, :orb] + outer[:, orb:]
                    for k, s in enumerate(SHIFTS):
                        d = e - s + REACH
                        term = (phonon[a, k, j] * live) * outer
                        sums[d] = term if sums[d] is None else sums[d] + term
                results.append((total, a, sums))
        for total, a, sums in results:
            for d, value in enumerate(sums):
                if value is not None:
                    total[d, a] += value

    lax.fori_loop(0, (found + size - 1) // size, batch, None)


def fetch_kernel(green, coupling, phonon, neighbours, *rest):
    *results, sems = rest
    sources = [green.at[0], green.at[1], green, coupling, phonon, neighbours]
    copies = [
        pltpu.make_async_copy(source, result, sems.at[i])
        for i, (source, result) in enumerate(zip(sources, results))
    ]
    for copy in copies:
        copy.start()
    for copy in copies:
        copy.wait()


def own_kernel(neighbours, phonon, coupling, green0, green1, total0, total1, blocks, picked):
    for c, (green, total) in enumerate(((green0, total0), (green1, total1))):
        put_blocks(blocks, c, green)
        total[...] = jnp.zeros_like(total)
    add_pairs(OWN, neighbours, phonon, coupling, blocks, (total0, total1), picked, 2)


def pair_kernel(neighbours, phonon, coupling, ahead, before, total, blocks, picked):
    total[...] = before[...]
    put_blocks(blocks, 0, ahead)
    add_pairs(PAIR, neighbours, phonon, coupling, blocks, (total,), picked, 4)


def turn_kernel(
    size, neighbours, phonon, coupling, ahead, before, total0, green, by_core, by_cross,
    total, turned, partial, blocks, picked,
):
    e_local, a_local = green.shape[1], green.shape[2]
    core, cross = partner_energies(turned.shape[1])
    has_core, has_cross = has_partners(size)
    for c in range(2):
        for a in range(a_local):
            for e in range(e_local):
                turned[c, REACH + e, a] = green[c, e, a].T
            for e in range(REACH):
                turned[c, core + e, a] = by_core[c, e, a].T * has_core
                turned[c, cross + e, a] = by_cross[c, e, a].T * has_cross
    for a in range(a_local):
        partial[a] = rate_sums(total0, turned, 0, a)
    pair_kernel(neighbours, phonon, coupling, ahead, before, total, blocks, picked)


def partner_energies(spread):
    odd = lax.axis_index("energy") & 1
    return jnp.where(odd == 0, spread - REACH, 0), jnp.where(odd == 0, 0, spread - REACH)


def has_partners(size):
    me = lax.axis_index("energy")
    above, below = jnp.where(me < size - 1, 1.0, 0.0), jnp.where(me > 0, 1.0, 0.0)
    odd = me & 1
    return jnp.where(odd == 0, above, below), jnp.where(odd == 0, below, above)


def finish(total, core, cross):
    to_core, to_cross = partner_energies(total.shape[0])
    for e in range(REACH):
        core[e] = total[to_core + e]
        cross[e] = total[to_cross + e]


def rate_sums(total, turned, c, a):
    sums = total[0, a] * turned[c, 0, a]
    for d in range(1, total.shape[0]):
        sums += total[d, a] * turned[c, d, a]
    return sums


def far_kernel(neighbours, phonon, coupling, across, before, total, core, cross, blocks, picked):
    add_far(neighbours, phonon, coupling, across, before, total, blocks, picked)
    finish(total, core, cross)


def add_far(neighbours, phonon, coupling, across, before, total, blocks, picked):
    total[...] = before[...]
    put_blocks(blocks, 0, across)
    add_pairs(FAR, neighbours, phonon, coupling, blocks, (total,), picked, 4)


def last_kernel(
    scale, neighbours, phonon, coupling, across, before, turned, partial,
    total, core, cross, rate, blocks, picked,
):
    add_far(neighbours, phonon, coupling, across, before, total, blocks, picked)
    finish(total, core, cross)
    for a in range(partial.shape[0]):
        sums = partial[a] - rate_sums(total, turned, 1, a)
        rate[a : a + 1, :] = jnp.sum(sums.T, axis=0, keepdims=True) * scale


def addends(x, axis):
    size = lax.axis_size(axis)
    if size > FEW:
        return [lax.psum(x, axis)]
    turns = [[(i, (i + k) % size) for i in range(size)] for k in range(1, size)]
    return [x] + [lax.ppermute(x, axis, turn) for turn in turns]


def end_kernel(size, total0, total1, cross0, core0, cross1, core1, *rest):
    *rates, out, rate = rest
    e_local = out.shape[1]
    has_core, has_cross = has_partners(size)
    for c, (total, cross, core) in enumerate(((total0, cross0, core0), (total1, cross1, core1))):
        for e in range(e_local):
            out[c, e] = total[REACH + e] + core[e] * has_core + cross[e] * has_cross
    rate[...] = sum(r[...] for r in rates)


def per_device(green, coupling, phonon, neighbours):
    _, e_local, a_local, orb, _ = green.shape
    energies = lax.axis_size("energy")
    points = e_local * energies
    spread = (e_local + 2 * REACH, a_local, orb, orb)
    edge = (REACH, a_local, orb, orb)

    def call(kernel, out, operands, parts=1):
        return pl.pallas_call(
            kernel,
            out_shape=[jax.ShapeDtypeStruct(shape, jnp.float32) for shape in out],
            in_specs=[SMEM, SMEM] + [VMEM] * (1 + len(operands)),
            out_specs=[VMEM] * len(out),
            scratch_shapes=[
                pltpu.VMEM((parts, a_local, e_local, orb, 2 * orb), jnp.bfloat16),
                pltpu.SMEM((a_local * neighbours.shape[1] + 1,), jnp.int32),
            ],
            compiler_params=pltpu.CompilerParams(vmem_limit_bytes=24 * 2**20),
            cost_estimate=pl.CostEstimate(flops=10**6, bytes_accessed=10**4, transcendentals=0),
        )(neighbours, phonon, coupling, *operands)

    sources = (green, coupling, jnp.swapaxes(phonon, 1, 2), neighbours)
    green0, green1, green, coupling, phonon, neighbours = pl.pallas_call(
        fetch_kernel,
        out_shape=[jax.ShapeDtypeStruct(green.shape[1:], green.dtype)] * 2
        + [jax.ShapeDtypeStruct(x.shape, x.dtype) for x in sources],
        in_specs=[ANY] * 4,
        out_specs=[VMEM] * 6,
        scratch_shapes=[pltpu.SemaphoreType.DMA((6,))],
        compiler_params=pltpu.CompilerParams(vmem_limit_bytes=24 * 2**20),
    )(*(pltpu.with_memory_space_constraint(x, pltpu.HBM) for x in sources))
    ahead1 = swap(green1, "atom", 0)
    ahead0 = swap(green0, "atom", 0)
    by_core, by_cross = swap(green, "energy", 0), swap(green, "energy", 1, close=True)
    total0, total1 = call(own_kernel, [spread] * 2, (green0, green1), parts=2)
    ahead0, total0, total1 = lax.optimization_barrier((ahead0, total0, total1))
    across0 = forward(ahead0, "atom")
    (total0,) = call(pair_kernel, [spread], (ahead0, total0))
    green1, total0 = lax.optimization_barrier((green1, total0))
    across1 = diagonal_swap(green1)
    ahead1, total0 = lax.optimization_barrier((ahead1, total0))
    total0, core0, cross0 = call(far_kernel, [spread, edge, edge], (across0, total0))
    core0, cross0 = swap(core0, "energy", 0), cross_swap(cross0)
    total1, turned, partial = call(
        functools.partial(turn_kernel, energies),
        [spread, (2,) + spread, (a_local, orb, orb)],
        (ahead1, total1, total0, green, by_core, by_cross),
    )
    total1, core1, cross1, rate = call(
        functools.partial(last_kernel, 1.0 / (4.0 * points)),
        [spread, edge, edge, (a_local, orb)],
        (across1, total1, turned, partial),
    )
    core1, cross1 = swap(core1, "energy", 0), cross_swap(cross1)
    cross0, core0, rate = lax.optimization_barrier((cross0, core0, rate))
    rates = addends(rate, "energy")
    return pl.pallas_call(
        functools.partial(end_kernel, energies),
        out_shape=[
            jax.ShapeDtypeStruct(green.shape, jnp.float32),
            jax.ShapeDtypeStruct((a_local, orb), jnp.float32),
        ],
        in_specs=[VMEM] * (6 + len(rates)),
        out_specs=[VMEM] * 2,
        compiler_params=pltpu.CompilerParams(vmem_limit_bytes=24 * 2**20),
        cost_estimate=pl.CostEstimate(flops=10**6, bytes_accessed=2 * 10**6, transcendentals=0),
    )(total0, total1, cross0, core0, cross1, core1, *rates)


def solution(mesh):
    return jax.shard_map(
        per_device,
        mesh=mesh,
        in_specs=(
            P(None, "energy", "atom", None, None),
            P("atom", None, None, None),
            P("atom", None, None),
            P("atom", None),
        ),
        out_specs=(P(None, "energy", "atom", None, None), P("atom", None)),
        check_vma=False,
    )
```

```python
import functools

import jax
import jax.numpy as jnp
from jax import lax
from jax.experimental import pallas as pl
from jax.experimental.pallas import tpu as pltpu
from jax.sharding import PartitionSpec as P

SHIFTS = (-2, -1, 1, 2)
REACH = max(SHIFTS)
OWN, PAIR, FAR = 0, 1, 2
FEW = 4
VMEM = pl.BlockSpec(memory_space=pltpu.VMEM)
SMEM = pl.BlockSpec(memory_space=pltpu.SMEM)
ANY = pl.BlockSpec(memory_space=pl.ANY)


def halves(x):
    high = x.astype(jnp.bfloat16)
    return high, (x - high.astype(jnp.float32)).astype(jnp.bfloat16)


def swap(x, axis, first, close=False):
    size = lax.axis_size(axis)
    pairs = [(i, i + 1) for i in range(first, size - 1, 2)]
    if close and first == 1 and size % 2 == 0:
        pairs.append((0, size - 1))
    return lax.ppermute(x, axis, pairs + [(j, i) for i, j in pairs])


def exchange(x, partner, spare):
    energies, atoms = lax.axis_size("energy"), lax.axis_size("atom")
    perm = []
    for e in range(energies):
        for a in range(atoms):
            to_e, to_a = partner(e, a)
            if not (0 <= to_e < energies and 0 <= to_a < atoms):
                to_e, to_a = spare(e, a)
            if 0 <= to_e < energies and 0 <= to_a < atoms:
                perm.append((e * atoms + a, to_e * atoms + to_a))
    return lax.ppermute(x, ("energy", "atom"), perm)


def cross_swap(x):
    step = 2 if lax.axis_size("atom") % 4 == 0 else 1
    return exchange(x, lambda e, a: (e + 1 if e % 2 else e - 1, a), lambda e, a: (e, a ^ step))


def forward(x, axis):
    size = lax.axis_size(axis)
    ups = [(i, min(i + 2, size - 1)) for i in range(0, size, 2)]
    downs = [(i, max(i - 2, 0)) for i in range(1, size, 2)]
    return lax.ppermute(x, axis, [(i, j) for i, j in ups + downs if i != j])


def put_blocks(blocks, c, green):
    orb = green.shape[-1]
    for e in range(green.shape[0]):
        for a in range(green.shape[1]):
            high, low = halves(green[e, a])
            blocks[c, a, e, :, :orb] = high
            blocks[c, a, e, :, orb:] = low


def add_pairs(group, neighbours, phonon, coupling, blocks, totals, picked, size):
    atoms, slots, orb = coupling.shape[0], coupling.shape[1], coupling.shape[-1]
    e_local = blocks.shape[2]
    index = lax.axis_index("atom")
    base = index * atoms
    if group != OWN:
        upper = (index & 1) == (0 if group == PAIR else 1)
        base += jnp.where(upper, atoms, -atoms)

    found = jnp.int32(0)
    for a in range(atoms):
        for j in range(slots):
            picked[found] = a * slots + j
            b = neighbours[a, j] - base
            found += ((b >= 0) & (b < atoms)).astype(jnp.int32)

    def batch(step, _):
        pairs = []
        for u in range(size):
            at = step * size + u
            item = picked[jnp.minimum(at, found - 1)]
            a = item // slots
            j = item - a * slots
            high, low = halves(coupling[a, j])
            left = jnp.concatenate([high, low], 1)
            right = jnp.concatenate(
                [jnp.concatenate([high, high], 1), jnp.concatenate([low, low], 1)], 0
            )
            pairs.append((a, j, neighbours[a, j] - base, jnp.where(at < found, 1.0, 0.0), left, right))
        inners = []
        for a, j, b, live, left, right in pairs:
            for c in range(len(totals)):
                near = blocks[c, b].reshape(e_local * orb, 2 * orb)
                inner = lax.dot_general(
                    near, right, (((1,), (1,)), ((), ())), preferred_element_type=jnp.float32
                )
                inners.append(inner[:, :orb] + inner[:, orb:])
        results = []
        for a, j, b, live, left, right in pairs:
            for total in totals:
                inner = inners.pop(0)
                sums = [None] * (e_local + 2 * REACH)
                for e in range(e_local):
                    high, low = halves(inner[e * orb : (e + 1) * orb])
                    both = jnp.concatenate([high, low], 1)
                    outer = jnp.dot(
                        left, jnp.concatenate([both, both], 0), preferred_element_type=jnp.float32
                    )
                    outer = outer[:, :orb] + outer[:, orb:]
                    for k, s in enumerate(SHIFTS):
                        d = e - s + REACH
                        term = (phonon[a, k, j] * live) * outer
                        sums[d] = term if sums[d] is None else sums[d] + term
                results.append((total, a, sums))
        for total, a, sums in results:
            for d, value in enumerate(sums):
                if value is not None:
                    total[d, a] += value

    lax.fori_loop(0, (found + size - 1) // size, batch, None)


def fetch_kernel(green, coupling, phonon, neighbours, *rest):
    *results, sems = rest
    sources = [green.at[0], green.at[1], green, coupling, phonon, neighbours]
    copies = [
        pltpu.make_async_copy(source, result, sems.at[i])
        for i, (source, result) in enumerate(zip(sources, results))
    ]
    for copy in copies:
        copy.start()
    for copy in copies:
        copy.wait()


def own_kernel(neighbours, phonon, coupling, green0, green1, total0, total1, blocks, picked):
    for c, (green, total) in enumerate(((green0, total0), (green1, total1))):
        put_blocks(blocks, c, green)
        total[...] = jnp.zeros_like(total)
    add_pairs(OWN, neighbours, phonon, coupling, blocks, (total0, total1), picked, 2)


def pair_kernel(neighbours, phonon, coupling, ahead, before, total, blocks, picked):
    total[...] = before[...]
    put_blocks(blocks, 0, ahead)
    add_pairs(PAIR, neighbours, phonon, coupling, blocks, (total,), picked, 4)


def turn_kernel(
    size, neighbours, phonon, coupling, ahead, before, total0, green, by_core, by_cross,
    total, turned, partial, blocks, picked,
):
    e_local, a_local = green.shape[1], green.shape[2]
    core, cross = partner_energies(turned.shape[1])
    has_core, has_cross = has_partners(size)
    for c in range(2):
        for a in range(a_local):
            for e in range(e_local):
                turned[c, REACH + e, a] = green[c, e, a].T
            for e in range(REACH):
                turned[c, core + e, a] = by_core[c, e, a].T * has_core
                turned[c, cross + e, a] = by_cross[c, e, a].T * has_cross
    for a in range(a_local):
        partial[a] = rate_sums(total0, turned, 0, a)
    pair_kernel(neighbours, phonon, coupling, ahead, before, total, blocks, picked)


def partner_energies(spread):
    odd = lax.axis_index("energy") & 1
    return jnp.where(odd == 0, spread - REACH, 0), jnp.where(odd == 0, 0, spread - REACH)


def has_partners(size):
    me = lax.axis_index("energy")
    above, below = jnp.where(me < size - 1, 1.0, 0.0), jnp.where(me > 0, 1.0, 0.0)
    odd = me & 1
    return jnp.where(odd == 0, above, below), jnp.where(odd == 0, below, above)


def finish(total, core, cross):
    to_core, to_cross = partner_energies(total.shape[0])
    for e in range(REACH):
        core[e] = total[to_core + e]
        cross[e] = total[to_cross + e]


def rate_sums(total, turned, c, a):
    sums = total[0, a] * turned[c, 0, a]
    for d in range(1, total.shape[0]):
        sums += total[d, a] * turned[c, d, a]
    return sums


def far_kernel(neighbours, phonon, coupling, across, before, total, core, cross, blocks, picked):
    add_far(neighbours, phonon, coupling, across, before, total, blocks, picked)
    finish(total, core, cross)


def add_far(neighbours, phonon, coupling, across, before, total, blocks, picked):
    total[...] = before[...]
    put_blocks(blocks, 0, across)
    add_pairs(FAR, neighbours, phonon, coupling, blocks, (total,), picked, 4)


def last_kernel(
    scale, neighbours, phonon, coupling, across, before, turned, partial,
    total, core, cross, rate, blocks, picked,
):
    add_far(neighbours, phonon, coupling, across, before, total, blocks, picked)
    finish(total, core, cross)
    for a in range(partial.shape[0]):
        sums = partial[a] - rate_sums(total, turned, 1, a)
        rate[a : a + 1, :] = jnp.sum(sums.T, axis=0, keepdims=True) * scale


def addends(x, axis):
    size = lax.axis_size(axis)
    if size > FEW:
        return [lax.psum(x, axis)]
    turns = [[(i, (i + k) % size) for i in range(size)] for k in range(1, size)]
    return [x] + [lax.ppermute(x, axis, turn) for turn in turns]


def end_kernel(size, total0, total1, cross0, core0, cross1, core1, *rest):
    *rates, out, rate = rest
    e_local = out.shape[1]
    has_core, has_cross = has_partners(size)
    for c, (total, cross, core) in enumerate(((total0, cross0, core0), (total1, cross1, core1))):
        for e in range(e_local):
            out[c, e] = total[REACH + e] + core[e] * has_core + cross[e] * has_cross
    rate[...] = sum(r[...] for r in rates)


def per_device(green, coupling, phonon, neighbours):
    _, e_local, a_local, orb, _ = green.shape
    energies = lax.axis_size("energy")
    points = e_local * energies
    spread = (e_local + 2 * REACH, a_local, orb, orb)
    edge = (REACH, a_local, orb, orb)

    def call(kernel, out, operands, parts=1):
        return pl.pallas_call(
            kernel,
            out_shape=[jax.ShapeDtypeStruct(shape, jnp.float32) for shape in out],
            in_specs=[SMEM, SMEM] + [VMEM] * (1 + len(operands)),
            out_specs=[VMEM] * len(out),
            scratch_shapes=[
                pltpu.VMEM((parts, a_local, e_local, orb, 2 * orb), jnp.bfloat16),
                pltpu.SMEM((a_local * neighbours.shape[1] + 1,), jnp.int32),
            ],
            compiler_params=pltpu.CompilerParams(vmem_limit_bytes=24 * 2**20),
            cost_estimate=pl.CostEstimate(flops=10**6, bytes_accessed=10**4, transcendentals=0),
        )(neighbours, phonon, coupling, *operands)

    sources = (green, coupling, jnp.swapaxes(phonon, 1, 2), neighbours)
    green0, green1, green, coupling, phonon, neighbours = pl.pallas_call(
        fetch_kernel,
        out_shape=[jax.ShapeDtypeStruct(green.shape[1:], green.dtype)] * 2
        + [jax.ShapeDtypeStruct(x.shape, x.dtype) for x in sources],
        in_specs=[ANY] * 4,
        out_specs=[VMEM] * 6,
        scratch_shapes=[pltpu.SemaphoreType.DMA((6,))],
        compiler_params=pltpu.CompilerParams(vmem_limit_bytes=24 * 2**20),
    )(*(pltpu.with_memory_space_constraint(x, pltpu.HBM) for x in sources))
    ahead1 = swap(green1, "atom", 0)
    ahead0 = swap(green0, "atom", 0)
    by_core, by_cross = swap(green, "energy", 0), swap(green, "energy", 1, close=True)
    total0, total1 = call(own_kernel, [spread] * 2, (green0, green1), parts=2)
    ahead0, total0, total1 = lax.optimization_barrier((ahead0, total0, total1))
    across0 = forward(ahead0, "atom")
    green1, ahead0 = lax.optimization_barrier((green1, ahead0))
    across1 = swap(green1, "atom", 1)
    (total0,) = call(pair_kernel, [spread], (ahead0, total0))
    ahead1, total0 = lax.optimization_barrier((ahead1, total0))
    total0, core0, cross0 = call(far_kernel, [spread, edge, edge], (across0, total0))
    core0, cross0 = swap(core0, "energy", 0), cross_swap(cross0)
    total1, turned, partial = call(
        functools.partial(turn_kernel, energies),
        [spread, (2,) + spread, (a_local, orb, orb)],
        (ahead1, total1, total0, green, by_core, by_cross),
    )
    total1, core1, cross1, rate = call(
        functools.partial(last_kernel, 1.0 / (4.0 * points)),
        [spread, edge, edge, (a_local, orb)],
        (across1, total1, turned, partial),
    )
    core1, cross1 = swap(core1, "energy", 0), cross_swap(cross1)
    cross0, core0, rate = lax.optimization_barrier((cross0, core0, rate))
    rates = addends(rate, "energy")
    return pl.pallas_call(
        functools.partial(end_kernel, energies),
        out_shape=[
            jax.ShapeDtypeStruct(green.shape, jnp.float32),
            jax.ShapeDtypeStruct((a_local, orb), jnp.float32),
        ],
        in_specs=[VMEM] * (6 + len(rates)),
        out_specs=[VMEM] * 2,
        compiler_params=pltpu.CompilerParams(vmem_limit_bytes=24 * 2**20),
        cost_estimate=pl.CostEstimate(flops=10**6, bytes_accessed=2 * 10**6, transcendentals=0),
    )(total0, total1, cross0, core0, cross1, core1, *rates)


def solution(mesh):
    return jax.shard_map(
        per_device,
        mesh=mesh,
        in_specs=(
            P(None, "energy", "atom", None, None),
            P("atom", None, None, None),
            P("atom", None, None),
            P("atom", None),
        ),
        out_specs=(P(None, "energy", "atom", None, None), P("atom", None)),
        check_vma=False,
    )
```

```python
import functools

import jax
import jax.numpy as jnp
from jax import lax
from jax.experimental import pallas as pl
from jax.experimental.pallas import tpu as pltpu
from jax.sharding import PartitionSpec as P

SHIFTS = (-2, -1, 1, 2)
REACH = max(SHIFTS)
OWN, PAIR, FAR = 0, 1, 2
FEW = 4
VMEM = pl.BlockSpec(memory_space=pltpu.VMEM)
SMEM = pl.BlockSpec(memory_space=pltpu.SMEM)
ANY = pl.BlockSpec(memory_space=pl.ANY)


def halves(x):
    high = x.astype(jnp.bfloat16)
    return high, (x - high.astype(jnp.float32)).astype(jnp.bfloat16)


def swap(x, axis, first, close=False):
    size = lax.axis_size(axis)
    pairs = [(i, i + 1) for i in range(first, size - 1, 2)]
    if close and first == 1 and size % 2 == 0:
        pairs.append((0, size - 1))
    return lax.ppermute(x, axis, pairs + [(j, i) for i, j in pairs])


def exchange(x, partner, spare):
    energies, atoms = lax.axis_size("energy"), lax.axis_size("atom")
    perm = []
    for e in range(energies):
        for a in range(atoms):
            to_e, to_a = partner(e, a)
            if not (0 <= to_e < energies and 0 <= to_a < atoms):
                to_e, to_a = spare(e, a)
            if 0 <= to_e < energies and 0 <= to_a < atoms:
                perm.append((e * atoms + a, to_e * atoms + to_a))
    return lax.ppermute(x, ("energy", "atom"), perm)


def cross_swap(x):
    step = 2 if lax.axis_size("atom") % 4 == 0 else 1
    return exchange(x, lambda e, a: (e + 1 if e % 2 else e - 1, a), lambda e, a: (e, a ^ step))


def forward(x, axis):
    size = lax.axis_size(axis)
    ups = [(i, min(i + 2, size - 1)) for i in range(0, size, 2)]
    downs = [(i, max(i - 2, 0)) for i in range(1, size, 2)]
    return lax.ppermute(x, axis, [(i, j) for i, j in ups + downs if i != j])


def put_blocks(blocks, c, green):
    orb = green.shape[-1]
    for e in range(green.shape[0]):
        for a in range(green.shape[1]):
            high, low = halves(green[e, a])
            blocks[c, a, e, :, :orb] = high
            blocks[c, a, e, :, orb:] = low


def add_pairs(group, neighbours, phonon, coupling, blocks, totals, picked, size):
    atoms, slots, orb = coupling.shape[0], coupling.shape[1], coupling.shape[-1]
    e_local = blocks.shape[2]
    index = lax.axis_index("atom")
    base = index * atoms
    if group != OWN:
        upper = (index & 1) == (0 if group == PAIR else 1)
        base += jnp.where(upper, atoms, -atoms)

    found = jnp.int32(0)
    for a in range(atoms):
        for j in range(slots):
            picked[found] = a * slots + j
            b = neighbours[a, j] - base
            found += ((b >= 0) & (b < atoms)).astype(jnp.int32)

    def batch(step, _):
        pairs = []
        for u in range(size):
            at = step * size + u
            item = picked[jnp.minimum(at, found - 1)]
            a = item // slots
            j = item - a * slots
            high, low = halves(coupling[a, j])
            left = jnp.concatenate([high, low], 1)
            right = jnp.concatenate(
                [jnp.concatenate([high, high], 1), jnp.concatenate([low, low], 1)], 0
            )
            pairs.append((a, j, neighbours[a, j] - base, jnp.where(at < found, 1.0, 0.0), left, right))
        inners = []
        for a, j, b, live, left, right in pairs:
            for c in range(len(totals)):
                near = blocks[c, b].reshape(e_local * orb, 2 * orb)
                inner = lax.dot_general(
                    near, right, (((1,), (1,)), ((), ())), preferred_element_type=jnp.float32
                )
                inners.append(inner[:, :orb] + inner[:, orb:])
        results = []
        for a, j, b, live, left, right in pairs:
            for total in totals:
                inner = inners.pop(0)
                sums = [None] * (e_local + 2 * REACH)
                for e in range(e_local):
                    high, low = halves(inner[e * orb : (e + 1) * orb])
                    both = jnp.concatenate([high, low], 1)
                    outer = jnp.dot(
                        left, jnp.concatenate([both, both], 0), preferred_element_type=jnp.float32
                    )
                    outer = outer[:, :orb] + outer[:, orb:]
                    for k, s in enumerate(SHIFTS):
                        d = e - s + REACH
                        term = (phonon[a, k, j] * live) * outer
                        sums[d] = term if sums[d] is None else sums[d] + term
                results.append((total, a, sums))
        for total, a, sums in results:
            for d, value in enumerate(sums):
                if value is not None:
                    total[d, a] += value

    lax.fori_loop(0, (found + size - 1) // size, batch, None)


def fetch_kernel(green, coupling, phonon, neighbours, *rest):
    *results, sems = rest
    sources = [green.at[0], green.at[1], green, coupling, phonon, neighbours]
    copies = [
        pltpu.make_async_copy(source, result, sems.at[i])
        for i, (source, result) in enumerate(zip(sources, results))
    ]
    for copy in copies:
        copy.start()
    for copy in copies:
        copy.wait()


def own_kernel(neighbours, phonon, coupling, green0, green1, total0, total1, blocks, picked):
    for c, (green, total) in enumerate(((green0, total0), (green1, total1))):
        put_blocks(blocks, c, green)
        total[...] = jnp.zeros_like(total)
    add_pairs(OWN, neighbours, phonon, coupling, blocks, (total0, total1), picked, 2)


def pair_kernel(neighbours, phonon, coupling, ahead, before, total, blocks, picked):
    total[...] = before[...]
    put_blocks(blocks, 0, ahead)
    add_pairs(PAIR, neighbours, phonon, coupling, blocks, (total,), picked, 4)


def turn_kernel(
    size, neighbours, phonon, coupling, ahead, before, green, by_core, by_cross,
    total, turned, blocks, picked,
):
    e_local, a_local = green.shape[1], green.shape[2]
    core, cross = partner_energies(turned.shape[1])
    has_core, has_cross = has_partners(size)
    for c in range(2):
        for a in range(a_local):
            for e in range(e_local):
                turned[c, REACH + e, a] = green[c, e, a].T
            for e in range(REACH):
                turned[c, core + e, a] = by_core[c, e, a].T * has_core
                turned[c, cross + e, a] = by_cross[c, e, a].T * has_cross
    pair_kernel(neighbours, phonon, coupling, ahead, before, total, blocks, picked)


def partner_energies(spread):
    odd = lax.axis_index("energy") & 1
    return jnp.where(odd == 0, spread - REACH, 0), jnp.where(odd == 0, 0, spread - REACH)


def has_partners(size):
    me = lax.axis_index("energy")
    above, below = jnp.where(me < size - 1, 1.0, 0.0), jnp.where(me > 0, 1.0, 0.0)
    odd = me & 1
    return jnp.where(odd == 0, above, below), jnp.where(odd == 0, below, above)


def finish(total, core, cross):
    to_core, to_cross = partner_energies(total.shape[0])
    for e in range(REACH):
        core[e] = total[to_core + e]
        cross[e] = total[to_cross + e]


def rate_sums(total, turned, c, a):
    sums = total[0, a] * turned[c, 0, a]
    for d in range(1, total.shape[0]):
        sums += total[d, a] * turned[c, d, a]
    return sums


def far_kernel(
    neighbours, phonon, coupling, across, before, turned, total, core, cross, partial, blocks, picked
):
    add_far(neighbours, phonon, coupling, across, before, total, blocks, picked)
    finish(total, core, cross)
    for a in range(partial.shape[0]):
        partial[a] = rate_sums(total, turned, 0, a)


def add_far(neighbours, phonon, coupling, across, before, total, blocks, picked):
    total[...] = before[...]
    put_blocks(blocks, 0, across)
    add_pairs(FAR, neighbours, phonon, coupling, blocks, (total,), picked, 4)


def last_kernel(
    scale, neighbours, phonon, coupling, across, before, turned, partial,
    total, core, cross, rate, blocks, picked,
):
    add_far(neighbours, phonon, coupling, across, before, total, blocks, picked)
    finish(total, core, cross)
    for a in range(partial.shape[0]):
        sums = partial[a] - rate_sums(total, turned, 1, a)
        rate[a : a + 1, :] = jnp.sum(sums.T, axis=0, keepdims=True) * scale


def addends(x, axis):
    size = lax.axis_size(axis)
    if size > FEW:
        return [lax.psum(x, axis)]
    turns = [[(i, (i + k) % size) for i in range(size)] for k in range(1, size)]
    return [x] + [lax.ppermute(x, axis, turn) for turn in turns]


def end_kernel(size, total0, total1, cross0, core0, cross1, core1, *rest):
    *rates, out, rate = rest
    e_local = out.shape[1]
    has_core, has_cross = has_partners(size)
    for c, (total, cross, core) in enumerate(((total0, cross0, core0), (total1, cross1, core1))):
        for e in range(e_local):
            out[c, e] = total[REACH + e] + core[e] * has_core + cross[e] * has_cross
    rate[...] = sum(r[...] for r in rates)


def per_device(green, coupling, phonon, neighbours):
    _, e_local, a_local, orb, _ = green.shape
    energies = lax.axis_size("energy")
    points = e_local * energies
    spread = (e_local + 2 * REACH, a_local, orb, orb)
    edge = (REACH, a_local, orb, orb)

    def call(kernel, out, operands, parts=1):
        return pl.pallas_call(
            kernel,
            out_shape=[jax.ShapeDtypeStruct(shape, jnp.float32) for shape in out],
            in_specs=[SMEM, SMEM] + [VMEM] * (1 + len(operands)),
            out_specs=[VMEM] * len(out),
            scratch_shapes=[
                pltpu.VMEM((parts, a_local, e_local, orb, 2 * orb), jnp.bfloat16),
                pltpu.SMEM((a_local * neighbours.shape[1] + 1,), jnp.int32),
            ],
            compiler_params=pltpu.CompilerParams(vmem_limit_bytes=24 * 2**20),
            cost_estimate=pl.CostEstimate(flops=10**6, bytes_accessed=10**4, transcendentals=0),
        )(neighbours, phonon, coupling, *operands)

    sources = (green, coupling, jnp.swapaxes(phonon, 1, 2), neighbours)
    green0, green1, green, coupling, phonon, neighbours = pl.pallas_call(
        fetch_kernel,
        out_shape=[jax.ShapeDtypeStruct(green.shape[1:], green.dtype)] * 2
        + [jax.ShapeDtypeStruct(x.shape, x.dtype) for x in sources],
        in_specs=[ANY] * 4,
        out_specs=[VMEM] * 6,
        scratch_shapes=[pltpu.SemaphoreType.DMA((6,))],
        compiler_params=pltpu.CompilerParams(vmem_limit_bytes=24 * 2**20),
    )(*(pltpu.with_memory_space_constraint(x, pltpu.HBM) for x in sources))
    ahead1 = swap(green1, "atom", 0)
    ahead0 = swap(green0, "atom", 0)
    by_core, by_cross = swap(green, "energy", 0), swap(green, "energy", 1, close=True)
    total0, total1 = call(own_kernel, [spread] * 2, (green0, green1), parts=2)
    ahead0, total0, total1 = lax.optimization_barrier((ahead0, total0, total1))
    across0 = forward(ahead0, "atom")
    (total0,) = call(pair_kernel, [spread], (ahead0, total0))
    green1, total0 = lax.optimization_barrier((green1, total0))
    across1 = swap(green1, "atom", 1)
    total1, turned = call(
        functools.partial(turn_kernel, energies),
        [spread, (2,) + spread],
        (ahead1, total1, green, by_core, by_cross),
    )
    total0, core0, cross0, partial = call(
        far_kernel, [spread, edge, edge, (a_local, orb, orb)], (across0, total0, turned)
    )
    core0, cross0 = swap(core0, "energy", 0), cross_swap(cross0)
    total1, core1, cross1, rate = call(
        functools.partial(last_kernel, 1.0 / (4.0 * points)),
        [spread, edge, edge, (a_local, orb)],
        (across1, total1, turned, partial),
    )
    core1, cross1 = swap(core1, "energy", 0), cross_swap(cross1)
    cross0, core0, rate = lax.optimization_barrier((cross0, core0, rate))
    rates = addends(rate, "energy")
    return pl.pallas_call(
        functools.partial(end_kernel, energies),
        out_shape=[
            jax.ShapeDtypeStruct(green.shape, jnp.float32),
            jax.ShapeDtypeStruct((a_local, orb), jnp.float32),
        ],
        in_specs=[VMEM] * (6 + len(rates)),
        out_specs=[VMEM] * 2,
        compiler_params=pltpu.CompilerParams(vmem_limit_bytes=24 * 2**20),
        cost_estimate=pl.CostEstimate(flops=10**6, bytes_accessed=2 * 10**6, transcendentals=0),
    )(total0, total1, cross0, core0, cross1, core1, *rates)


def solution(mesh):
    return jax.shard_map(
        per_device,
        mesh=mesh,
        in_specs=(
            P(None, "energy", "atom", None, None),
            P("atom", None, None, None),
            P("atom", None, None),
            P("atom", None),
        ),
        out_specs=(P(None, "energy", "atom", None, None), P("atom", None)),
        check_vma=False,
    )
```

```python
import functools

import jax
import jax.numpy as jnp
from jax import lax
from jax.experimental import pallas as pl
from jax.experimental.pallas import tpu as pltpu
from jax.sharding import PartitionSpec as P

SHIFTS = (-2, -1, 1, 2)
REACH = max(SHIFTS)
OWN, PAIR, FAR = 0, 1, 2
FEW = 4
VMEM = pl.BlockSpec(memory_space=pltpu.VMEM)
SMEM = pl.BlockSpec(memory_space=pltpu.SMEM)
ANY = pl.BlockSpec(memory_space=pl.ANY)


def halves(x):
    high = x.astype(jnp.bfloat16)
    return high, (x - high.astype(jnp.float32)).astype(jnp.bfloat16)


def swap(x, axis, first):
    low = range(first, lax.axis_size(axis) - 1, 2)
    return lax.ppermute(x, axis, [(i, i + 1) for i in low] + [(i + 1, i) for i in low])


def exchange(x, partner, spare):
    energies, atoms = lax.axis_size("energy"), lax.axis_size("atom")
    perm = []
    for e in range(energies):
        for a in range(atoms):
            to_e, to_a = partner(e, a)
            if not (0 <= to_e < energies and 0 <= to_a < atoms):
                to_e, to_a = spare(e, a)
            if 0 <= to_e < energies and 0 <= to_a < atoms:
                perm.append((e * atoms + a, to_e * atoms + to_a))
    return lax.ppermute(x, ("energy", "atom"), perm)


def cross_swap(x, step):
    return exchange(x, lambda e, a: (e + 1 if e % 2 else e - 1, a), lambda e, a: (e, a ^ step))


def forward(x, axis):
    size = lax.axis_size(axis)
    ups = [(i, min(i + 2, size - 1)) for i in range(0, size, 2)]
    downs = [(i, max(i - 2, 0)) for i in range(1, size, 2)]
    return lax.ppermute(x, axis, [(i, j) for i, j in ups + downs if i != j])


def put_blocks(blocks, c, green):
    orb = green.shape[-1]
    for e in range(green.shape[0]):
        for a in range(green.shape[1]):
            high, low = halves(green[e, a])
            blocks[c, a, e, :, :orb] = high
            blocks[c, a, e, :, orb:] = low


def add_pairs(group, neighbours, phonon, coupling, blocks, totals, picked, size):
    atoms, slots, orb = coupling.shape[0], coupling.shape[1], coupling.shape[-1]
    e_local = blocks.shape[2]
    index = lax.axis_index("atom")
    base = index * atoms
    if group != OWN:
        upper = (index & 1) == (0 if group == PAIR else 1)
        base += jnp.where(upper, atoms, -atoms)

    found = jnp.int32(0)
    for a in range(atoms):
        for j in range(slots):
            picked[found] = a * slots + j
            b = neighbours[a, j] - base
            found += ((b >= 0) & (b < atoms)).astype(jnp.int32)

    def batch(step, _):
        pairs = []
        for u in range(size):
            at = step * size + u
            item = picked[jnp.minimum(at, found - 1)]
            a = item // slots
            j = item - a * slots
            high, low = halves(coupling[a, j])
            left = jnp.concatenate([high, low], 1)
            right = jnp.concatenate(
                [jnp.concatenate([high, high], 1), jnp.concatenate([low, low], 1)], 0
            )
            pairs.append((a, j, neighbours[a, j] - base, jnp.where(at < found, 1.0, 0.0), left, right))
        inners = []
        for a, j, b, live, left, right in pairs:
            for c in range(len(totals)):
                near = blocks[c, b].reshape(e_local * orb, 2 * orb)
                inner = lax.dot_general(
                    near, right, (((1,), (1,)), ((), ())), preferred_element_type=jnp.float32
                )
                inners.append(inner[:, :orb] + inner[:, orb:])
        results = []
        for a, j, b, live, left, right in pairs:
            for total in totals:
                inner = inners.pop(0)
                sums = [None] * (e_local + 2 * REACH)
                for e in range(e_local):
                    high, low = halves(inner[e * orb : (e + 1) * orb])
                    both = jnp.concatenate([high, low], 1)
                    outer = jnp.dot(
                        left, jnp.concatenate([both, both], 0), preferred_element_type=jnp.float32
                    )
                    outer = outer[:, :orb] + outer[:, orb:]
                    for k, s in enumerate(SHIFTS):
                        d = e - s + REACH
                        term = (phonon[a, k, j] * live) * outer
                        sums[d] = term if sums[d] is None else sums[d] + term
                results.append((total, a, sums))
        for total, a, sums in results:
            for d, value in enumerate(sums):
                if value is not None:
                    total[d, a] += value

    lax.fori_loop(0, (found + size - 1) // size, batch, None)


def fetch_kernel(green, coupling, phonon, neighbours, *rest):
    *results, sems = rest
    sources = [green.at[0], green.at[1], green, coupling, phonon, neighbours]
    copies = [
        pltpu.make_async_copy(source, result, sems.at[i])
        for i, (source, result) in enumerate(zip(sources, results))
    ]
    for copy in copies:
        copy.start()
    for copy in copies:
        copy.wait()


def own_kernel(neighbours, phonon, coupling, green0, green1, total0, total1, blocks, picked):
    for c, (green, total) in enumerate(((green0, total0), (green1, total1))):
        put_blocks(blocks, c, green)
        total[...] = jnp.zeros_like(total)
    add_pairs(OWN, neighbours, phonon, coupling, blocks, (total0, total1), picked, 2)


def pair_kernel(neighbours, phonon, coupling, ahead, before, total, blocks, picked):
    total[...] = before[...]
    put_blocks(blocks, 0, ahead)
    add_pairs(PAIR, neighbours, phonon, coupling, blocks, (total,), picked, 4)


def turn_kernel(
    size, neighbours, phonon, coupling, ahead, before, green, by_core, by_cross,
    total, turned, blocks, picked,
):
    e_local, a_local = green.shape[1], green.shape[2]
    core, cross = partner_energies(turned.shape[1])
    has_core, has_cross = has_partners(size)
    for c in range(2):
        for a in range(a_local):
            for e in range(e_local):
                turned[c, REACH + e, a] = green[c, e, a].T
            for e in range(REACH):
                turned[c, core + e, a] = by_core[c, e, a].T * has_core
                turned[c, cross + e, a] = by_cross[c, e, a].T * has_cross
    pair_kernel(neighbours, phonon, coupling, ahead, before, total, blocks, picked)


def partner_energies(spread):
    odd = lax.axis_index("energy") & 1
    return jnp.where(odd == 0, spread - REACH, 0), jnp.where(odd == 0, 0, spread - REACH)


def has_partners(size):
    me = lax.axis_index("energy")
    above, below = jnp.where(me < size - 1, 1.0, 0.0), jnp.where(me > 0, 1.0, 0.0)
    odd = me & 1
    return jnp.where(odd == 0, above, below), jnp.where(odd == 0, below, above)


def finish(total, core, cross):
    to_core, to_cross = partner_energies(total.shape[0])
    for e in range(REACH):
        core[e] = total[to_core + e]
        cross[e] = total[to_cross + e]


def rate_sums(total, turned, c, a):
    sums = total[0, a] * turned[c, 0, a]
    for d in range(1, total.shape[0]):
        sums += total[d, a] * turned[c, d, a]
    return sums


def far_kernel(
    neighbours, phonon, coupling, across, before, turned, total, core, cross, partial, blocks, picked
):
    add_far(neighbours, phonon, coupling, across, before, total, blocks, picked)
    finish(total, core, cross)
    for a in range(partial.shape[0]):
        partial[a] = rate_sums(total, turned, 0, a)


def add_far(neighbours, phonon, coupling, across, before, total, blocks, picked):
    total[...] = before[...]
    put_blocks(blocks, 0, across)
    add_pairs(FAR, neighbours, phonon, coupling, blocks, (total,), picked, 4)


def last_kernel(
    scale, neighbours, phonon, coupling, across, before, turned, partial,
    total, core, cross, rate, blocks, picked,
):
    add_far(neighbours, phonon, coupling, across, before, total, blocks, picked)
    finish(total, core, cross)
    for a in range(partial.shape[0]):
        sums = partial[a] - rate_sums(total, turned, 1, a)
        rate[a : a + 1, :] = jnp.sum(sums.T, axis=0, keepdims=True) * scale


def addends(x, axis):
    size = lax.axis_size(axis)
    if size > FEW:
        return [lax.psum(x, axis)]
    turns = [[(i, (i + k) % size) for i in range(size)] for k in range(1, size)]
    return [x] + [lax.ppermute(x, axis, turn) for turn in turns]


def end_kernel(size, total0, total1, cross0, core0, cross1, core1, *rest):
    *rates, out, rate = rest
    e_local = out.shape[1]
    has_core, has_cross = has_partners(size)
    for c, (total, cross, core) in enumerate(((total0, cross0, core0), (total1, cross1, core1))):
        for e in range(e_local):
            out[c, e] = total[REACH + e] + core[e] * has_core + cross[e] * has_cross
    rate[...] = sum(r[...] for r in rates)


def per_device(green, coupling, phonon, neighbours):
    _, e_local, a_local, orb, _ = green.shape
    energies = lax.axis_size("energy")
    points = e_local * energies
    spread = (e_local + 2 * REACH, a_local, orb, orb)
    edge = (REACH, a_local, orb, orb)

    def call(kernel, out, operands, parts=1):
        return pl.pallas_call(
            kernel,
            out_shape=[jax.ShapeDtypeStruct(shape, jnp.float32) for shape in out],
            in_specs=[SMEM, SMEM] + [VMEM] * (1 + len(operands)),
            out_specs=[VMEM] * len(out),
            scratch_shapes=[
                pltpu.VMEM((parts, a_local, e_local, orb, 2 * orb), jnp.bfloat16),
                pltpu.SMEM((a_local * neighbours.shape[1] + 1,), jnp.int32),
            ],
            compiler_params=pltpu.CompilerParams(vmem_limit_bytes=24 * 2**20),
            cost_estimate=pl.CostEstimate(flops=10**6, bytes_accessed=10**4, transcendentals=0),
        )(neighbours, phonon, coupling, *operands)

    sources = (green, coupling, jnp.swapaxes(phonon, 1, 2), neighbours)
    green0, green1, green, coupling, phonon, neighbours = pl.pallas_call(
        fetch_kernel,
        out_shape=[jax.ShapeDtypeStruct(green.shape[1:], green.dtype)] * 2
        + [jax.ShapeDtypeStruct(x.shape, x.dtype) for x in sources],
        in_specs=[ANY] * 4,
        out_specs=[VMEM] * 6,
        scratch_shapes=[pltpu.SemaphoreType.DMA((6,))],
        compiler_params=pltpu.CompilerParams(vmem_limit_bytes=24 * 2**20),
    )(*(pltpu.with_memory_space_constraint(x, pltpu.HBM) for x in sources))
    ahead1 = swap(green1, "atom", 0)
    ahead0 = swap(green0, "atom", 0)
    by_core, by_cross = swap(green, "energy", 0), cross_swap(green, 2)
    total0, total1 = call(own_kernel, [spread] * 2, (green0, green1), parts=2)
    ahead0, total0, total1 = lax.optimization_barrier((ahead0, total0, total1))
    across0 = forward(ahead0, "atom")
    (total0,) = call(pair_kernel, [spread], (ahead0, total0))
    green1, total0 = lax.optimization_barrier((green1, total0))
    across1 = swap(green1, "atom", 1)
    total1, turned = call(
        functools.partial(turn_kernel, energies),
        [spread, (2,) + spread],
        (ahead1, total1, green, by_core, by_cross),
    )
    total0, core0, cross0, partial = call(
        far_kernel, [spread, edge, edge, (a_local, orb, orb)], (across0, total0, turned)
    )
    core0, cross0 = swap(core0, "energy", 0), cross_swap(cross0, 2)
    total1, core1, cross1, rate = call(
        functools.partial(last_kernel, 1.0 / (4.0 * points)),
        [spread, edge, edge, (a_local, orb)],
        (across1, total1, turned, partial),
    )
    core1, cross1 = swap(core1, "energy", 0), cross_swap(cross1, 1)
    cross0, core0, rate = lax.optimization_barrier((cross0, core0, rate))
    rates = addends(rate, "energy")
    return pl.pallas_call(
        functools.partial(end_kernel, energies),
        out_shape=[
            jax.ShapeDtypeStruct(green.shape, jnp.float32),
            jax.ShapeDtypeStruct((a_local, orb), jnp.float32),
        ],
        in_specs=[VMEM] * (6 + len(rates)),
        out_specs=[VMEM] * 2,
        compiler_params=pltpu.CompilerParams(vmem_limit_bytes=24 * 2**20),
        cost_estimate=pl.CostEstimate(flops=10**6, bytes_accessed=2 * 10**6, transcendentals=0),
    )(total0, total1, cross0, core0, cross1, core1, *rates)


def solution(mesh):
    return jax.shard_map(
        per_device,
        mesh=mesh,
        in_specs=(
            P(None, "energy", "atom", None, None),
            P("atom", None, None, None),
            P("atom", None, None),
            P("atom", None),
        ),
        out_specs=(P(None, "energy", "atom", None, None), P("atom", None)),
        check_vma=False,
    )
```

```python
import functools

import jax
import jax.numpy as jnp
from jax import lax
from jax.experimental import pallas as pl
from jax.experimental.pallas import tpu as pltpu
from jax.sharding import PartitionSpec as P

SHIFTS = (-2, -1, 1, 2)
REACH = max(SHIFTS)
OWN, PAIR, FAR = 0, 1, 2
FEW = 4
BATCH = 6
VMEM = pl.BlockSpec(memory_space=pltpu.VMEM)
SMEM = pl.BlockSpec(memory_space=pltpu.SMEM)
ANY = pl.BlockSpec(memory_space=pl.ANY)


def halves(x):
    high = x.astype(jnp.bfloat16)
    return high, (x - high.astype(jnp.float32)).astype(jnp.bfloat16)


def swap(x, axis, first):
    low = range(first, lax.axis_size(axis) - 1, 2)
    return lax.ppermute(x, axis, [(i, i + 1) for i in low] + [(i + 1, i) for i in low])


def exchange(x, partner, spare):
    energies, atoms = lax.axis_size("energy"), lax.axis_size("atom")
    perm = []
    for e in range(energies):
        for a in range(atoms):
            to_e, to_a = partner(e, a)
            if not (0 <= to_e < energies and 0 <= to_a < atoms):
                to_e, to_a = spare(e, a)
            if 0 <= to_e < energies and 0 <= to_a < atoms:
                perm.append((e * atoms + a, to_e * atoms + to_a))
    return lax.ppermute(x, ("energy", "atom"), perm)


def cross_swap(x, step):
    return exchange(x, lambda e, a: (e + 1 if e % 2 else e - 1, a), lambda e, a: (e, a ^ step))


def forward(x, axis):
    size = lax.axis_size(axis)
    ups = [(i, min(i + 2, size - 1)) for i in range(0, size, 2)]
    downs = [(i, max(i - 2, 0)) for i in range(1, size, 2)]
    return lax.ppermute(x, axis, [(i, j) for i, j in ups + downs if i != j])


def put_blocks(blocks, c, green):
    orb = green.shape[-1]
    for e in range(green.shape[0]):
        for a in range(green.shape[1]):
            high, low = halves(green[e, a])
            blocks[c, a, e, :, :orb] = high
            blocks[c, a, e, :, orb:] = low


def add_pairs(group, neighbours, phonon, coupling, blocks, totals, picked, size):
    atoms, slots, orb = coupling.shape[0], coupling.shape[1], coupling.shape[-1]
    e_local = blocks.shape[2]
    index = lax.axis_index("atom")
    base = index * atoms
    if group != OWN:
        upper = (index & 1) == (0 if group == PAIR else 1)
        base += jnp.where(upper, atoms, -atoms)

    found = jnp.int32(0)
    for a in range(atoms):
        for j in range(slots):
            picked[found] = a * slots + j
            b = neighbours[a, j] - base
            found += ((b >= 0) & (b < atoms)).astype(jnp.int32)

    def batch(step, _):
        pairs = []
        for u in range(size):
            at = step * size + u
            item = picked[jnp.minimum(at, found - 1)]
            a = item // slots
            j = item - a * slots
            high, low = halves(coupling[a, j])
            left = jnp.concatenate([high, low], 1)
            right = jnp.concatenate(
                [jnp.concatenate([high, high], 1), jnp.concatenate([low, low], 1)], 0
            )
            pairs.append((a, j, neighbours[a, j] - base, jnp.where(at < found, 1.0, 0.0), left, right))
        inners = []
        for a, j, b, live, left, right in pairs:
            for c in range(len(totals)):
                near = blocks[c, b].reshape(e_local * orb, 2 * orb)
                inner = lax.dot_general(
                    near, right, (((1,), (1,)), ((), ())), preferred_element_type=jnp.float32
                )
                inners.append(inner[:, :orb] + inner[:, orb:])
        results = []
        for a, j, b, live, left, right in pairs:
            for total in totals:
                inner = inners.pop(0)
                sums = [None] * (e_local + 2 * REACH)
                for e in range(e_local):
                    high, low = halves(inner[e * orb : (e + 1) * orb])
                    both = jnp.concatenate([high, low], 1)
                    outer = jnp.dot(
                        left, jnp.concatenate([both, both], 0), preferred_element_type=jnp.float32
                    )
                    outer = outer[:, :orb] + outer[:, orb:]
                    for k, s in enumerate(SHIFTS):
                        d = e - s + REACH
                        term = (phonon[a, k, j] * live) * outer
                        sums[d] = term if sums[d] is None else sums[d] + term
                results.append((total, a, sums))
        for total, a, sums in results:
            for d, value in enumerate(sums):
                if value is not None:
                    total[d, a] += value

    lax.fori_loop(0, (found + size - 1) // size, batch, None)


def fetch_kernel(green, coupling, phonon, neighbours, *rest):
    *results, sems = rest
    sources = [green.at[0], green.at[1], green, coupling, phonon, neighbours]
    copies = [
        pltpu.make_async_copy(source, result, sems.at[i])
        for i, (source, result) in enumerate(zip(sources, results))
    ]
    for copy in copies:
        copy.start()
    for copy in copies:
        copy.wait()


def own_kernel(neighbours, phonon, coupling, green0, green1, total0, total1, blocks, picked):
    for c, (green, total) in enumerate(((green0, total0), (green1, total1))):
        put_blocks(blocks, c, green)
        total[...] = jnp.zeros_like(total)
    add_pairs(OWN, neighbours, phonon, coupling, blocks, (total0, total1), picked, 2)


def pair_kernel(neighbours, phonon, coupling, ahead, before, total, blocks, picked):
    total[...] = before[...]
    put_blocks(blocks, 0, ahead)
    add_pairs(PAIR, neighbours, phonon, coupling, blocks, (total,), picked, BATCH)


def turn_kernel(
    size, neighbours, phonon, coupling, ahead, before, total0, green, by_core, by_cross,
    total, turned, partial, blocks, picked,
):
    e_local, a_local = green.shape[1], green.shape[2]
    core, cross = partner_energies(turned.shape[1])
    has_core, has_cross = has_partners(size)
    for c in range(2):
        for a in range(a_local):
            for e in range(e_local):
                turned[c, REACH + e, a] = green[c, e, a].T
            for e in range(REACH):
                turned[c, core + e, a] = by_core[c, e, a].T * has_core
                turned[c, cross + e, a] = by_cross[c, e, a].T * has_cross
    for a in range(a_local):
        partial[a] = rate_sums(total0, turned, 0, a)
    pair_kernel(neighbours, phonon, coupling, ahead, before, total, blocks, picked)


def partner_energies(spread):
    odd = lax.axis_index("energy") & 1
    return jnp.where(odd == 0, spread - REACH, 0), jnp.where(odd == 0, 0, spread - REACH)


def has_partners(size):
    me = lax.axis_index("energy")
    above, below = jnp.where(me < size - 1, 1.0, 0.0), jnp.where(me > 0, 1.0, 0.0)
    odd = me & 1
    return jnp.where(odd == 0, above, below), jnp.where(odd == 0, below, above)


def finish(total, core, cross):
    to_core, to_cross = partner_energies(total.shape[0])
    for e in range(REACH):
        core[e] = total[to_core + e]
        cross[e] = total[to_cross + e]


def rate_sums(total, turned, c, a):
    sums = total[0, a] * turned[c, 0, a]
    for d in range(1, total.shape[0]):
        sums += total[d, a] * turned[c, d, a]
    return sums


def far_kernel(neighbours, phonon, coupling, across, before, total, core, cross, blocks, picked):
    add_far(neighbours, phonon, coupling, across, before, total, blocks, picked)
    finish(total, core, cross)


def add_far(neighbours, phonon, coupling, across, before, total, blocks, picked):
    total[...] = before[...]
    put_blocks(blocks, 0, across)
    add_pairs(FAR, neighbours, phonon, coupling, blocks, (total,), picked, BATCH)


def last_kernel(
    scale, neighbours, phonon, coupling, across, before, turned, partial,
    total, core, cross, rate, blocks, picked,
):
    add_far(neighbours, phonon, coupling, across, before, total, blocks, picked)
    finish(total, core, cross)
    for a in range(partial.shape[0]):
        sums = partial[a] - rate_sums(total, turned, 1, a)
        rate[a : a + 1, :] = jnp.sum(sums.T, axis=0, keepdims=True) * scale


def addends(x, axis):
    size = lax.axis_size(axis)
    if size > FEW:
        return [lax.psum(x, axis)]
    turns = [[(i, (i + k) % size) for i in range(size)] for k in range(1, size)]
    return [x] + [lax.ppermute(x, axis, turn) for turn in turns]


def end_kernel(size, total0, total1, cross0, core0, cross1, core1, *rest):
    *rates, out, rate = rest
    e_local = out.shape[1]
    has_core, has_cross = has_partners(size)
    for c, (total, cross, core) in enumerate(((total0, cross0, core0), (total1, cross1, core1))):
        for e in range(e_local):
            out[c, e] = total[REACH + e] + core[e] * has_core + cross[e] * has_cross
    rate[...] = sum(r[...] for r in rates)


def per_device(green, coupling, phonon, neighbours):
    _, e_local, a_local, orb, _ = green.shape
    energies = lax.axis_size("energy")
    points = e_local * energies
    spread = (e_local + 2 * REACH, a_local, orb, orb)
    edge = (REACH, a_local, orb, orb)

    def call(kernel, out, operands, parts=1):
        return pl.pallas_call(
            kernel,
            out_shape=[jax.ShapeDtypeStruct(shape, jnp.float32) for shape in out],
            in_specs=[SMEM, SMEM] + [VMEM] * (1 + len(operands)),
            out_specs=[VMEM] * len(out),
            scratch_shapes=[
                pltpu.VMEM((parts, a_local, e_local, orb, 2 * orb), jnp.bfloat16),
                pltpu.SMEM((a_local * neighbours.shape[1] + 1,), jnp.int32),
            ],
            compiler_params=pltpu.CompilerParams(vmem_limit_bytes=24 * 2**20),
            cost_estimate=pl.CostEstimate(flops=10**6, bytes_accessed=10**4, transcendentals=0),
        )(neighbours, phonon, coupling, *operands)

    sources = (green, coupling, jnp.swapaxes(phonon, 1, 2), neighbours)
    green0, green1, green, coupling, phonon, neighbours = pl.pallas_call(
        fetch_kernel,
        out_shape=[jax.ShapeDtypeStruct(green.shape[1:], green.dtype)] * 2
        + [jax.ShapeDtypeStruct(x.shape, x.dtype) for x in sources],
        in_specs=[ANY] * 4,
        out_specs=[VMEM] * 6,
        scratch_shapes=[pltpu.SemaphoreType.DMA((6,))],
        compiler_params=pltpu.CompilerParams(vmem_limit_bytes=24 * 2**20),
    )(*(pltpu.with_memory_space_constraint(x, pltpu.HBM) for x in sources))
    ahead1 = swap(green1, "atom", 0)
    ahead0 = swap(green0, "atom", 0)
    by_core, by_cross = swap(green, "energy", 0), cross_swap(green, 2)
    total0, total1 = call(own_kernel, [spread] * 2, (green0, green1), parts=2)
    ahead0, total0, total1 = lax.optimization_barrier((ahead0, total0, total1))
    across0 = forward(ahead0, "atom")
    (total0,) = call(pair_kernel, [spread], (ahead0, total0))
    green1, total0 = lax.optimization_barrier((green1, total0))
    across1 = swap(green1, "atom", 1)
    ahead1, total0 = lax.optimization_barrier((ahead1, total0))
    total0, core0, cross0 = call(far_kernel, [spread, edge, edge], (across0, total0))
    core0, cross0 = swap(core0, "energy", 0), cross_swap(cross0, 2)
    total1, turned, partial = call(
        functools.partial(turn_kernel, energies),
        [spread, (2,) + spread, (a_local, orb, orb)],
        (ahead1, total1, total0, green, by_core, by_cross),
    )
    total1, core1, cross1, rate = call(
        functools.partial(last_kernel, 1.0 / (4.0 * points)),
        [spread, edge, edge, (a_local, orb)],
        (across1, total1, turned, partial),
    )
    core1, cross1 = swap(core1, "energy", 0), cross_swap(cross1, 1)
    cross0, core0, rate = lax.optimization_barrier((cross0, core0, rate))
    rates = addends(rate, "energy")
    return pl.pallas_call(
        functools.partial(end_kernel, energies),
        out_shape=[
            jax.ShapeDtypeStruct(green.shape, jnp.float32),
            jax.ShapeDtypeStruct((a_local, orb), jnp.float32),
        ],
        in_specs=[VMEM] * (6 + len(rates)),
        out_specs=[VMEM] * 2,
        compiler_params=pltpu.CompilerParams(vmem_limit_bytes=24 * 2**20),
        cost_estimate=pl.CostEstimate(flops=10**6, bytes_accessed=2 * 10**6, transcendentals=0),
    )(total0, total1, cross0, core0, cross1, core1, *rates)


def solution(mesh):
    return jax.shard_map(
        per_device,
        mesh=mesh,
        in_specs=(
            P(None, "energy", "atom", None, None),
            P("atom", None, None, None),
            P("atom", None, None),
            P("atom", None),
        ),
        out_specs=(P(None, "energy", "atom", None, None), P("atom", None)),
        check_vma=False,
    )
```

```python
import functools

import jax
import jax.numpy as jnp
from jax import lax
from jax.experimental import pallas as pl
from jax.experimental.pallas import tpu as pltpu
from jax.sharding import PartitionSpec as P

SHIFTS = (-2, -1, 1, 2)
REACH = max(SHIFTS)
OWN, PAIR, FAR = 0, 1, 2
FEW = 4
BATCH = 6
VMEM = pl.BlockSpec(memory_space=pltpu.VMEM)
SMEM = pl.BlockSpec(memory_space=pltpu.SMEM)
ANY = pl.BlockSpec(memory_space=pl.ANY)


def halves(x):
    high = x.astype(jnp.bfloat16)
    return high, (x - high.astype(jnp.float32)).astype(jnp.bfloat16)


def swap(x, axis, first):
    low = range(first, lax.axis_size(axis) - 1, 2)
    return lax.ppermute(x, axis, [(i, i + 1) for i in low] + [(i + 1, i) for i in low])


def exchange(x, partner, spare):
    energies, atoms = lax.axis_size("energy"), lax.axis_size("atom")
    perm = []
    for e in range(energies):
        for a in range(atoms):
            to_e, to_a = partner(e, a)
            if not (0 <= to_e < energies and 0 <= to_a < atoms):
                to_e, to_a = spare(e, a)
            if 0 <= to_e < energies and 0 <= to_a < atoms:
                perm.append((e * atoms + a, to_e * atoms + to_a))
    return lax.ppermute(x, ("energy", "atom"), perm)


def step_aside(a):
    return a ^ 2


def ends_apart(a):
    atoms = lax.axis_size("atom")
    return ((a - 2) ^ 2) + 2 if atoms % 4 == 0 and 2 <= a < atoms - 2 else a ^ 1


def cross_swap(x, other):
    return exchange(x, lambda e, a: (e + 1 if e % 2 else e - 1, a), lambda e, a: (e, other(a)))


def forward(x, axis):
    size = lax.axis_size(axis)
    ups = [(i, min(i + 2, size - 1)) for i in range(0, size, 2)]
    downs = [(i, max(i - 2, 0)) for i in range(1, size, 2)]
    return lax.ppermute(x, axis, [(i, j) for i, j in ups + downs if i != j])


def put_blocks(blocks, c, green):
    orb = green.shape[-1]
    for e in range(green.shape[0]):
        for a in range(green.shape[1]):
            high, low = halves(green[e, a])
            blocks[c, a, e, :, :orb] = high
            blocks[c, a, e, :, orb:] = low


def add_pairs(group, neighbours, phonon, coupling, blocks, totals, picked, size):
    atoms, slots, orb = coupling.shape[0], coupling.shape[1], coupling.shape[-1]
    e_local = blocks.shape[2]
    index = lax.axis_index("atom")
    base = index * atoms
    if group != OWN:
        upper = (index & 1) == (0 if group == PAIR else 1)
        base += jnp.where(upper, atoms, -atoms)

    found = jnp.int32(0)
    for a in range(atoms):
        for j in range(slots):
            picked[found] = a * slots + j
            b = neighbours[a, j] - base
            found += ((b >= 0) & (b < atoms)).astype(jnp.int32)

    def batch(step, _):
        pairs = []
        for u in range(size):
            at = step * size + u
            item = picked[jnp.minimum(at, found - 1)]
            a = item // slots
            j = item - a * slots
            high, low = halves(coupling[a, j])
            left = jnp.concatenate([high, low], 1)
            right = jnp.concatenate(
                [jnp.concatenate([high, high], 1), jnp.concatenate([low, low], 1)], 0
            )
            pairs.append((a, j, neighbours[a, j] - base, jnp.where(at < found, 1.0, 0.0), left, right))
        inners = []
        for a, j, b, live, left, right in pairs:
            for c in range(len(totals)):
                near = blocks[c, b].reshape(e_local * orb, 2 * orb)
                inner = lax.dot_general(
                    near, right, (((1,), (1,)), ((), ())), preferred_element_type=jnp.float32
                )
                inners.append(inner[:, :orb] + inner[:, orb:])
        results = []
        for a, j, b, live, left, right in pairs:
            for total in totals:
                inner = inners.pop(0)
                sums = [None] * (e_local + 2 * REACH)
                for e in range(e_local):
                    high, low = halves(inner[e * orb : (e + 1) * orb])
                    both = jnp.concatenate([high, low], 1)
                    outer = jnp.dot(
                        left, jnp.concatenate([both, both], 0), preferred_element_type=jnp.float32
                    )
                    outer = outer[:, :orb] + outer[:, orb:]
                    for k, s in enumerate(SHIFTS):
                        d = e - s + REACH
                        term = (phonon[a, k, j] * live) * outer
                        sums[d] = term if sums[d] is None else sums[d] + term
                results.append((total, a, sums))
        for total, a, sums in results:
            for d, value in enumerate(sums):
                if value is not None:
                    total[d, a] += value

    lax.fori_loop(0, (found + size - 1) // size, batch, None)


def fetch_kernel(green, coupling, phonon, neighbours, *rest):
    *results, sems = rest
    sources = [green.at[0], green.at[1], green, coupling, phonon, neighbours]
    copies = [
        pltpu.make_async_copy(source, result, sems.at[i])
        for i, (source, result) in enumerate(zip(sources, results))
    ]
    for copy in copies:
        copy.start()
    for copy in copies:
        copy.wait()


def own_kernel(neighbours, phonon, coupling, green0, green1, total0, total1, blocks, picked):
    for c, (green, total) in enumerate(((green0, total0), (green1, total1))):
        put_blocks(blocks, c, green)
        total[...] = jnp.zeros_like(total)
    add_pairs(OWN, neighbours, phonon, coupling, blocks, (total0, total1), picked, 2)


def pair_kernel(neighbours, phonon, coupling, ahead, before, total, blocks, picked):
    total[...] = before[...]
    put_blocks(blocks, 0, ahead)
    add_pairs(PAIR, neighbours, phonon, coupling, blocks, (total,), picked, BATCH)


def turn_kernel(
    size, neighbours, phonon, coupling, ahead, before, green, by_core, by_cross,
    total, turned, blocks, picked,
):
    e_local, a_local = green.shape[1], green.shape[2]
    core, cross = partner_energies(turned.shape[1])
    has_core, has_cross = has_partners(size)
    for c in range(2):
        for a in range(a_local):
            for e in range(e_local):
                turned[c, REACH + e, a] = green[c, e, a].T
            for e in range(REACH):
                turned[c, core + e, a] = by_core[c, e, a].T * has_core
                turned[c, cross + e, a] = by_cross[c, e, a].T * has_cross
    pair_kernel(neighbours, phonon, coupling, ahead, before, total, blocks, picked)


def partner_energies(spread):
    odd = lax.axis_index("energy") & 1
    return jnp.where(odd == 0, spread - REACH, 0), jnp.where(odd == 0, 0, spread - REACH)


def has_partners(size):
    me = lax.axis_index("energy")
    above, below = jnp.where(me < size - 1, 1.0, 0.0), jnp.where(me > 0, 1.0, 0.0)
    odd = me & 1
    return jnp.where(odd == 0, above, below), jnp.where(odd == 0, below, above)


def finish(total, core, cross):
    to_core, to_cross = partner_energies(total.shape[0])
    for e in range(REACH):
        core[e] = total[to_core + e]
        cross[e] = total[to_cross + e]


def rate_sums(total, turned, c, a):
    sums = total[0, a] * turned[c, 0, a]
    for d in range(1, total.shape[0]):
        sums += total[d, a] * turned[c, d, a]
    return sums


def far_kernel(
    neighbours, phonon, coupling, across, before, turned, total, core, cross, partial, blocks, picked
):
    add_far(neighbours, phonon, coupling, across, before, total, blocks, picked)
    finish(total, core, cross)
    for a in range(partial.shape[0]):
        partial[a] = rate_sums(total, turned, 0, a)


def add_far(neighbours, phonon, coupling, across, before, total, blocks, picked):
    total[...] = before[...]
    put_blocks(blocks, 0, across)
    add_pairs(FAR, neighbours, phonon, coupling, blocks, (total,), picked, BATCH)


def last_kernel(
    scale, neighbours, phonon, coupling, across, before, turned, partial,
    total, core, cross, rate, blocks, picked,
):
    add_far(neighbours, phonon, coupling, across, before, total, blocks, picked)
    finish(total, core, cross)
    for a in range(partial.shape[0]):
        sums = partial[a] - rate_sums(total, turned, 1, a)
        rate[a : a + 1, :] = jnp.sum(sums.T, axis=0, keepdims=True) * scale


def addends(x, axis):
    size = lax.axis_size(axis)
    if size > FEW:
        return [lax.psum(x, axis)]
    turns = [[(i, (i + k) % size) for i in range(size)] for k in range(1, size)]
    return [x] + [lax.ppermute(x, axis, turn) for turn in turns]


def end_kernel(size, total0, total1, cross0, core0, cross1, core1, *rest):
    *rates, out, rate = rest
    e_local = out.shape[1]
    has_core, has_cross = has_partners(size)
    for c, (total, cross, core) in enumerate(((total0, cross0, core0), (total1, cross1, core1))):
        for e in range(e_local):
            out[c, e] = total[REACH + e] + core[e] * has_core + cross[e] * has_cross
    rate[...] = sum(r[...] for r in rates)


def per_device(green, coupling, phonon, neighbours):
    _, e_local, a_local, orb, _ = green.shape
    energies = lax.axis_size("energy")
    points = e_local * energies
    spread = (e_local + 2 * REACH, a_local, orb, orb)
    edge = (REACH, a_local, orb, orb)

    def call(kernel, out, operands, parts=1):
        return pl.pallas_call(
            kernel,
            out_shape=[jax.ShapeDtypeStruct(shape, jnp.float32) for shape in out],
            in_specs=[SMEM, SMEM] + [VMEM] * (1 + len(operands)),
            out_specs=[VMEM] * len(out),
            scratch_shapes=[
                pltpu.VMEM((parts, a_local, e_local, orb, 2 * orb), jnp.bfloat16),
                pltpu.SMEM((a_local * neighbours.shape[1] + 1,), jnp.int32),
            ],
            compiler_params=pltpu.CompilerParams(vmem_limit_bytes=24 * 2**20),
            cost_estimate=pl.CostEstimate(flops=10**6, bytes_accessed=10**4, transcendentals=0),
        )(neighbours, phonon, coupling, *operands)

    sources = (green, coupling, jnp.swapaxes(phonon, 1, 2), neighbours)
    green0, green1, green, coupling, phonon, neighbours = pl.pallas_call(
        fetch_kernel,
        out_shape=[jax.ShapeDtypeStruct(green.shape[1:], green.dtype)] * 2
        + [jax.ShapeDtypeStruct(x.shape, x.dtype) for x in sources],
        in_specs=[ANY] * 4,
        out_specs=[VMEM] * 6,
        scratch_shapes=[pltpu.SemaphoreType.DMA((6,))],
        compiler_params=pltpu.CompilerParams(vmem_limit_bytes=24 * 2**20),
    )(*(pltpu.with_memory_space_constraint(x, pltpu.HBM) for x in sources))
    ahead1 = swap(green1, "atom", 0)
    ahead0 = swap(green0, "atom", 0)
    by_core, by_cross = swap(green, "energy", 0), cross_swap(green, step_aside)
    total0, total1 = call(own_kernel, [spread] * 2, (green0, green1), parts=2)
    ahead0, total0, total1 = lax.optimization_barrier((ahead0, total0, total1))
    across0 = forward(ahead0, "atom")
    (total0,) = call(pair_kernel, [spread], (ahead0, total0))
    green1, total0 = lax.optimization_barrier((green1, total0))
    across1 = swap(green1, "atom", 1)
    total1, turned = call(
        functools.partial(turn_kernel, energies),
        [spread, (2,) + spread],
        (ahead1, total1, green, by_core, by_cross),
    )
    total0, core0, cross0, partial = call(
        far_kernel, [spread, edge, edge, (a_local, orb, orb)], (across0, total0, turned)
    )
    core0, cross0 = swap(core0, "energy", 0), cross_swap(cross0, ends_apart)
    total1, core1, cross1, rate = call(
        functools.partial(last_kernel, 1.0 / (4.0 * points)),
        [spread, edge, edge, (a_local, orb)],
        (across1, total1, turned, partial),
    )
    core1, cross1 = swap(core1, "energy", 0), swap(cross1, "energy", 1)
    cross0, core0, rate = lax.optimization_barrier((cross0, core0, rate))
    rates = addends(rate, "energy")
    return pl.pallas_call(
        functools.partial(end_kernel, energies),
        out_shape=[
            jax.ShapeDtypeStruct(green.shape, jnp.float32),
            jax.ShapeDtypeStruct((a_local, orb), jnp.float32),
        ],
        in_specs=[VMEM] * (6 + len(rates)),
        out_specs=[VMEM] * 2,
        compiler_params=pltpu.CompilerParams(vmem_limit_bytes=24 * 2**20),
        cost_estimate=pl.CostEstimate(flops=10**6, bytes_accessed=2 * 10**6, transcendentals=0),
    )(total0, total1, cross0, core0, cross1, core1, *rates)


def solution(mesh):
    return jax.shard_map(
        per_device,
        mesh=mesh,
        in_specs=(
            P(None, "energy", "atom", None, None),
            P("atom", None, None, None),
            P("atom", None, None),
            P("atom", None),
        ),
        out_specs=(P(None, "energy", "atom", None, None), P("atom", None)),
        check_vma=False,
    )
```

```python
import functools

import jax
import jax.numpy as jnp
from jax import lax
from jax.experimental import pallas as pl
from jax.experimental.pallas import tpu as pltpu
from jax.sharding import PartitionSpec as P

SHIFTS = (-2, -1, 1, 2)
REACH = max(SHIFTS)
OWN, PAIR, FAR = 0, 1, 2
FEW = 4
BATCH = 6
VMEM = pl.BlockSpec(memory_space=pltpu.VMEM)
SMEM = pl.BlockSpec(memory_space=pltpu.SMEM)
ANY = pl.BlockSpec(memory_space=pl.ANY)


def halves(x):
    high = x.astype(jnp.bfloat16)
    return high, (x - high.astype(jnp.float32)).astype(jnp.bfloat16)


def swap(x, axis, first):
    low = range(first, lax.axis_size(axis) - 1, 2)
    return lax.ppermute(x, axis, [(i, i + 1) for i in low] + [(i + 1, i) for i in low])


def exchange(x, partner, spare):
    energies, atoms = lax.axis_size("energy"), lax.axis_size("atom")
    perm = []
    for e in range(energies):
        for a in range(atoms):
            to_e, to_a = partner(e, a)
            if not (0 <= to_e < energies and 0 <= to_a < atoms):
                to_e, to_a = spare(e, a)
            if 0 <= to_e < energies and 0 <= to_a < atoms:
                perm.append((e * atoms + a, to_e * atoms + to_a))
    return lax.ppermute(x, ("energy", "atom"), perm)


def cross_swap(x, step):
    return exchange(x, lambda e, a: (e + 1 if e % 2 else e - 1, a), lambda e, a: (e, a ^ step))


def forward(x, axis):
    size = lax.axis_size(axis)
    ups = [(i, min(i + 2, size - 1)) for i in range(0, size, 2)]
    downs = [(i, max(i - 2, 0)) for i in range(1, size, 2)]
    return lax.ppermute(x, axis, [(i, j) for i, j in ups + downs if i != j])


def put_blocks(blocks, c, green):
    orb = green.shape[-1]
    for e in range(green.shape[0]):
        for a in range(green.shape[1]):
            high, low = halves(green[e, a])
            blocks[c, a, e, :, :orb] = high
            blocks[c, a, e, :, orb:] = low


def add_pairs(group, neighbours, phonon, coupling, blocks, totals, picked, size):
    atoms, slots, orb = coupling.shape[0], coupling.shape[1], coupling.shape[-1]
    e_local = blocks.shape[2]
    index = lax.axis_index("atom")
    base = index * atoms
    if group != OWN:
        upper = (index & 1) == (0 if group == PAIR else 1)
        base += jnp.where(upper, atoms, -atoms)

    found = jnp.int32(0)
    for a in range(atoms):
        for j in range(slots):
            picked[found] = a * slots + j
            b = neighbours[a, j] - base
            found += ((b >= 0) & (b < atoms)).astype(jnp.int32)

    def batch(step, _):
        pairs = []
        for u in range(size):
            at = step * size + u
            item = picked[jnp.minimum(at, found - 1)]
            a = item // slots
            j = item - a * slots
            high, low = halves(coupling[a, j])
            left = jnp.concatenate([high, low], 1)
            right = jnp.concatenate(
                [jnp.concatenate([high, high], 1), jnp.concatenate([low, low], 1)], 0
            )
            pairs.append((a, j, neighbours[a, j] - base, jnp.where(at < found, 1.0, 0.0), left, right))
        inners = []
        for a, j, b, live, left, right in pairs:
            for c in range(len(totals)):
                near = blocks[c, b].reshape(e_local * orb, 2 * orb)
                inner = lax.dot_general(
                    near, right, (((1,), (1,)), ((), ())), preferred_element_type=jnp.float32
                )
                inners.append(inner[:, :orb] + inner[:, orb:])
        results = []
        for a, j, b, live, left, right in pairs:
            for total in totals:
                inner = inners.pop(0)
                sums = [None] * (e_local + 2 * REACH)
                for e in range(e_local):
                    high, low = halves(inner[e * orb : (e + 1) * orb])
                    both = jnp.concatenate([high, low], 1)
                    outer = jnp.dot(
                        left, jnp.concatenate([both, both], 0), preferred_element_type=jnp.float32
                    )
                    outer = outer[:, :orb] + outer[:, orb:]
                    for k, s in enumerate(SHIFTS):
                        d = e - s + REACH
                        term = (phonon[a, k, j] * live) * outer
                        sums[d] = term if sums[d] is None else sums[d] + term
                results.append((total, a, sums))
        for total, a, sums in results:
            for d, value in enumerate(sums):
                if value is not None:
                    total[d, a] += value

    lax.fori_loop(0, (found + size - 1) // size, batch, None)


def copy_all(sources, results, sems):
    copies = [
        pltpu.make_async_copy(source, result, sems.at[i])
        for i, (source, result) in enumerate(zip(sources, results))
    ]
    for copy in copies:
        copy.start()
    for copy in copies:
        copy.wait()


def part_kernel(green, part, sems):
    copy_all([green.at[0]], [part], sems)


def fetch_kernel(green, coupling, phonon, neighbours, *rest):
    copy_all([green.at[1], green, coupling, phonon, neighbours], rest[:-1], rest[-1])


def own_kernel(neighbours, phonon, coupling, green0, green1, total0, total1, blocks, picked):
    for c, (green, total) in enumerate(((green0, total0), (green1, total1))):
        put_blocks(blocks, c, green)
        total[...] = jnp.zeros_like(total)
    add_pairs(OWN, neighbours, phonon, coupling, blocks, (total0, total1), picked, 2)


def pair_kernel(neighbours, phonon, coupling, ahead, before, total, blocks, picked):
    total[...] = before[...]
    put_blocks(blocks, 0, ahead)
    add_pairs(PAIR, neighbours, phonon, coupling, blocks, (total,), picked, BATCH)


def turn_kernel(
    size, neighbours, phonon, coupling, ahead, before, green, by_core, by_cross,
    total, turned, blocks, picked,
):
    e_local, a_local = green.shape[1], green.shape[2]
    core, cross = partner_energies(turned.shape[1])
    has_core, has_cross = has_partners(size)
    for c in range(2):
        for a in range(a_local):
            for e in range(e_local):
                turned[c, REACH + e, a] = green[c, e, a].T
            for e in range(REACH):
                turned[c, core + e, a] = by_core[c, e, a].T * has_core
                turned[c, cross + e, a] = by_cross[c, e, a].T * has_cross
    pair_kernel(neighbours, phonon, coupling, ahead, before, total, blocks, picked)


def partner_energies(spread):
    odd = lax.axis_index("energy") & 1
    return jnp.where(odd == 0, spread - REACH, 0), jnp.where(odd == 0, 0, spread - REACH)


def has_partners(size):
    me = lax.axis_index("energy")
    above, below = jnp.where(me < size - 1, 1.0, 0.0), jnp.where(me > 0, 1.0, 0.0)
    odd = me & 1
    return jnp.where(odd == 0, above, below), jnp.where(odd == 0, below, above)


def finish(total, core, cross):
    to_core, to_cross = partner_energies(total.shape[0])
    for e in range(REACH):
        core[e] = total[to_core + e]
        cross[e] = total[to_cross + e]


def rate_sums(total, turned, c, a):
    sums = total[0, a] * turned[c, 0, a]
    for d in range(1, total.shape[0]):
        sums += total[d, a] * turned[c, d, a]
    return sums


def far_kernel(
    neighbours, phonon, coupling, across, before, turned, total, core, cross, partial, blocks, picked
):
    add_far(neighbours, phonon, coupling, across, before, total, blocks, picked)
    finish(total, core, cross)
    for a in range(partial.shape[0]):
        partial[a] = rate_sums(total, turned, 0, a)


def add_far(neighbours, phonon, coupling, across, before, total, blocks, picked):
    total[...] = before[...]
    put_blocks(blocks, 0, across)
    add_pairs(FAR, neighbours, phonon, coupling, blocks, (total,), picked, BATCH)


def last_kernel(
    scale, neighbours, phonon, coupling, across, before, turned, partial,
    total, core, cross, rate, blocks, picked,
):
    add_far(neighbours, phonon, coupling, across, before, total, blocks, picked)
    finish(total, core, cross)
    for a in range(partial.shape[0]):
        sums = partial[a] - rate_sums(total, turned, 1, a)
        rate[a : a + 1, :] = jnp.sum(sums.T, axis=0, keepdims=True) * scale


def addends(x, axis):
    size = lax.axis_size(axis)
    if size > FEW:
        return [lax.psum(x, axis)]
    turns = [[(i, (i + k) % size) for i in range(size)] for k in range(1, size)]
    return [x] + [lax.ppermute(x, axis, turn) for turn in turns]


def end_kernel(size, total0, total1, cross0, core0, cross1, core1, *rest):
    *rates, out, rate = rest
    e_local = out.shape[1]
    has_core, has_cross = has_partners(size)
    for c, (total, cross, core) in enumerate(((total0, cross0, core0), (total1, cross1, core1))):
        for e in range(e_local):
            out[c, e] = total[REACH + e] + core[e] * has_core + cross[e] * has_cross
    rate[...] = sum(r[...] for r in rates)


def per_device(green, coupling, phonon, neighbours):
    _, e_local, a_local, orb, _ = green.shape
    energies = lax.axis_size("energy")
    points = e_local * energies
    spread = (e_local + 2 * REACH, a_local, orb, orb)
    edge = (REACH, a_local, orb, orb)

    def call(kernel, out, operands, parts=1):
        return pl.pallas_call(
            kernel,
            out_shape=[jax.ShapeDtypeStruct(shape, jnp.float32) for shape in out],
            in_specs=[SMEM, SMEM] + [VMEM] * (1 + len(operands)),
            out_specs=[VMEM] * len(out),
            scratch_shapes=[
                pltpu.VMEM((parts, a_local, e_local, orb, 2 * orb), jnp.bfloat16),
                pltpu.SMEM((a_local * neighbours.shape[1] + 1,), jnp.int32),
            ],
            compiler_params=pltpu.CompilerParams(vmem_limit_bytes=24 * 2**20),
            cost_estimate=pl.CostEstimate(flops=10**6, bytes_accessed=10**4, transcendentals=0),
        )(neighbours, phonon, coupling, *operands)

    def fetch(kernel, out, sources):
        return pl.pallas_call(
            kernel,
            out_shape=[jax.ShapeDtypeStruct(x.shape, x.dtype) for x in out],
            in_specs=[ANY] * len(sources),
            out_specs=[VMEM] * len(out),
            scratch_shapes=[pltpu.SemaphoreType.DMA((len(out),))],
            compiler_params=pltpu.CompilerParams(vmem_limit_bytes=24 * 2**20),
        )(*(pltpu.with_memory_space_constraint(x, pltpu.HBM) for x in sources))

    sources = (green, coupling, jnp.swapaxes(phonon, 1, 2), neighbours)
    part = jax.ShapeDtypeStruct(green.shape[1:], green.dtype)
    (green0,) = fetch(part_kernel, [part], [green])
    green0, *sources = lax.optimization_barrier((green0, *sources))
    green1, green, coupling, phonon, neighbours = fetch(fetch_kernel, [part, *sources], sources)
    ahead1 = swap(green1, "atom", 0)
    ahead0 = swap(green0, "atom", 0)
    by_core, by_cross = swap(green, "energy", 0), cross_swap(green, 2)
    total0, total1 = call(own_kernel, [spread] * 2, (green0, green1), parts=2)
    ahead0, total0, total1 = lax.optimization_barrier((ahead0, total0, total1))
    across0 = forward(ahead0, "atom")
    (total0,) = call(pair_kernel, [spread], (ahead0, total0))
    green1, total0 = lax.optimization_barrier((green1, total0))
    across1 = swap(green1, "atom", 1)
    total1, turned = call(
        functools.partial(turn_kernel, energies),
        [spread, (2,) + spread],
        (ahead1, total1, green, by_core, by_cross),
    )
    total0, core0, cross0, partial = call(
        far_kernel, [spread, edge, edge, (a_local, orb, orb)], (across0, total0, turned)
    )
    core0, cross0 = swap(core0, "energy", 0), cross_swap(cross0, 2)
    total1, core1, cross1, rate = call(
        functools.partial(last_kernel, 1.0 / (4.0 * points)),
        [spread, edge, edge, (a_local, orb)],
        (across1, total1, turned, partial),
    )
    core1, cross1 = swap(core1, "energy", 0), cross_swap(cross1, 1)
    cross0, core0, rate = lax.optimization_barrier((cross0, core0, rate))
    rates = addends(rate, "energy")
    return pl.pallas_call(
        functools.partial(end_kernel, energies),
        out_shape=[
            jax.ShapeDtypeStruct(green.shape, jnp.float32),
            jax.ShapeDtypeStruct((a_local, orb), jnp.float32),
        ],
        in_specs=[VMEM] * (6 + len(rates)),
        out_specs=[VMEM] * 2,
        compiler_params=pltpu.CompilerParams(vmem_limit_bytes=24 * 2**20),
        cost_estimate=pl.CostEstimate(flops=10**6, bytes_accessed=2 * 10**6, transcendentals=0),
    )(total0, total1, cross0, core0, cross1, core1, *rates)


def solution(mesh):
    return jax.shard_map(
        per_device,
        mesh=mesh,
        in_specs=(
            P(None, "energy", "atom", None, None),
            P("atom", None, None, None),
            P("atom", None, None),
            P("atom", None),
        ),
        out_specs=(P(None, "energy", "atom", None, None), P("atom", None)),
        check_vma=False,
    )
```

```python
import functools

import jax
import jax.numpy as jnp
from jax import lax
from jax.experimental import pallas as pl
from jax.experimental.pallas import tpu as pltpu
from jax.sharding import PartitionSpec as P

SHIFTS = (-2, -1, 1, 2)
REACH = max(SHIFTS)
OWN, PAIR, FAR = 0, 1, 2
FEW = 4
BATCH = 6
VMEM = pl.BlockSpec(memory_space=pltpu.VMEM)
SMEM = pl.BlockSpec(memory_space=pltpu.SMEM)
ANY = pl.BlockSpec(memory_space=pl.ANY)


def halves(x):
    high = x.astype(jnp.bfloat16)
    return high, (x - high.astype(jnp.float32)).astype(jnp.bfloat16)


def swap(x, axis, first):
    low = range(first, lax.axis_size(axis) - 1, 2)
    return lax.ppermute(x, axis, [(i, i + 1) for i in low] + [(i + 1, i) for i in low])


def exchange(x, partner, spare):
    energies, atoms = lax.axis_size("energy"), lax.axis_size("atom")
    perm = []
    for e in range(energies):
        for a in range(atoms):
            to_e, to_a = partner(e, a)
            if not (0 <= to_e < energies and 0 <= to_a < atoms):
                to_e, to_a = spare(e, a)
            if 0 <= to_e < energies and 0 <= to_a < atoms:
                perm.append((e * atoms + a, to_e * atoms + to_a))
    return lax.ppermute(x, ("energy", "atom"), perm)


def cross_swap(x, step):
    return exchange(x, lambda e, a: (e + 1 if e % 2 else e - 1, a), lambda e, a: (e, a ^ step))


def forward(x, axis):
    size = lax.axis_size(axis)
    ups = [(i, min(i + 2, size - 1)) for i in range(0, size, 2)]
    downs = [(i, max(i - 2, 0)) for i in range(1, size, 2)]
    return lax.ppermute(x, axis, [(i, j) for i, j in ups + downs if i != j])


def put_blocks(blocks, c, green):
    orb = green.shape[-1]
    for e in range(green.shape[0]):
        for a in range(green.shape[1]):
            high, low = halves(green[e, a])
            blocks[c, a, e, :, :orb] = high
            blocks[c, a, e, :, orb:] = low


def add_pairs(group, neighbours, phonon, coupling, blocks, totals, picked, size):
    atoms, slots, orb = coupling.shape[0], coupling.shape[1], coupling.shape[-1]
    e_local = blocks.shape[2]
    index = lax.axis_index("atom")
    base = index * atoms
    if group != OWN:
        upper = (index & 1) == (0 if group == PAIR else 1)
        base += jnp.where(upper, atoms, -atoms)

    found = jnp.int32(0)
    for a in range(atoms):
        for j in range(slots):
            picked[found] = a * slots + j
            b = neighbours[a, j] - base
            found += ((b >= 0) & (b < atoms)).astype(jnp.int32)

    def batch(step, _):
        pairs = []
        for u in range(size):
            at = step * size + u
            item = picked[jnp.minimum(at, found - 1)]
            a = item // slots
            j = item - a * slots
            high, low = halves(coupling[a, j])
            left = jnp.concatenate([high, low], 1)
            right = jnp.concatenate(
                [jnp.concatenate([high, high], 1), jnp.concatenate([low, low], 1)], 0
            )
            pairs.append((a, j, neighbours[a, j] - base, jnp.where(at < found, 1.0, 0.0), left, right))
        inners = []
        for a, j, b, live, left, right in pairs:
            for c in range(len(totals)):
                near = blocks[c, b].reshape(e_local * orb, 2 * orb)
                inner = lax.dot_general(
                    near, right, (((1,), (1,)), ((), ())), preferred_element_type=jnp.float32
                )
                inners.append(inner[:, :orb] + inner[:, orb:])
        results = []
        for a, j, b, live, left, right in pairs:
            for total in totals:
                inner = inners.pop(0)
                sums = [None] * (e_local + 2 * REACH)
                for e in range(e_local):
                    high, low = halves(inner[e * orb : (e + 1) * orb])
                    both = jnp.concatenate([high, low], 1)
                    outer = jnp.dot(
                        left, jnp.concatenate([both, both], 0), preferred_element_type=jnp.float32
                    )
                    outer = outer[:, :orb] + outer[:, orb:]
                    for k, s in enumerate(SHIFTS):
                        d = e - s + REACH
                        term = (phonon[a, k, j] * live) * outer
                        sums[d] = term if sums[d] is None else sums[d] + term
                results.append((total, a, sums))
        for total, a, sums in results:
            for d, value in enumerate(sums):
                if value is not None:
                    total[d, a] += value

    lax.fori_loop(0, (found + size - 1) // size, batch, None)


def copy_all(sources, results, sems):
    copies = [
        pltpu.make_async_copy(source, result, sems.at[i])
        for i, (source, result) in enumerate(zip(sources, results))
    ]
    for copy in copies:
        copy.start()
    for copy in copies:
        copy.wait()


def part_kernel(green, part, sems):
    copy_all([green.at[0]], [part], sems)


def fetch_kernel(green, coupling, phonon, neighbours, *rest):
    copy_all([green.at[1], green, coupling, phonon, neighbours], rest[:-1], rest[-1])


def own_kernel(neighbours, phonon, coupling, green0, green1, total0, total1, blocks, picked):
    for c, (green, total) in enumerate(((green0, total0), (green1, total1))):
        put_blocks(blocks, c, green)
        total[...] = jnp.zeros_like(total)
    add_pairs(OWN, neighbours, phonon, coupling, blocks, (total0, total1), picked, 2)


def pair_kernel(neighbours, phonon, coupling, ahead, before, total, blocks, picked):
    total[...] = before[...]
    put_blocks(blocks, 0, ahead)
    add_pairs(PAIR, neighbours, phonon, coupling, blocks, (total,), picked, BATCH)


def turn_kernel(
    size, neighbours, phonon, coupling, ahead, before, green, by_core, by_cross,
    total, turned, blocks, picked,
):
    e_local, a_local = green.shape[1], green.shape[2]
    core, cross = partner_energies(turned.shape[1])
    has_core, has_cross = has_partners(size)
    for c in range(2):
        for a in range(a_local):
            for e in range(e_local):
                turned[c, REACH + e, a] = green[c, e, a].T
            for e in range(REACH):
                turned[c, core + e, a] = by_core[c, e, a].T * has_core
                turned[c, cross + e, a] = by_cross[c, e, a].T * has_cross
    pair_kernel(neighbours, phonon, coupling, ahead, before, total, blocks, picked)


def partner_energies(spread):
    odd = lax.axis_index("energy") & 1
    return jnp.where(odd == 0, spread - REACH, 0), jnp.where(odd == 0, 0, spread - REACH)


def has_partners(size):
    me = lax.axis_index("energy")
    above, below = jnp.where(me < size - 1, 1.0, 0.0), jnp.where(me > 0, 1.0, 0.0)
    odd = me & 1
    return jnp.where(odd == 0, above, below), jnp.where(odd == 0, below, above)


def finish(total, core, cross):
    to_core, to_cross = partner_energies(total.shape[0])
    for e in range(REACH):
        core[e] = total[to_core + e]
        cross[e] = total[to_cross + e]


def rate_sums(total, turned, c, a):
    sums = total[0, a] * turned[c, 0, a]
    for d in range(1, total.shape[0]):
        sums += total[d, a] * turned[c, d, a]
    return sums


def far_kernel(
    neighbours, phonon, coupling, across, before, turned, total, core, cross, partial, blocks, picked
):
    add_far(neighbours, phonon, coupling, across, before, total, blocks, picked)
    finish(total, core, cross)
    for a in range(partial.shape[0]):
        partial[a] = rate_sums(total, turned, 0, a)


def add_far(neighbours, phonon, coupling, across, before, total, blocks, picked):
    total[...] = before[...]
    put_blocks(blocks, 0, across)
    add_pairs(FAR, neighbours, phonon, coupling, blocks, (total,), picked, BATCH)


def last_kernel(
    scale, neighbours, phonon, coupling, across, before, turned, partial,
    total, core, cross, rate, blocks, picked,
):
    add_far(neighbours, phonon, coupling, across, before, total, blocks, picked)
    finish(total, core, cross)
    for a in range(partial.shape[0]):
        sums = partial[a] - rate_sums(total, turned, 1, a)
        rate[a : a + 1, :] = jnp.sum(sums.T, axis=0, keepdims=True) * scale


def addends(x, axis):
    size = lax.axis_size(axis)
    if size > FEW:
        return [lax.psum(x, axis)]
    turns = [[(i, (i + k) % size) for i in range(size)] for k in range(1, size)]
    return [x] + [lax.ppermute(x, axis, turn) for turn in turns]


def end_kernel(size, total0, total1, cross0, core0, cross1, core1, *rest):
    *rates, out, rate = rest
    e_local = out.shape[1]
    has_core, has_cross = has_partners(size)
    for c, (total, cross, core) in enumerate(((total0, cross0, core0), (total1, cross1, core1))):
        for e in range(e_local):
            out[c, e] = total[REACH + e] + core[e] * has_core + cross[e] * has_cross
    rate[...] = sum(r[...] for r in rates)


def per_device(green, coupling, phonon, neighbours):
    _, e_local, a_local, orb, _ = green.shape
    energies = lax.axis_size("energy")
    points = e_local * energies
    spread = (e_local + 2 * REACH, a_local, orb, orb)
    edge = (REACH, a_local, orb, orb)

    def call(kernel, out, operands, parts=1):
        return pl.pallas_call(
            kernel,
            out_shape=[jax.ShapeDtypeStruct(shape, jnp.float32) for shape in out],
            in_specs=[SMEM, SMEM] + [VMEM] * (1 + len(operands)),
            out_specs=[VMEM] * len(out),
            scratch_shapes=[
                pltpu.VMEM((parts, a_local, e_local, orb, 2 * orb), jnp.bfloat16),
                pltpu.SMEM((a_local * neighbours.shape[1] + 1,), jnp.int32),
            ],
            compiler_params=pltpu.CompilerParams(vmem_limit_bytes=24 * 2**20),
            cost_estimate=pl.CostEstimate(flops=10**6, bytes_accessed=10**4, transcendentals=0),
        )(neighbours, phonon, coupling, *operands)

    def fetch(kernel, out, sources):
        return pl.pallas_call(
            kernel,
            out_shape=[jax.ShapeDtypeStruct(x.shape, x.dtype) for x in out],
            in_specs=[ANY] * len(sources),
            out_specs=[VMEM] * len(out),
            scratch_shapes=[pltpu.SemaphoreType.DMA((len(out),))],
            compiler_params=pltpu.CompilerParams(vmem_limit_bytes=24 * 2**20),
        )(*(pltpu.with_memory_space_constraint(x, pltpu.HBM) for x in sources))

    sources = (green, coupling, jnp.swapaxes(phonon, 1, 2), neighbours)
    part = jax.ShapeDtypeStruct(green.shape[1:], green.dtype)
    (green0,) = fetch(part_kernel, [part], [green])
    green0, *sources = lax.optimization_barrier((green0, *sources))
    green1, green, coupling, phonon, neighbours = fetch(fetch_kernel, [part, *sources], sources)
    ahead1 = swap(green1, "atom", 0)
    ahead0 = swap(green0, "atom", 0)
    by_core, by_cross = swap(green, "energy", 0), cross_swap(green, 2)
    total0, total1 = call(own_kernel, [spread] * 2, (green0, green1), parts=2)
    ahead0, total0, total1 = lax.optimization_barrier((ahead0, total0, total1))
    across0 = forward(ahead0, "atom")
    (total0,) = call(pair_kernel, [spread], (ahead0, total0))
    green1, total0 = lax.optimization_barrier((green1, total0))
    across1 = swap(green1, "atom", 1)
    total1, turned = call(
        functools.partial(turn_kernel, energies),
        [spread, (2,) + spread],
        (ahead1, total1, green, by_core, by_cross),
    )
    total0, core0, cross0, partial = call(
        far_kernel, [spread, edge, edge, (a_local, orb, orb)], (across0, total0, turned)
    )
    core0, cross0 = swap(core0, "energy", 0), cross_swap(cross0, 2)
    total1, core1, cross1, rate = call(
        functools.partial(last_kernel, 1.0 / (4.0 * points)),
        [spread, edge, edge, (a_local, orb)],
        (across1, total1, turned, partial),
    )
    cross1 = cross_swap(cross1, 1)
    core0, rate = lax.optimization_barrier((core0, rate))
    rates = addends(rate, "energy")
    cross0, core1, rates = lax.optimization_barrier((cross0, core1, rates))
    core1 = swap(core1, "energy", 0)
    return pl.pallas_call(
        functools.partial(end_kernel, energies),
        out_shape=[
            jax.ShapeDtypeStruct(green.shape, jnp.float32),
            jax.ShapeDtypeStruct((a_local, orb), jnp.float32),
        ],
        in_specs=[VMEM] * (6 + len(rates)),
        out_specs=[VMEM] * 2,
        compiler_params=pltpu.CompilerParams(vmem_limit_bytes=24 * 2**20),
        cost_estimate=pl.CostEstimate(flops=10**6, bytes_accessed=2 * 10**6, transcendentals=0),
    )(total0, total1, cross0, core0, cross1, core1, *rates)


def solution(mesh):
    return jax.shard_map(
        per_device,
        mesh=mesh,
        in_specs=(
            P(None, "energy", "atom", None, None),
            P("atom", None, None, None),
            P("atom", None, None),
            P("atom", None),
        ),
        out_specs=(P(None, "energy", "atom", None, None), P("atom", None)),
        check_vma=False,
    )
```

```python
import functools

import jax
import jax.numpy as jnp
from jax import lax
from jax.experimental import pallas as pl
from jax.experimental.pallas import tpu as pltpu
from jax.sharding import PartitionSpec as P

SHIFTS = (-2, -1, 1, 2)
REACH = max(SHIFTS)
OWN, PAIR, FAR = 0, 1, 2
FEW = 4
BATCH = 6
VMEM = pl.BlockSpec(memory_space=pltpu.VMEM)
SMEM = pl.BlockSpec(memory_space=pltpu.SMEM)
ANY = pl.BlockSpec(memory_space=pl.ANY)


def halves(x):
    high = x.astype(jnp.bfloat16)
    return high, (x - high.astype(jnp.float32)).astype(jnp.bfloat16)


def swap(x, axis, first):
    low = range(first, lax.axis_size(axis) - 1, 2)
    return lax.ppermute(x, axis, [(i, i + 1) for i in low] + [(i + 1, i) for i in low])


def exchange(x, partner, spare):
    energies, atoms = lax.axis_size("energy"), lax.axis_size("atom")
    perm = []
    for e in range(energies):
        for a in range(atoms):
            to_e, to_a = partner(e, a)
            if not (0 <= to_e < energies and 0 <= to_a < atoms):
                to_e, to_a = spare(e, a)
            if 0 <= to_e < energies and 0 <= to_a < atoms:
                perm.append((e * atoms + a, to_e * atoms + to_a))
    return lax.ppermute(x, ("energy", "atom"), perm)


def cross_swap(x, step):
    return exchange(x, lambda e, a: (e + 1 if e % 2 else e - 1, a), lambda e, a: (e, a ^ step))


def forward(x, axis):
    size = lax.axis_size(axis)
    ups = [(i, min(i + 2, size - 1)) for i in range(0, size, 2)]
    downs = [(i, max(i - 2, 0)) for i in range(1, size, 2)]
    return lax.ppermute(x, axis, [(i, j) for i, j in ups + downs if i != j])


def put_blocks(blocks, c, green):
    orb = green.shape[-1]
    for e in range(green.shape[0]):
        for a in range(green.shape[1]):
            high, low = halves(green[e, a])
            blocks[c, a, e, :, :orb] = high
            blocks[c, a, e, :, orb:] = low


def add_pairs(group, neighbours, phonon, coupling, blocks, totals, picked, size):
    atoms, slots, orb = coupling.shape[0], coupling.shape[1], coupling.shape[-1]
    e_local = blocks.shape[2]
    index = lax.axis_index("atom")
    base = index * atoms
    if group != OWN:
        upper = (index & 1) == (0 if group == PAIR else 1)
        base += jnp.where(upper, atoms, -atoms)

    found = jnp.int32(0)
    for a in range(atoms):
        for j in range(slots):
            picked[found] = a * slots + j
            b = neighbours[a, j] - base
            found += ((b >= 0) & (b < atoms)).astype(jnp.int32)

    def batch(step, _):
        pairs = []
        for u in range(size):
            at = step * size + u
            item = picked[jnp.minimum(at, found - 1)]
            a = item // slots
            j = item - a * slots
            high, low = halves(coupling[a, j])
            left = jnp.concatenate([high, low], 1)
            right = jnp.concatenate(
                [jnp.concatenate([high, high], 1), jnp.concatenate([low, low], 1)], 0
            )
            pairs.append((a, j, neighbours[a, j] - base, jnp.where(at < found, 1.0, 0.0), left, right))
        inners = []
        for a, j, b, live, left, right in pairs:
            for c in range(len(totals)):
                near = blocks[c, b].reshape(e_local * orb, 2 * orb)
                inner = lax.dot_general(
                    near, right, (((1,), (1,)), ((), ())), preferred_element_type=jnp.float32
                )
                inners.append(inner[:, :orb] + inner[:, orb:])
        results = []
        for a, j, b, live, left, right in pairs:
            for total in totals:
                inner = inners.pop(0)
                sums = [None] * (e_local + 2 * REACH)
                for e in range(e_local):
                    high, low = halves(inner[e * orb : (e + 1) * orb])
                    both = jnp.concatenate([high, low], 1)
                    outer = jnp.dot(
                        left, jnp.concatenate([both, both], 0), preferred_element_type=jnp.float32
                    )
                    outer = outer[:, :orb] + outer[:, orb:]
                    for k, s in enumerate(SHIFTS):
                        d = e - s + REACH
                        term = (phonon[a, k, j] * live) * outer
                        sums[d] = term if sums[d] is None else sums[d] + term
                results.append((total, a, sums))
        for total, a, sums in results:
            for d, value in enumerate(sums):
                if value is not None:
                    total[d, a] += value

    lax.fori_loop(0, (found + size - 1) // size, batch, None)


def copy_all(sources, results, sems):
    copies = [
        pltpu.make_async_copy(source, result, sems.at[i])
        for i, (source, result) in enumerate(zip(sources, results))
    ]
    for copy in copies:
        copy.start()
    for copy in copies:
        copy.wait()


def part_kernel(green, part, sems):
    copy_all([green.at[0]], [part], sems)


def fetch_kernel(green, coupling, phonon, neighbours, *rest):
    copy_all([green.at[1], green, coupling, phonon, neighbours], rest[:-1], rest[-1])


def own_kernel(neighbours, phonon, coupling, green0, green1, total0, total1, blocks, picked):
    for c, (green, total) in enumerate(((green0, total0), (green1, total1))):
        put_blocks(blocks, c, green)
        total[...] = jnp.zeros_like(total)
    add_pairs(OWN, neighbours, phonon, coupling, blocks, (total0, total1), picked, 2)


def pair_kernel(neighbours, phonon, coupling, ahead, before, total, blocks, picked):
    total[...] = before[...]
    put_blocks(blocks, 0, ahead)
    add_pairs(PAIR, neighbours, phonon, coupling, blocks, (total,), picked, BATCH)


def turn_kernel(size, total0, green, by_core, by_cross, turned, partial):
    e_local, a_local = green.shape[1], green.shape[2]
    core, cross = partner_energies(turned.shape[1])
    has_core, has_cross = has_partners(size)
    for c in range(2):
        for a in range(a_local):
            for e in range(e_local):
                turned[c, REACH + e, a] = green[c, e, a].T
            for e in range(REACH):
                turned[c, core + e, a] = by_core[c, e, a].T * has_core
                turned[c, cross + e, a] = by_cross[c, e, a].T * has_cross
    for a in range(a_local):
        partial[a] = rate_sums(total0, turned, 0, a)


def partner_energies(spread):
    odd = lax.axis_index("energy") & 1
    return jnp.where(odd == 0, spread - REACH, 0), jnp.where(odd == 0, 0, spread - REACH)


def has_partners(size):
    me = lax.axis_index("energy")
    above, below = jnp.where(me < size - 1, 1.0, 0.0), jnp.where(me > 0, 1.0, 0.0)
    odd = me & 1
    return jnp.where(odd == 0, above, below), jnp.where(odd == 0, below, above)


def finish(total, core, cross):
    to_core, to_cross = partner_energies(total.shape[0])
    for e in range(REACH):
        core[e] = total[to_core + e]
        cross[e] = total[to_cross + e]


def rate_sums(total, turned, c, a):
    sums = total[0, a] * turned[c, 0, a]
    for d in range(1, total.shape[0]):
        sums += total[d, a] * turned[c, d, a]
    return sums


def far_kernel(neighbours, phonon, coupling, across, before, total, core, cross, blocks, picked):
    add_far(neighbours, phonon, coupling, across, before, total, blocks, picked)
    finish(total, core, cross)


def add_far(neighbours, phonon, coupling, across, before, total, blocks, picked):
    total[...] = before[...]
    put_blocks(blocks, 0, across)
    add_pairs(FAR, neighbours, phonon, coupling, blocks, (total,), picked, BATCH)


def last_kernel(
    scale, neighbours, phonon, coupling, across, before, turned, partial,
    total, core, cross, rate, blocks, picked,
):
    add_far(neighbours, phonon, coupling, across, before, total, blocks, picked)
    finish(total, core, cross)
    for a in range(partial.shape[0]):
        sums = partial[a] - rate_sums(total, turned, 1, a)
        rate[a : a + 1, :] = jnp.sum(sums.T, axis=0, keepdims=True) * scale


def addends(x, axis):
    size = lax.axis_size(axis)
    if size > FEW:
        return [lax.psum(x, axis)]
    turns = [[(i, (i + k) % size) for i in range(size)] for k in range(1, size)]
    return [x] + [lax.ppermute(x, axis, turn) for turn in turns]


def end_kernel(size, total0, total1, cross0, core0, cross1, core1, *rest):
    *rates, out, rate = rest
    e_local = out.shape[1]
    has_core, has_cross = has_partners(size)
    for c, (total, cross, core) in enumerate(((total0, cross0, core0), (total1, cross1, core1))):
        for e in range(e_local):
            out[c, e] = total[REACH + e] + core[e] * has_core + cross[e] * has_cross
    rate[...] = sum(r[...] for r in rates)


def per_device(green, coupling, phonon, neighbours):
    _, e_local, a_local, orb, _ = green.shape
    energies = lax.axis_size("energy")
    points = e_local * energies
    spread = (e_local + 2 * REACH, a_local, orb, orb)
    edge = (REACH, a_local, orb, orb)

    def call(kernel, out, operands, parts=1):
        return pl.pallas_call(
            kernel,
            out_shape=[jax.ShapeDtypeStruct(shape, jnp.float32) for shape in out],
            in_specs=[SMEM, SMEM] + [VMEM] * (1 + len(operands)),
            out_specs=[VMEM] * len(out),
            scratch_shapes=[
                pltpu.VMEM((parts, a_local, e_local, orb, 2 * orb), jnp.bfloat16),
                pltpu.SMEM((a_local * neighbours.shape[1] + 1,), jnp.int32),
            ],
            compiler_params=pltpu.CompilerParams(vmem_limit_bytes=24 * 2**20),
            cost_estimate=pl.CostEstimate(flops=10**6, bytes_accessed=10**4, transcendentals=0),
        )(neighbours, phonon, coupling, *operands)

    def fetch(kernel, out, sources):
        return pl.pallas_call(
            kernel,
            out_shape=[jax.ShapeDtypeStruct(x.shape, x.dtype) for x in out],
            in_specs=[ANY] * len(sources),
            out_specs=[VMEM] * len(out),
            scratch_shapes=[pltpu.SemaphoreType.DMA((len(out),))],
            compiler_params=pltpu.CompilerParams(vmem_limit_bytes=24 * 2**20),
        )(*(pltpu.with_memory_space_constraint(x, pltpu.HBM) for x in sources))

    sources = (green, coupling, jnp.swapaxes(phonon, 1, 2), neighbours)
    part = jax.ShapeDtypeStruct(green.shape[1:], green.dtype)
    (green0,) = fetch(part_kernel, [part], [green])
    green0, *sources = lax.optimization_barrier((green0, *sources))
    green1, green, coupling, phonon, neighbours = fetch(fetch_kernel, [part, *sources], sources)
    ahead1 = swap(green1, "atom", 0)
    ahead0 = swap(green0, "atom", 0)
    by_core, by_cross = swap(green, "energy", 0), cross_swap(green, 2)
    total0, total1 = call(own_kernel, [spread] * 2, (green0, green1), parts=2)
    ahead0, total0, total1 = lax.optimization_barrier((ahead0, total0, total1))
    across0 = forward(ahead0, "atom")
    (total0,) = call(pair_kernel, [spread], (ahead0, total0))
    green1, total0 = lax.optimization_barrier((green1, total0))
    across1 = swap(green1, "atom", 1)
    (total1,) = call(pair_kernel, [spread], (ahead1, total1))
    total0, total1 = lax.optimization_barrier((total0, total1))
    total0, core0, cross0 = call(far_kernel, [spread, edge, edge], (across0, total0))
    core0, cross0 = swap(core0, "energy", 0), cross_swap(cross0, 2)
    turned, partial = pl.pallas_call(
        functools.partial(turn_kernel, energies),
        out_shape=[
            jax.ShapeDtypeStruct((2,) + spread, jnp.float32),
            jax.ShapeDtypeStruct((a_local, orb, orb), jnp.float32),
        ],
        in_specs=[VMEM] * 4,
        out_specs=[VMEM] * 2,
        compiler_params=pltpu.CompilerParams(vmem_limit_bytes=24 * 2**20),
        cost_estimate=pl.CostEstimate(flops=10**6, bytes_accessed=10**4, transcendentals=0),
    )(total0, green, by_core, by_cross)
    total1, core1, cross1, rate = call(
        functools.partial(last_kernel, 1.0 / (4.0 * points)),
        [spread, edge, edge, (a_local, orb)],
        (across1, total1, turned, partial),
    )
    core1, cross1 = swap(core1, "energy", 0), cross_swap(cross1, 1)
    cross0, core0, rate = lax.optimization_barrier((cross0, core0, rate))
    rates = addends(rate, "energy")
    return pl.pallas_call(
        functools.partial(end_kernel, energies),
        out_shape=[
            jax.ShapeDtypeStruct(green.shape, jnp.float32),
            jax.ShapeDtypeStruct((a_local, orb), jnp.float32),
        ],
        in_specs=[VMEM] * (6 + len(rates)),
        out_specs=[VMEM] * 2,
        compiler_params=pltpu.CompilerParams(vmem_limit_bytes=24 * 2**20),
        cost_estimate=pl.CostEstimate(flops=10**6, bytes_accessed=2 * 10**6, transcendentals=0),
    )(total0, total1, cross0, core0, cross1, core1, *rates)


def solution(mesh):
    return jax.shard_map(
        per_device,
        mesh=mesh,
        in_specs=(
            P(None, "energy", "atom", None, None),
            P("atom", None, None, None),
            P("atom", None, None),
            P("atom", None),
        ),
        out_specs=(P(None, "energy", "atom", None, None), P("atom", None)),
        check_vma=False,
    )
```

```python
import functools

import jax
import jax.numpy as jnp
from jax import lax
from jax.experimental import pallas as pl
from jax.experimental.pallas import tpu as pltpu
from jax.sharding import PartitionSpec as P

SHIFTS = (-2, -1, 1, 2)
REACH = max(SHIFTS)
OWN, PAIR, FAR = 0, 1, 2
FEW = 4
BATCH = 6
VMEM = pl.BlockSpec(memory_space=pltpu.VMEM)
SMEM = pl.BlockSpec(memory_space=pltpu.SMEM)
ANY = pl.BlockSpec(memory_space=pl.ANY)


def halves(x):
    high = x.astype(jnp.bfloat16)
    return high, (x - high.astype(jnp.float32)).astype(jnp.bfloat16)


def swap(x, axis, first):
    low = range(first, lax.axis_size(axis) - 1, 2)
    return lax.ppermute(x, axis, [(i, i + 1) for i in low] + [(i + 1, i) for i in low])


def exchange(x, partner, spare):
    energies, atoms = lax.axis_size("energy"), lax.axis_size("atom")
    perm = []
    for e in range(energies):
        for a in range(atoms):
            to_e, to_a = partner(e, a)
            if not (0 <= to_e < energies and 0 <= to_a < atoms):
                to_e, to_a = spare(e, a)
            if 0 <= to_e < energies and 0 <= to_a < atoms:
                perm.append((e * atoms + a, to_e * atoms + to_a))
    return lax.ppermute(x, ("energy", "atom"), perm)


def cross_swap(x, step):
    return exchange(x, lambda e, a: (e + 1 if e % 2 else e - 1, a), lambda e, a: (e, a ^ step))


def forward(x, axis):
    size = lax.axis_size(axis)
    ups = [(i, min(i + 2, size - 1)) for i in range(0, size, 2)]
    downs = [(i, max(i - 2, 0)) for i in range(1, size, 2)]
    return lax.ppermute(x, axis, [(i, j) for i, j in ups + downs if i != j])


def put_blocks(blocks, c, green):
    orb = green.shape[-1]
    for e in range(green.shape[0]):
        for a in range(green.shape[1]):
            high, low = halves(green[e, a])
            blocks[c, a, e, :, :orb] = high
            blocks[c, a, e, :, orb:] = low


def add_pairs(group, neighbours, phonon, coupling, blocks, totals, picked, size):
    atoms, slots, orb = coupling.shape[0], coupling.shape[1], coupling.shape[-1]
    e_local = blocks.shape[2]
    index = lax.axis_index("atom")
    base = index * atoms
    if group != OWN:
        upper = (index & 1) == (0 if group == PAIR else 1)
        base += jnp.where(upper, atoms, -atoms)

    found = jnp.int32(0)
    for a in range(atoms):
        for j in range(slots):
            picked[found] = a * slots + j
            b = neighbours[a, j] - base
            found += ((b >= 0) & (b < atoms)).astype(jnp.int32)

    def batch(step, _):
        pairs = []
        for u in range(size):
            at = step * size + u
            item = picked[jnp.minimum(at, found - 1)]
            a = item // slots
            j = item - a * slots
            high, low = halves(coupling[a, j])
            left = jnp.concatenate([high, low], 1)
            right = jnp.concatenate(
                [jnp.concatenate([high, high], 1), jnp.concatenate([low, low], 1)], 0
            )
            pairs.append((a, j, neighbours[a, j] - base, jnp.where(at < found, 1.0, 0.0), left, right))
        inners = []
        for a, j, b, live, left, right in pairs:
            for c in range(len(totals)):
                near = blocks[c, b].reshape(e_local * orb, 2 * orb)
                inner = lax.dot_general(
                    near, right, (((1,), (1,)), ((), ())), preferred_element_type=jnp.float32
                )
                inners.append(inner[:, :orb] + inner[:, orb:])
        results = []
        for a, j, b, live, left, right in pairs:
            for total in totals:
                inner = inners.pop(0)
                sums = [None] * (e_local + 2 * REACH)
                for e in range(e_local):
                    high, low = halves(inner[e * orb : (e + 1) * orb])
                    both = jnp.concatenate([high, low], 1)
                    outer = jnp.dot(
                        left, jnp.concatenate([both, both], 0), preferred_element_type=jnp.float32
                    )
                    outer = outer[:, :orb] + outer[:, orb:]
                    for k, s in enumerate(SHIFTS):
                        d = e - s + REACH
                        term = (phonon[a, k, j] * live) * outer
                        sums[d] = term if sums[d] is None else sums[d] + term
                results.append((total, a, sums))
        for total, a, sums in results:
            for d, value in enumerate(sums):
                if value is not None:
                    total[d, a] += value

    lax.fori_loop(0, (found + size - 1) // size, batch, None)


def copy_all(sources, results, sems):
    copies = [
        pltpu.make_async_copy(source, result, sems.at[i])
        for i, (source, result) in enumerate(zip(sources, results))
    ]
    for copy in copies:
        copy.start()
    for copy in copies:
        copy.wait()


def part_kernel(green, part, sems):
    copy_all([green.at[0]], [part], sems)


def fetch_kernel(green, coupling, phonon, neighbours, *rest):
    copy_all([green.at[1], green, coupling, phonon, neighbours], rest[:-1], rest[-1])


def own_kernel(neighbours, phonon, coupling, green0, green1, total0, total1, blocks, picked):
    for c, (green, total) in enumerate(((green0, total0), (green1, total1))):
        put_blocks(blocks, c, green)
        total[...] = jnp.zeros_like(total)
    add_pairs(OWN, neighbours, phonon, coupling, blocks, (total0, total1), picked, 2)


def pair_kernel(neighbours, phonon, coupling, ahead, before, total, blocks, picked):
    total[...] = before[...]
    put_blocks(blocks, 0, ahead)
    add_pairs(PAIR, neighbours, phonon, coupling, blocks, (total,), picked, BATCH)


def turn_kernel(size, total0, green, by_core, by_cross, turned, partial):
    e_local, a_local = green.shape[1], green.shape[2]
    core, cross = partner_energies(turned.shape[1])
    has_core, has_cross = has_partners(size)
    for c in range(2):
        for a in range(a_local):
            for e in range(e_local):
                turned[c, REACH + e, a] = green[c, e, a].T
            for e in range(REACH):
                turned[c, core + e, a] = by_core[c, e, a].T * has_core
                turned[c, cross + e, a] = by_cross[c, e, a].T * has_cross
    for a in range(a_local):
        partial[a] = rate_sums(total0, turned, 0, a)


def partner_energies(spread):
    odd = lax.axis_index("energy") & 1
    return jnp.where(odd == 0, spread - REACH, 0), jnp.where(odd == 0, 0, spread - REACH)


def has_partners(size):
    me = lax.axis_index("energy")
    above, below = jnp.where(me < size - 1, 1.0, 0.0), jnp.where(me > 0, 1.0, 0.0)
    odd = me & 1
    return jnp.where(odd == 0, above, below), jnp.where(odd == 0, below, above)


def finish(total, core, cross):
    to_core, to_cross = partner_energies(total.shape[0])
    for e in range(REACH):
        core[e] = total[to_core + e]
        cross[e] = total[to_cross + e]


def rate_sums(total, turned, c, a):
    sums = total[0, a] * turned[c, 0, a]
    for d in range(1, total.shape[0]):
        sums += total[d, a] * turned[c, d, a]
    return sums


def far_kernel(neighbours, phonon, coupling, across, before, total, core, cross, blocks, picked):
    add_far(neighbours, phonon, coupling, across, before, total, blocks, picked)
    finish(total, core, cross)


def add_far(neighbours, phonon, coupling, across, before, total, blocks, picked):
    total[...] = before[...]
    put_blocks(blocks, 0, across)
    add_pairs(FAR, neighbours, phonon, coupling, blocks, (total,), picked, BATCH)


def last_kernel(
    scale, neighbours, phonon, coupling, across, before, turned, partial,
    total, core, cross, rate, blocks, picked,
):
    add_far(neighbours, phonon, coupling, across, before, total, blocks, picked)
    finish(total, core, cross)
    for a in range(partial.shape[0]):
        sums = partial[a] - rate_sums(total, turned, 1, a)
        rate[a : a + 1, :] = jnp.sum(sums.T, axis=0, keepdims=True) * scale


def addends(x, axis):
    size = lax.axis_size(axis)
    if size > FEW:
        return [lax.psum(x, axis)]
    if size & (size - 1):
        turns = [[(i, (i + k) % size) for i in range(size)] for k in range(1, size)]
    else:
        turns = [[(i, i ^ k) for i in range(size)] for k in range(1, size)]
    return [x] + [lax.ppermute(x, axis, turn) for turn in turns]


def end_kernel(size, total0, total1, cross0, core0, cross1, core1, *rest):
    *rates, out, rate = rest
    e_local = out.shape[1]
    has_core, has_cross = has_partners(size)
    for c, (total, cross, core) in enumerate(((total0, cross0, core0), (total1, cross1, core1))):
        for e in range(e_local):
            out[c, e] = total[REACH + e] + core[e] * has_core + cross[e] * has_cross
    rate[...] = sum(r[...] for r in rates)


def per_device(green, coupling, phonon, neighbours):
    _, e_local, a_local, orb, _ = green.shape
    energies = lax.axis_size("energy")
    points = e_local * energies
    spread = (e_local + 2 * REACH, a_local, orb, orb)
    edge = (REACH, a_local, orb, orb)

    def call(kernel, out, operands, parts=1):
        return pl.pallas_call(
            kernel,
            out_shape=[jax.ShapeDtypeStruct(shape, jnp.float32) for shape in out],
            in_specs=[SMEM, SMEM] + [VMEM] * (1 + len(operands)),
            out_specs=[VMEM] * len(out),
            scratch_shapes=[
                pltpu.VMEM((parts, a_local, e_local, orb, 2 * orb), jnp.bfloat16),
                pltpu.SMEM((a_local * neighbours.shape[1] + 1,), jnp.int32),
            ],
            compiler_params=pltpu.CompilerParams(vmem_limit_bytes=24 * 2**20),
            cost_estimate=pl.CostEstimate(flops=10**6, bytes_accessed=10**4, transcendentals=0),
        )(neighbours, phonon, coupling, *operands)

    def fetch(kernel, out, sources):
        return pl.pallas_call(
            kernel,
            out_shape=[jax.ShapeDtypeStruct(x.shape, x.dtype) for x in out],
            in_specs=[ANY] * len(sources),
            out_specs=[VMEM] * len(out),
            scratch_shapes=[pltpu.SemaphoreType.DMA((len(out),))],
            compiler_params=pltpu.CompilerParams(vmem_limit_bytes=24 * 2**20),
        )(*(pltpu.with_memory_space_constraint(x, pltpu.HBM) for x in sources))

    sources = (green, coupling, jnp.swapaxes(phonon, 1, 2), neighbours)
    part = jax.ShapeDtypeStruct(green.shape[1:], green.dtype)
    (green0,) = fetch(part_kernel, [part], [green])
    green0, *sources = lax.optimization_barrier((green0, *sources))
    green1, green, coupling, phonon, neighbours = fetch(fetch_kernel, [part, *sources], sources)
    ahead1 = swap(green1, "atom", 0)
    ahead0 = swap(green0, "atom", 0)
    by_core, by_cross = swap(green, "energy", 0), cross_swap(green, 2)
    total0, total1 = call(own_kernel, [spread] * 2, (green0, green1), parts=2)
    ahead0, total0, total1 = lax.optimization_barrier((ahead0, total0, total1))
    across0 = forward(ahead0, "atom")
    (total0,) = call(pair_kernel, [spread], (ahead0, total0))
    green1, total0 = lax.optimization_barrier((green1, total0))
    across1 = swap(green1, "atom", 1)
    (total1,) = call(pair_kernel, [spread], (ahead1, total1))
    total0, total1 = lax.optimization_barrier((total0, total1))
    total0, core0, cross0 = call(far_kernel, [spread, edge, edge], (across0, total0))
    core0, cross0 = swap(core0, "energy", 0), cross_swap(cross0, 2)
    turned, partial = pl.pallas_call(
        functools.partial(turn_kernel, energies),
        out_shape=[
            jax.ShapeDtypeStruct((2,) + spread, jnp.float32),
            jax.ShapeDtypeStruct((a_local, orb, orb), jnp.float32),
        ],
        in_specs=[VMEM] * 4,
        out_specs=[VMEM] * 2,
        compiler_params=pltpu.CompilerParams(vmem_limit_bytes=24 * 2**20),
        cost_estimate=pl.CostEstimate(flops=10**6, bytes_accessed=10**4, transcendentals=0),
    )(total0, green, by_core, by_cross)
    total1, core1, cross1, rate = call(
        functools.partial(last_kernel, 1.0 / (4.0 * points)),
        [spread, edge, edge, (a_local, orb)],
        (across1, total1, turned, partial),
    )
    core1, cross1 = swap(core1, "energy", 0), cross_swap(cross1, 1)
    cross0, core0, rate = lax.optimization_barrier((cross0, core0, rate))
    rates = addends(rate, "energy")
    return pl.pallas_call(
        functools.partial(end_kernel, energies),
        out_shape=[
            jax.ShapeDtypeStruct(green.shape, jnp.float32),
            jax.ShapeDtypeStruct((a_local, orb), jnp.float32),
        ],
        in_specs=[VMEM] * (6 + len(rates)),
        out_specs=[VMEM] * 2,
        compiler_params=pltpu.CompilerParams(vmem_limit_bytes=24 * 2**20),
        cost_estimate=pl.CostEstimate(flops=10**6, bytes_accessed=2 * 10**6, transcendentals=0),
    )(total0, total1, cross0, core0, cross1, core1, *rates)


def solution(mesh):
    return jax.shard_map(
        per_device,
        mesh=mesh,
        in_specs=(
            P(None, "energy", "atom", None, None),
            P("atom", None, None, None),
            P("atom", None, None),
            P("atom", None),
        ),
        out_specs=(P(None, "energy", "atom", None, None), P("atom", None)),
        check_vma=False,
    )
```

```python
import functools

import jax
import jax.numpy as jnp
from jax import lax
from jax.experimental import pallas as pl
from jax.experimental.pallas import tpu as pltpu
from jax.sharding import PartitionSpec as P

SHIFTS = (-2, -1, 1, 2)
REACH = max(SHIFTS)
OWN, PAIR, FAR = 0, 1, 2
FEW = 4
BATCH = 6
VMEM = pl.BlockSpec(memory_space=pltpu.VMEM)
SMEM = pl.BlockSpec(memory_space=pltpu.SMEM)
ANY = pl.BlockSpec(memory_space=pl.ANY)


def halves(x):
    high = x.astype(jnp.bfloat16)
    return high, (x - high.astype(jnp.float32)).astype(jnp.bfloat16)


def swap(x, axis, first):
    low = range(first, lax.axis_size(axis) - 1, 2)
    return lax.ppermute(x, axis, [(i, i + 1) for i in low] + [(i + 1, i) for i in low])


def exchange(x, partner, spare):
    energies, atoms = lax.axis_size("energy"), lax.axis_size("atom")
    perm = []
    for e in range(energies):
        for a in range(atoms):
            to_e, to_a = partner(e, a)
            if not (0 <= to_e < energies and 0 <= to_a < atoms):
                to_e, to_a = spare(e, a)
            if 0 <= to_e < energies and 0 <= to_a < atoms:
                perm.append((e * atoms + a, to_e * atoms + to_a))
    return lax.ppermute(x, ("energy", "atom"), perm)


def cross_swap(x, low_step, high_step):
    half = lax.axis_size("atom") // 2
    if half % 4:
        low_step = high_step = 1

    def spare(e, a):
        return e, a ^ (low_step if a < half else high_step)

    return exchange(x, lambda e, a: (e + 1 if e % 2 else e - 1, a), spare)


def forward(x, axis):
    size = lax.axis_size(axis)
    ups = [(i, min(i + 2, size - 1)) for i in range(0, size, 2)]
    downs = [(i, max(i - 2, 0)) for i in range(1, size, 2)]
    return lax.ppermute(x, axis, [(i, j) for i, j in ups + downs if i != j])


def put_blocks(blocks, c, green):
    orb = green.shape[-1]
    for e in range(green.shape[0]):
        for a in range(green.shape[1]):
            high, low = halves(green[e, a])
            blocks[c, a, e, :, :orb] = high
            blocks[c, a, e, :, orb:] = low


def add_pairs(group, neighbours, phonon, coupling, blocks, totals, picked, size):
    atoms, slots, orb = coupling.shape[0], coupling.shape[1], coupling.shape[-1]
    e_local = blocks.shape[2]
    index = lax.axis_index("atom")
    base = index * atoms
    if group != OWN:
        upper = (index & 1) == (0 if group == PAIR else 1)
        base += jnp.where(upper, atoms, -atoms)

    found = jnp.int32(0)
    for a in range(atoms):
        for j in range(slots):
            picked[found] = a * slots + j
            b = neighbours[a, j] - base
            found += ((b >= 0) & (b < atoms)).astype(jnp.int32)

    def batch(step, _):
        pairs = []
        for u in range(size):
            at = step * size + u
            item = picked[jnp.minimum(at, found - 1)]
            a = item // slots
            j = item - a * slots
            high, low = halves(coupling[a, j])
            left = jnp.concatenate([high, low], 1)
            right = jnp.concatenate(
                [jnp.concatenate([high, high], 1), jnp.concatenate([low, low], 1)], 0
            )
            pairs.append((a, j, neighbours[a, j] - base, jnp.where(at < found, 1.0, 0.0), left, right))
        inners = []
        for a, j, b, live, left, right in pairs:
            for c in range(len(totals)):
                near = blocks[c, b].reshape(e_local * orb, 2 * orb)
                inner = lax.dot_general(
                    near, right, (((1,), (1,)), ((), ())), preferred_element_type=jnp.float32
                )
                inners.append(inner[:, :orb] + inner[:, orb:])
        results = []
        for a, j, b, live, left, right in pairs:
            for total in totals:
                inner = inners.pop(0)
                sums = [None] * (e_local + 2 * REACH)
                for e in range(e_local):
                    high, low = halves(inner[e * orb : (e + 1) * orb])
                    both = jnp.concatenate([high, low], 1)
                    outer = jnp.dot(
                        left, jnp.concatenate([both, both], 0), preferred_element_type=jnp.float32
                    )
                    outer = outer[:, :orb] + outer[:, orb:]
                    for k, s in enumerate(SHIFTS):
                        d = e - s + REACH
                        term = (phonon[a, k, j] * live) * outer
                        sums[d] = term if sums[d] is None else sums[d] + term
                results.append((total, a, sums))
        for total, a, sums in results:
            for d, value in enumerate(sums):
                if value is not None:
                    total[d, a] += value

    lax.fori_loop(0, (found + size - 1) // size, batch, None)


def copy_all(sources, results, sems):
    copies = [
        pltpu.make_async_copy(source, result, sems.at[i])
        for i, (source, result) in enumerate(zip(sources, results))
    ]
    for copy in copies:
        copy.start()
    for copy in copies:
        copy.wait()


def part_kernel(green, part, sems):
    copy_all([green.at[0]], [part], sems)


def fetch_kernel(green, coupling, phonon, neighbours, *rest):
    copy_all([green.at[1], green, coupling, phonon, neighbours], rest[:-1], rest[-1])


def own_kernel(neighbours, phonon, coupling, green0, green1, total0, total1, blocks, picked):
    for c, (green, total) in enumerate(((green0, total0), (green1, total1))):
        put_blocks(blocks, c, green)
        total[...] = jnp.zeros_like(total)
    add_pairs(OWN, neighbours, phonon, coupling, blocks, (total0, total1), picked, 2)


def pair_kernel(neighbours, phonon, coupling, ahead, before, total, blocks, picked):
    total[...] = before[...]
    put_blocks(blocks, 0, ahead)
    add_pairs(PAIR, neighbours, phonon, coupling, blocks, (total,), picked, BATCH)


def turn_kernel(size, total0, green, by_core, by_cross, turned, partial):
    e_local, a_local = green.shape[1], green.shape[2]
    core, cross = partner_energies(turned.shape[1])
    has_core, has_cross = has_partners(size)
    for c in range(2):
        for a in range(a_local):
            for e in range(e_local):
                turned[c, REACH + e, a] = green[c, e, a].T
            for e in range(REACH):
                turned[c, core + e, a] = by_core[c, e, a].T * has_core
                turned[c, cross + e, a] = by_cross[c, e, a].T * has_cross
    for a in range(a_local):
        partial[a] = rate_sums(total0, turned, 0, a)


def partner_energies(spread):
    odd = lax.axis_index("energy") & 1
    return jnp.where(odd == 0, spread - REACH, 0), jnp.where(odd == 0, 0, spread - REACH)


def has_partners(size):
    me = lax.axis_index("energy")
    above, below = jnp.where(me < size - 1, 1.0, 0.0), jnp.where(me > 0, 1.0, 0.0)
    odd = me & 1
    return jnp.where(odd == 0, above, below), jnp.where(odd == 0, below, above)


def finish(total, core, cross):
    to_core, to_cross = partner_energies(total.shape[0])
    for e in range(REACH):
        core[e] = total[to_core + e]
        cross[e] = total[to_cross + e]


def rate_sums(total, turned, c, a):
    sums = total[0, a] * turned[c, 0, a]
    for d in range(1, total.shape[0]):
        sums += total[d, a] * turned[c, d, a]
    return sums


def far_kernel(neighbours, phonon, coupling, across, before, total, core, cross, blocks, picked):
    add_far(neighbours, phonon, coupling, across, before, total, blocks, picked)
    finish(total, core, cross)


def add_far(neighbours, phonon, coupling, across, before, total, blocks, picked):
    total[...] = before[...]
    put_blocks(blocks, 0, across)
    add_pairs(FAR, neighbours, phonon, coupling, blocks, (total,), picked, BATCH)


def last_kernel(
    scale, neighbours, phonon, coupling, across, before, turned, partial,
    total, core, cross, rate, blocks, picked,
):
    add_far(neighbours, phonon, coupling, across, before, total, blocks, picked)
    finish(total, core, cross)
    for a in range(partial.shape[0]):
        sums = partial[a] - rate_sums(total, turned, 1, a)
        rate[a : a + 1, :] = jnp.sum(sums.T, axis=0, keepdims=True) * scale


def addends(x, axis):
    size = lax.axis_size(axis)
    if size > FEW:
        return [lax.psum(x, axis)]
    if size & (size - 1):
        turns = [[(i, (i + k) % size) for i in range(size)] for k in range(1, size)]
    else:
        turns = [[(i, i ^ k) for i in range(size)] for k in range(1, size)]
    return [x] + [lax.ppermute(x, axis, turn) for turn in turns]


def end_kernel(size, total0, total1, cross0, core0, cross1, core1, *rest):
    *rates, out, rate = rest
    e_local = out.shape[1]
    has_core, has_cross = has_partners(size)
    for c, (total, cross, core) in enumerate(((total0, cross0, core0), (total1, cross1, core1))):
        for e in range(e_local):
            out[c, e] = total[REACH + e] + core[e] * has_core + cross[e] * has_cross
    rate[...] = sum(r[...] for r in rates)


def per_device(green, coupling, phonon, neighbours):
    _, e_local, a_local, orb, _ = green.shape
    energies = lax.axis_size("energy")
    points = e_local * energies
    spread = (e_local + 2 * REACH, a_local, orb, orb)
    edge = (REACH, a_local, orb, orb)

    def call(kernel, out, operands, parts=1):
        return pl.pallas_call(
            kernel,
            out_shape=[jax.ShapeDtypeStruct(shape, jnp.float32) for shape in out],
            in_specs=[SMEM, SMEM] + [VMEM] * (1 + len(operands)),
            out_specs=[VMEM] * len(out),
            scratch_shapes=[
                pltpu.VMEM((parts, a_local, e_local, orb, 2 * orb), jnp.bfloat16),
                pltpu.SMEM((a_local * neighbours.shape[1] + 1,), jnp.int32),
            ],
            compiler_params=pltpu.CompilerParams(vmem_limit_bytes=24 * 2**20),
            cost_estimate=pl.CostEstimate(flops=10**6, bytes_accessed=10**4, transcendentals=0),
        )(neighbours, phonon, coupling, *operands)

    def fetch(kernel, out, sources):
        return pl.pallas_call(
            kernel,
            out_shape=[jax.ShapeDtypeStruct(x.shape, x.dtype) for x in out],
            in_specs=[ANY] * len(sources),
            out_specs=[VMEM] * len(out),
            scratch_shapes=[pltpu.SemaphoreType.DMA((len(out),))],
            compiler_params=pltpu.CompilerParams(vmem_limit_bytes=24 * 2**20),
        )(*(pltpu.with_memory_space_constraint(x, pltpu.HBM) for x in sources))

    sources = (green, coupling, jnp.swapaxes(phonon, 1, 2), neighbours)
    part = jax.ShapeDtypeStruct(green.shape[1:], green.dtype)
    (green0,) = fetch(part_kernel, [part], [green])
    green0, *sources = lax.optimization_barrier((green0, *sources))
    green1, green, coupling, phonon, neighbours = fetch(fetch_kernel, [part, *sources], sources)
    ahead1 = swap(green1, "atom", 0)
    ahead0 = swap(green0, "atom", 0)
    by_core, by_cross = swap(green, "energy", 0), cross_swap(green, 2, 2)
    total0, total1 = call(own_kernel, [spread] * 2, (green0, green1), parts=2)
    ahead0, total0, total1 = lax.optimization_barrier((ahead0, total0, total1))
    across0 = forward(ahead0, "atom")
    (total0,) = call(pair_kernel, [spread], (ahead0, total0))
    green1, total0 = lax.optimization_barrier((green1, total0))
    across1 = swap(green1, "atom", 1)
    (total1,) = call(pair_kernel, [spread], (ahead1, total1))
    total0, total1 = lax.optimization_barrier((total0, total1))
    total0, core0, cross0 = call(far_kernel, [spread, edge, edge], (across0, total0))
    core0, cross0 = swap(core0, "energy", 0), cross_swap(cross0, 2, 2)
    turned, partial = pl.pallas_call(
        functools.partial(turn_kernel, energies),
        out_shape=[
            jax.ShapeDtypeStruct((2,) + spread, jnp.float32),
            jax.ShapeDtypeStruct((a_local, orb, orb), jnp.float32),
        ],
        in_specs=[VMEM] * 4,
        out_specs=[VMEM] * 2,
        compiler_params=pltpu.CompilerParams(vmem_limit_bytes=24 * 2**20),
        cost_estimate=pl.CostEstimate(flops=10**6, bytes_accessed=10**4, transcendentals=0),
    )(total0, green, by_core, by_cross)
    total1, core1, cross1, rate = call(
        functools.partial(last_kernel, 1.0 / (4.0 * points)),
        [spread, edge, edge, (a_local, orb)],
        (across1, total1, turned, partial),
    )
    core1, cross1 = swap(core1, "energy", 0), cross_swap(cross1, 2, 1)
    cross0, core0, rate = lax.optimization_barrier((cross0, core0, rate))
    rates = addends(rate, "energy")
    return pl.pallas_call(
        functools.partial(end_kernel, energies),
        out_shape=[
            jax.ShapeDtypeStruct(green.shape, jnp.float32),
            jax.ShapeDtypeStruct((a_local, orb), jnp.float32),
        ],
        in_specs=[VMEM] * (6 + len(rates)),
        out_specs=[VMEM] * 2,
        compiler_params=pltpu.CompilerParams(vmem_limit_bytes=24 * 2**20),
        cost_estimate=pl.CostEstimate(flops=10**6, bytes_accessed=2 * 10**6, transcendentals=0),
    )(total0, total1, cross0, core0, cross1, core1, *rates)


def solution(mesh):
    return jax.shard_map(
        per_device,
        mesh=mesh,
        in_specs=(
            P(None, "energy", "atom", None, None),
            P("atom", None, None, None),
            P("atom", None, None),
            P("atom", None),
        ),
        out_specs=(P(None, "energy", "atom", None, None), P("atom", None)),
        check_vma=False,
    )
```

```python
import functools

import jax
import jax.numpy as jnp
from jax import lax
from jax.experimental import pallas as pl
from jax.experimental.pallas import tpu as pltpu
from jax.sharding import PartitionSpec as P

SHIFTS = (-2, -1, 1, 2)
REACH = max(SHIFTS)
OWN, PAIR, FAR = 0, 1, 2
FEW = 4
BATCH = 6
VMEM = pl.BlockSpec(memory_space=pltpu.VMEM)
SMEM = pl.BlockSpec(memory_space=pltpu.SMEM)
ANY = pl.BlockSpec(memory_space=pl.ANY)


def halves(x):
    high = x.astype(jnp.bfloat16)
    return high, (x - high.astype(jnp.float32)).astype(jnp.bfloat16)


def swap(x, axis, first):
    low = range(first, lax.axis_size(axis) - 1, 2)
    return lax.ppermute(x, axis, [(i, i + 1) for i in low] + [(i + 1, i) for i in low])


def exchange(x, partner, spare):
    energies, atoms = lax.axis_size("energy"), lax.axis_size("atom")
    perm = []
    for e in range(energies):
        for a in range(atoms):
            to_e, to_a = partner(e, a)
            if not (0 <= to_e < energies and 0 <= to_a < atoms):
                to_e, to_a = spare(e, a)
            if 0 <= to_e < energies and 0 <= to_a < atoms:
                perm.append((e * atoms + a, to_e * atoms + to_a))
    return lax.ppermute(x, ("energy", "atom"), perm)


def cross_swap(x, low_step, high_step):
    half = lax.axis_size("atom") // 2
    if half % 4:
        low_step = high_step = 1

    def spare(e, a):
        return e, a ^ (low_step if a < half else high_step)

    return exchange(x, lambda e, a: (e + 1 if e % 2 else e - 1, a), spare)


def forward(x, axis):
    size = lax.axis_size(axis)
    ups = [(i, min(i + 2, size - 1)) for i in range(0, size, 2)]
    downs = [(i, max(i - 2, 0)) for i in range(1, size, 2)]
    return lax.ppermute(x, axis, [(i, j) for i, j in ups + downs if i != j])


def put_blocks(blocks, c, green):
    orb = green.shape[-1]
    for e in range(green.shape[0]):
        for a in range(green.shape[1]):
            high, low = halves(green[e, a])
            blocks[c, a, e, :, :orb] = high
            blocks[c, a, e, :, orb:] = low


def add_pairs(group, neighbours, phonon, coupling, blocks, totals, picked, size):
    atoms, slots, orb = coupling.shape[0], coupling.shape[1], coupling.shape[-1]
    e_local = blocks.shape[2]
    index = lax.axis_index("atom")
    base = index * atoms
    if group != OWN:
        upper = (index & 1) == (0 if group == PAIR else 1)
        base += jnp.where(upper, atoms, -atoms)

    found = jnp.int32(0)
    for a in range(atoms):
        for j in range(slots):
            picked[found] = a * slots + j
            b = neighbours[a, j] - base
            found += ((b >= 0) & (b < atoms)).astype(jnp.int32)

    def batch(step, _):
        pairs = []
        for u in range(size):
            at = step * size + u
            item = picked[jnp.minimum(at, found - 1)]
            a = item // slots
            j = item - a * slots
            high, low = halves(coupling[a, j])
            left = jnp.concatenate([high, low], 1)
            right = jnp.concatenate(
                [jnp.concatenate([high, high], 1), jnp.concatenate([low, low], 1)], 0
            )
            pairs.append((a, j, neighbours[a, j] - base, jnp.where(at < found, 1.0, 0.0), left, right))
        inners = []
        for a, j, b, live, left, right in pairs:
            for c in range(len(totals)):
                near = blocks[c, b].reshape(e_local * orb, 2 * orb)
                inner = lax.dot_general(
                    near, right, (((1,), (1,)), ((), ())), preferred_element_type=jnp.float32
                )
                inners.append(inner[:, :orb] + inner[:, orb:])
        results = []
        for a, j, b, live, left, right in pairs:
            for total in totals:
                inner = inners.pop(0)
                sums = [None] * (e_local + 2 * REACH)
                for e in range(e_local):
                    high, low = halves(inner[e * orb : (e + 1) * orb])
                    both = jnp.concatenate([high, low], 1)
                    outer = jnp.dot(
                        left, jnp.concatenate([both, both], 0), preferred_element_type=jnp.float32
                    )
                    outer = outer[:, :orb] + outer[:, orb:]
                    for k, s in enumerate(SHIFTS):
                        d = e - s + REACH
                        term = (phonon[a, k, j] * live) * outer
                        sums[d] = term if sums[d] is None else sums[d] + term
                results.append((total, a, sums))
        for total, a, sums in results:
            for d, value in enumerate(sums):
                if value is not None:
                    total[d, a] += value

    lax.fori_loop(0, (found + size - 1) // size, batch, None)


def copy_all(sources, results, sems):
    copies = [
        pltpu.make_async_copy(source, result, sems.at[i])
        for i, (source, result) in enumerate(zip(sources, results))
    ]
    for copy in copies:
        copy.start()
    for copy in copies:
        copy.wait()


def part_kernel(green, part, sems):
    copy_all([green.at[0]], [part], sems)


def fetch_kernel(green, coupling, phonon, neighbours, *rest):
    copy_all([green.at[1], green, coupling, phonon, neighbours], rest[:-1], rest[-1])


def own_kernel(neighbours, phonon, coupling, green0, green1, total0, total1, blocks, picked):
    for c, (green, total) in enumerate(((green0, total0), (green1, total1))):
        put_blocks(blocks, c, green)
        total[...] = jnp.zeros_like(total)
    add_pairs(OWN, neighbours, phonon, coupling, blocks, (total0, total1), picked, 2)


def pair_kernel(neighbours, phonon, coupling, ahead, before, total, blocks, picked):
    total[...] = before[...]
    put_blocks(blocks, 0, ahead)
    add_pairs(PAIR, neighbours, phonon, coupling, blocks, (total,), picked, BATCH)


def turn_kernel(size, total0, green, by_core, by_cross, turned, partial):
    e_local, a_local = green.shape[1], green.shape[2]
    core, cross = partner_energies(turned.shape[1])
    has_core, has_cross = has_partners(size)
    for c in range(2):
        for a in range(a_local):
            for e in range(e_local):
                turned[c, REACH + e, a] = green[c, e, a].T
            for e in range(REACH):
                turned[c, core + e, a] = by_core[c, e, a].T * has_core
                turned[c, cross + e, a] = by_cross[c, e, a].T * has_cross
    for a in range(a_local):
        partial[a] = rate_sums(total0, turned, 0, a)


def partner_energies(spread):
    odd = lax.axis_index("energy") & 1
    return jnp.where(odd == 0, spread - REACH, 0), jnp.where(odd == 0, 0, spread - REACH)


def has_partners(size):
    me = lax.axis_index("energy")
    above, below = jnp.where(me < size - 1, 1.0, 0.0), jnp.where(me > 0, 1.0, 0.0)
    odd = me & 1
    return jnp.where(odd == 0, above, below), jnp.where(odd == 0, below, above)


def finish(total, core, cross):
    to_core, to_cross = partner_energies(total.shape[0])
    for e in range(REACH):
        core[e] = total[to_core + e]
        cross[e] = total[to_cross + e]


def rate_sums(total, turned, c, a):
    sums = total[0, a] * turned[c, 0, a]
    for d in range(1, total.shape[0]):
        sums += total[d, a] * turned[c, d, a]
    return sums


def far_kernel(neighbours, phonon, coupling, across, before, total, core, cross, blocks, picked):
    add_far(neighbours, phonon, coupling, across, before, total, blocks, picked)
    finish(total, core, cross)


def add_far(neighbours, phonon, coupling, across, before, total, blocks, picked):
    total[...] = before[...]
    put_blocks(blocks, 0, across)
    add_pairs(FAR, neighbours, phonon, coupling, blocks, (total,), picked, BATCH)


def last_kernel(
    scale, neighbours, phonon, coupling, across, before, turned, partial,
    total, core, cross, rate, blocks, picked,
):
    add_far(neighbours, phonon, coupling, across, before, total, blocks, picked)
    finish(total, core, cross)
    for a in range(partial.shape[0]):
        sums = partial[a] - rate_sums(total, turned, 1, a)
        rate[a : a + 1, :] = jnp.sum(sums.T, axis=0, keepdims=True) * scale


def addends(x, axis):
    size = lax.axis_size(axis)
    if size > FEW:
        return [lax.psum(x, axis)]
    if size & (size - 1):
        turns = [[(i, (i + k) % size) for i in range(size)] for k in range(1, size)]
    else:
        turns = [[(i, i ^ k) for i in range(size)] for k in range(1, size)]
    return [x] + [lax.ppermute(x, axis, turn) for turn in turns]


def end_kernel(size, total0, total1, cross0, core0, cross1, core1, *rest):
    *rates, out, rate = rest
    e_local = out.shape[1]
    has_core, has_cross = has_partners(size)
    for c, (total, cross, core) in enumerate(((total0, cross0, core0), (total1, cross1, core1))):
        for e in range(e_local):
            out[c, e] = total[REACH + e] + core[e] * has_core + cross[e] * has_cross
    rate[...] = sum(r[...] for r in rates)


def per_device(green, coupling, phonon, neighbours):
    _, e_local, a_local, orb, _ = green.shape
    energies = lax.axis_size("energy")
    points = e_local * energies
    spread = (e_local + 2 * REACH, a_local, orb, orb)
    edge = (REACH, a_local, orb, orb)

    def call(kernel, out, operands, parts=1):
        return pl.pallas_call(
            kernel,
            out_shape=[jax.ShapeDtypeStruct(shape, jnp.float32) for shape in out],
            in_specs=[SMEM, SMEM] + [VMEM] * (1 + len(operands)),
            out_specs=[VMEM] * len(out),
            scratch_shapes=[
                pltpu.VMEM((parts, a_local, e_local, orb, 2 * orb), jnp.bfloat16),
                pltpu.SMEM((a_local * neighbours.shape[1] + 1,), jnp.int32),
            ],
            compiler_params=pltpu.CompilerParams(vmem_limit_bytes=24 * 2**20),
            cost_estimate=pl.CostEstimate(flops=10**6, bytes_accessed=10**4, transcendentals=0),
        )(neighbours, phonon, coupling, *operands)

    def fetch(kernel, out, sources):
        return pl.pallas_call(
            kernel,
            out_shape=[jax.ShapeDtypeStruct(x.shape, x.dtype) for x in out],
            in_specs=[ANY] * len(sources),
            out_specs=[VMEM] * len(out),
            scratch_shapes=[pltpu.SemaphoreType.DMA((len(out),))],
            compiler_params=pltpu.CompilerParams(vmem_limit_bytes=24 * 2**20),
        )(*(pltpu.with_memory_space_constraint(x, pltpu.HBM) for x in sources))

    sources = (green, coupling, jnp.swapaxes(phonon, 1, 2), neighbours)
    part = jax.ShapeDtypeStruct(green.shape[1:], green.dtype)
    (green0,) = fetch(part_kernel, [part], [green])
    green0, *sources = lax.optimization_barrier((green0, *sources))
    green1, green, coupling, phonon, neighbours = fetch(fetch_kernel, [part, *sources], sources)
    ahead1 = swap(green1, "atom", 0)
    ahead0 = swap(green0, "atom", 0)
    by_core, by_cross = swap(green, "energy", 0), cross_swap(green, 2, 2)
    total0, total1 = call(own_kernel, [spread] * 2, (green0, green1), parts=2)
    ahead0, total0, total1 = lax.optimization_barrier((ahead0, total0, total1))
    across0 = forward(ahead0, "atom")
    (total0,) = call(pair_kernel, [spread], (ahead0, total0))
    green1, total0 = lax.optimization_barrier((green1, total0))
    across1 = swap(green1, "atom", 1)
    (total1,) = call(pair_kernel, [spread], (ahead1, total1))
    total0, total1 = lax.optimization_barrier((total0, total1))
    total0, core0, cross0 = call(far_kernel, [spread, edge, edge], (across0, total0))
    core0, cross0 = swap(core0, "energy", 0), cross_swap(cross0, 2, 2)
    turned, partial = pl.pallas_call(
        functools.partial(turn_kernel, energies),
        out_shape=[
            jax.ShapeDtypeStruct((2,) + spread, jnp.float32),
            jax.ShapeDtypeStruct((a_local, orb, orb), jnp.float32),
        ],
        in_specs=[VMEM] * 4,
        out_specs=[VMEM] * 2,
        compiler_params=pltpu.CompilerParams(vmem_limit_bytes=24 * 2**20),
        cost_estimate=pl.CostEstimate(flops=10**6, bytes_accessed=10**4, transcendentals=0),
    )(total0, green, by_core, by_cross)
    total1, core1, cross1, rate = call(
        functools.partial(last_kernel, 1.0 / (4.0 * points)),
        [spread, edge, edge, (a_local, orb)],
        (across1, total1, turned, partial),
    )
    core1, cross1 = swap(core1, "energy", 0), cross_swap(cross1, 2, 1)
    core0, cross0, rate = lax.optimization_barrier((core0, cross0, rate))
    rates = addends(rate, "energy")
    return pl.pallas_call(
        functools.partial(end_kernel, energies),
        out_shape=[
            jax.ShapeDtypeStruct(green.shape, jnp.float32),
            jax.ShapeDtypeStruct((a_local, orb), jnp.float32),
        ],
        in_specs=[VMEM] * (6 + len(rates)),
        out_specs=[VMEM] * 2,
        compiler_params=pltpu.CompilerParams(vmem_limit_bytes=24 * 2**20),
        cost_estimate=pl.CostEstimate(flops=10**6, bytes_accessed=2 * 10**6, transcendentals=0),
    )(total0, total1, cross0, core0, cross1, core1, *rates)


def solution(mesh):
    return jax.shard_map(
        per_device,
        mesh=mesh,
        in_specs=(
            P(None, "energy", "atom", None, None),
            P("atom", None, None, None),
            P("atom", None, None),
            P("atom", None),
        ),
        out_specs=(P(None, "energy", "atom", None, None), P("atom", None)),
        check_vma=False,
    )
```

```python
import functools

import jax
import jax.numpy as jnp
from jax import lax
from jax.experimental import pallas as pl
from jax.experimental.pallas import tpu as pltpu
from jax.sharding import PartitionSpec as P

SHIFTS = (-2, -1, 1, 2)
REACH = max(SHIFTS)
OWN, PAIR, FAR = 0, 1, 2
FEW = 4
BATCH = 6
VMEM = pl.BlockSpec(memory_space=pltpu.VMEM)
SMEM = pl.BlockSpec(memory_space=pltpu.SMEM)
ANY = pl.BlockSpec(memory_space=pl.ANY)


def halves(x):
    high = x.astype(jnp.bfloat16)
    return high, (x - high.astype(jnp.float32)).astype(jnp.bfloat16)


def swap(x, axis, first):
    low = range(first, lax.axis_size(axis) - 1, 2)
    return lax.ppermute(x, axis, [(i, i + 1) for i in low] + [(i + 1, i) for i in low])


def exchange(x, partner, spare):
    energies, atoms = lax.axis_size("energy"), lax.axis_size("atom")
    perm = []
    for e in range(energies):
        for a in range(atoms):
            to_e, to_a = partner(e, a)
            if not (0 <= to_e < energies and 0 <= to_a < atoms):
                to_e, to_a = spare(e, a)
            if 0 <= to_e < energies and 0 <= to_a < atoms:
                perm.append((e * atoms + a, to_e * atoms + to_a))
    return lax.ppermute(x, ("energy", "atom"), perm)


def cross_swap(x, step):
    return exchange(x, lambda e, a: (e + 1 if e % 2 else e - 1, a), lambda e, a: (e, a ^ step))


def forward(x, axis):
    size = lax.axis_size(axis)
    ups = [(i, min(i + 2, size - 1)) for i in range(0, size, 2)]
    downs = [(i, max(i - 2, 0)) for i in range(1, size, 2)]
    return lax.ppermute(x, axis, [(i, j) for i, j in ups + downs if i != j])


def put_blocks(blocks, c, green):
    orb = green.shape[-1]
    for e in range(green.shape[0]):
        for a in range(green.shape[1]):
            high, low = halves(green[e, a])
            blocks[c, a, e, :, :orb] = high
            blocks[c, a, e, :, orb:] = low


def add_pairs(group, neighbours, phonon, coupling, blocks, totals, picked, size):
    atoms, slots, orb = coupling.shape[0], coupling.shape[1], coupling.shape[-1]
    e_local = blocks.shape[2]
    index = lax.axis_index("atom")
    base = index * atoms
    if group != OWN:
        upper = (index & 1) == (0 if group == PAIR else 1)
        base += jnp.where(upper, atoms, -atoms)

    found = jnp.int32(0)
    for a in range(atoms):
        for j in range(slots):
            picked[found] = a * slots + j
            b = neighbours[a, j] - base
            found += ((b >= 0) & (b < atoms)).astype(jnp.int32)

    def batch(step, _):
        pairs = []
        for u in range(size):
            at = step * size + u
            item = picked[jnp.minimum(at, found - 1)]
            a = item // slots
            j = item - a * slots
            high, low = halves(coupling[a, j])
            left = jnp.concatenate([high, low], 1)
            right = jnp.concatenate(
                [jnp.concatenate([high, high], 1), jnp.concatenate([low, low], 1)], 0
            )
            pairs.append((a, j, neighbours[a, j] - base, jnp.where(at < found, 1.0, 0.0), left, right))
        inners = []
        for a, j, b, live, left, right in pairs:
            for c in range(len(totals)):
                near = blocks[c, b].reshape(e_local * orb, 2 * orb)
                inner = lax.dot_general(
                    near, right, (((1,), (1,)), ((), ())), preferred_element_type=jnp.float32
                )
                inners.append(inner[:, :orb] + inner[:, orb:])
        results = []
        for a, j, b, live, left, right in pairs:
            for total in totals:
                inner = inners.pop(0)
                sums = [None] * (e_local + 2 * REACH)
                for e in range(e_local):
                    high, low = halves(inner[e * orb : (e + 1) * orb])
                    both = jnp.concatenate([high, low], 1)
                    outer = jnp.dot(
                        left, jnp.concatenate([both, both], 0), preferred_element_type=jnp.float32
                    )
                    outer = outer[:, :orb] + outer[:, orb:]
                    for k, s in enumerate(SHIFTS):
                        d = e - s + REACH
                        term = (phonon[a, k, j] * live) * outer
                        sums[d] = term if sums[d] is None else sums[d] + term
                results.append((total, a, sums))
        for total, a, sums in results:
            for d, value in enumerate(sums):
                if value is not None:
                    total[d, a] += value

    lax.fori_loop(0, (found + size - 1) // size, batch, None)


def copy_all(sources, results, sems):
    copies = [
        pltpu.make_async_copy(source, result, sems.at[i])
        for i, (source, result) in enumerate(zip(sources, results))
    ]
    for copy in copies:
        copy.start()
    for copy in copies:
        copy.wait()


def part_kernel(green, part, sems):
    copy_all([green.at[0]], [part], sems)


def fetch_kernel(green, coupling, phonon, neighbours, *rest):
    copy_all([green.at[1], green, coupling, phonon, neighbours], rest[:-1], rest[-1])


def own_kernel(neighbours, phonon, coupling, green0, green1, total0, total1, blocks, picked):
    for c, (green, total) in enumerate(((green0, total0), (green1, total1))):
        put_blocks(blocks, c, green)
        total[...] = jnp.zeros_like(total)
    add_pairs(OWN, neighbours, phonon, coupling, blocks, (total0, total1), picked, 2)


def pair_kernel(neighbours, phonon, coupling, ahead, before, total, blocks, picked):
    total[...] = before[...]
    put_blocks(blocks, 0, ahead)
    add_pairs(PAIR, neighbours, phonon, coupling, blocks, (total,), picked, BATCH)


def turn_kernel(size, total0, green, by_core, by_cross, turned, partial):
    e_local, a_local = green.shape[1], green.shape[2]
    core, cross = partner_energies(turned.shape[1])
    has_core, has_cross = has_partners(size)
    for c in range(2):
        for a in range(a_local):
            for e in range(e_local):
                turned[c, REACH + e, a] = green[c, e, a].T
            for e in range(REACH):
                turned[c, core + e, a] = by_core[c, e, a].T * has_core
                turned[c, cross + e, a] = by_cross[c, e, a].T * has_cross
    for a in range(a_local):
        partial[a] = rate_sums(total0, turned, 0, a)


def partner_energies(spread):
    odd = lax.axis_index("energy") & 1
    return jnp.where(odd == 0, spread - REACH, 0), jnp.where(odd == 0, 0, spread - REACH)


def has_partners(size):
    me = lax.axis_index("energy")
    above, below = jnp.where(me < size - 1, 1.0, 0.0), jnp.where(me > 0, 1.0, 0.0)
    odd = me & 1
    return jnp.where(odd == 0, above, below), jnp.where(odd == 0, below, above)


def finish(total, core, cross):
    to_core, to_cross = partner_energies(total.shape[0])
    for e in range(REACH):
        core[e] = total[to_core + e]
        cross[e] = total[to_cross + e]


def rate_sums(total, turned, c, a):
    sums = total[0, a] * turned[c, 0, a]
    for d in range(1, total.shape[0]):
        sums += total[d, a] * turned[c, d, a]
    return sums


def far_kernel(neighbours, phonon, coupling, across, before, total, core, cross, blocks, picked):
    add_far(neighbours, phonon, coupling, across, before, total, blocks, picked)
    finish(total, core, cross)


def add_far(neighbours, phonon, coupling, across, before, total, blocks, picked):
    total[...] = before[...]
    put_blocks(blocks, 0, across)
    add_pairs(FAR, neighbours, phonon, coupling, blocks, (total,), picked, BATCH)


def last_kernel(
    scale, neighbours, phonon, coupling, across, before, turned, partial,
    total, core, cross, rate, blocks, picked,
):
    add_far(neighbours, phonon, coupling, across, before, total, blocks, picked)
    finish(total, core, cross)
    for a in range(partial.shape[0]):
        sums = partial[a] - rate_sums(total, turned, 1, a)
        rate[a : a + 1, :] = jnp.sum(sums.T, axis=0, keepdims=True) * scale


def addends(x, axis):
    size = lax.axis_size(axis)
    if size > FEW:
        return [lax.psum(x, axis)]
    if size & (size - 1):
        turns = [[(i, (i + k) % size) for i in range(size)] for k in range(1, size)]
    else:
        turns = [[(i, i ^ k) for i in range(size)] for k in range(1, size)]
    return [x] + [lax.ppermute(x, axis, turn) for turn in turns]


def end_kernel(size, total0, total1, cross0, core0, cross1, core1, *rest):
    *rates, out, rate, work, sems = rest
    e_local = out.shape[1]
    has_core, has_cross = has_partners(size)
    copies = []
    for c, (total, cross, core) in enumerate(((total0, cross0, core0), (total1, cross1, core1))):
        for e in range(e_local):
            work[c, e] = total[REACH + e] + core[e] * has_core + cross[e] * has_cross
        copies.append(pltpu.make_async_copy(work.at[c], out.at[c], sems.at[c]))
        copies[-1].start()
    rate[...] = sum(r[...] for r in rates)
    for copy in copies:
        copy.wait()


def per_device(green, coupling, phonon, neighbours):
    _, e_local, a_local, orb, _ = green.shape
    energies = lax.axis_size("energy")
    points = e_local * energies
    spread = (e_local + 2 * REACH, a_local, orb, orb)
    edge = (REACH, a_local, orb, orb)

    def call(kernel, out, operands, parts=1):
        return pl.pallas_call(
            kernel,
            out_shape=[jax.ShapeDtypeStruct(shape, jnp.float32) for shape in out],
            in_specs=[SMEM, SMEM] + [VMEM] * (1 + len(operands)),
            out_specs=[VMEM] * len(out),
            scratch_shapes=[
                pltpu.VMEM((parts, a_local, e_local, orb, 2 * orb), jnp.bfloat16),
                pltpu.SMEM((a_local * neighbours.shape[1] + 1,), jnp.int32),
            ],
            compiler_params=pltpu.CompilerParams(vmem_limit_bytes=24 * 2**20),
            cost_estimate=pl.CostEstimate(flops=10**6, bytes_accessed=10**4, transcendentals=0),
        )(neighbours, phonon, coupling, *operands)

    def fetch(kernel, out, sources):
        return pl.pallas_call(
            kernel,
            out_shape=[jax.ShapeDtypeStruct(x.shape, x.dtype) for x in out],
            in_specs=[ANY] * len(sources),
            out_specs=[VMEM] * len(out),
            scratch_shapes=[pltpu.SemaphoreType.DMA((len(out),))],
            compiler_params=pltpu.CompilerParams(vmem_limit_bytes=24 * 2**20),
        )(*(pltpu.with_memory_space_constraint(x, pltpu.HBM) for x in sources))

    sources = (green, coupling, jnp.swapaxes(phonon, 1, 2), neighbours)
    part = jax.ShapeDtypeStruct(green.shape[1:], green.dtype)
    (green0,) = fetch(part_kernel, [part], [green])
    green0, *sources = lax.optimization_barrier((green0, *sources))
    green1, green, coupling, phonon, neighbours = fetch(fetch_kernel, [part, *sources], sources)
    ahead1 = swap(green1, "atom", 0)
    ahead0 = swap(green0, "atom", 0)
    by_core, by_cross = swap(green, "energy", 0), cross_swap(green, 2)
    total0, total1 = call(own_kernel, [spread] * 2, (green0, green1), parts=2)
    ahead0, total0, total1 = lax.optimization_barrier((ahead0, total0, total1))
    across0 = forward(ahead0, "atom")
    (total0,) = call(pair_kernel, [spread], (ahead0, total0))
    green1, total0 = lax.optimization_barrier((green1, total0))
    across1 = swap(green1, "atom", 1)
    (total1,) = call(pair_kernel, [spread], (ahead1, total1))
    total0, total1 = lax.optimization_barrier((total0, total1))
    total0, core0, cross0 = call(far_kernel, [spread, edge, edge], (across0, total0))
    core0, cross0 = swap(core0, "energy", 0), cross_swap(cross0, 2)
    turned, partial = pl.pallas_call(
        functools.partial(turn_kernel, energies),
        out_shape=[
            jax.ShapeDtypeStruct((2,) + spread, jnp.float32),
            jax.ShapeDtypeStruct((a_local, orb, orb), jnp.float32),
        ],
        in_specs=[VMEM] * 4,
        out_specs=[VMEM] * 2,
        compiler_params=pltpu.CompilerParams(vmem_limit_bytes=24 * 2**20),
        cost_estimate=pl.CostEstimate(flops=10**6, bytes_accessed=10**4, transcendentals=0),
    )(total0, green, by_core, by_cross)
    total1, core1, cross1, rate = call(
        functools.partial(last_kernel, 1.0 / (4.0 * points)),
        [spread, edge, edge, (a_local, orb)],
        (across1, total1, turned, partial),
    )
    core1, cross1 = swap(core1, "energy", 0), cross_swap(cross1, 1)
    cross0, core0, rate = lax.optimization_barrier((cross0, core0, rate))
    rates = addends(rate, "energy")
    return pl.pallas_call(
        functools.partial(end_kernel, energies),
        out_shape=[
            jax.ShapeDtypeStruct(green.shape, jnp.float32),
            jax.ShapeDtypeStruct((a_local, orb), jnp.float32),
        ],
        in_specs=[VMEM] * (6 + len(rates)),
        out_specs=[ANY, VMEM],
        scratch_shapes=[
            pltpu.VMEM(green.shape, jnp.float32),
            pltpu.SemaphoreType.DMA((2,)),
        ],
        compiler_params=pltpu.CompilerParams(vmem_limit_bytes=24 * 2**20),
        cost_estimate=pl.CostEstimate(flops=10**6, bytes_accessed=2 * 10**6, transcendentals=0),
    )(total0, total1, cross0, core0, cross1, core1, *rates)


def solution(mesh):
    return jax.shard_map(
        per_device,
        mesh=mesh,
        in_specs=(
            P(None, "energy", "atom", None, None),
            P("atom", None, None, None),
            P("atom", None, None),
            P("atom", None),
        ),
        out_specs=(P(None, "energy", "atom", None, None), P("atom", None)),
        check_vma=False,
    )
```

```python
import functools

import jax
import jax.numpy as jnp
from jax import lax
from jax.experimental import pallas as pl
from jax.experimental.pallas import tpu as pltpu
from jax.sharding import PartitionSpec as P

SHIFTS = (-2, -1, 1, 2)
REACH = max(SHIFTS)
OWN, PAIR, FAR = 0, 1, 2
FEW = 4
BATCH = 6
VMEM = pl.BlockSpec(memory_space=pltpu.VMEM)
SMEM = pl.BlockSpec(memory_space=pltpu.SMEM)
ANY = pl.BlockSpec(memory_space=pl.ANY)


def halves(x):
    high = x.astype(jnp.bfloat16)
    return high, (x - high.astype(jnp.float32)).astype(jnp.bfloat16)


def swap(x, axis, first):
    low = range(first, lax.axis_size(axis) - 1, 2)
    return lax.ppermute(x, axis, [(i, i + 1) for i in low] + [(i + 1, i) for i in low])


def exchange(x, partner, spare):
    energies, atoms = lax.axis_size("energy"), lax.axis_size("atom")
    perm = []
    for e in range(energies):
        for a in range(atoms):
            to_e, to_a = partner(e, a)
            if not (0 <= to_e < energies and 0 <= to_a < atoms):
                to_e, to_a = spare(e, a)
            if 0 <= to_e < energies and 0 <= to_a < atoms:
                perm.append((e * atoms + a, to_e * atoms + to_a))
    return lax.ppermute(x, ("energy", "atom"), perm)


def cross_swap(x, step):
    return exchange(x, lambda e, a: (e + 1 if e % 2 else e - 1, a), lambda e, a: (e, a ^ step))


def forward(x, axis):
    size = lax.axis_size(axis)
    ups = [(i, min(i + 2, size - 1)) for i in range(0, size, 2)]
    downs = [(i, max(i - 2, 0)) for i in range(1, size, 2)]
    return lax.ppermute(x, axis, [(i, j) for i, j in ups + downs if i != j])


def put_blocks(blocks, c, green):
    orb = green.shape[-1]
    for e in range(green.shape[0]):
        for a in range(green.shape[1]):
            high, low = halves(green[e, a])
            blocks[c, a, e, :, :orb] = high
            blocks[c, a, e, :, orb:] = low


def add_pairs(group, neighbours, phonon, coupling, blocks, totals, picked, size):
    atoms, slots, orb = coupling.shape[0], coupling.shape[1], coupling.shape[-1]
    e_local = blocks.shape[2]
    index = lax.axis_index("atom")
    base = index * atoms
    if group != OWN:
        upper = (index & 1) == (0 if group == PAIR else 1)
        base += jnp.where(upper, atoms, -atoms)

    found = jnp.int32(0)
    for a in range(atoms):
        for j in range(slots):
            picked[found] = a * slots + j
            b = neighbours[a, j] - base
            found += ((b >= 0) & (b < atoms)).astype(jnp.int32)

    def batch(step, _):
        pairs = []
        for u in range(size):
            at = step * size + u
            item = picked[jnp.minimum(at, found - 1)]
            a = item // slots
            j = item - a * slots
            high, low = halves(coupling[a, j])
            left = jnp.concatenate([high, low], 1)
            right = jnp.concatenate(
                [jnp.concatenate([high, high], 1), jnp.concatenate([low, low], 1)], 0
            )
            pairs.append((a, j, neighbours[a, j] - base, jnp.where(at < found, 1.0, 0.0), left, right))
        inners = []
        for a, j, b, live, left, right in pairs:
            for c in range(len(totals)):
                near = blocks[c, b].reshape(e_local * orb, 2 * orb)
                inner = lax.dot_general(
                    near, right, (((1,), (1,)), ((), ())), preferred_element_type=jnp.float32
                )
                inners.append(inner[:, :orb] + inner[:, orb:])
        results = []
        for a, j, b, live, left, right in pairs:
            for total in totals:
                inner = inners.pop(0)
                sums = [None] * (e_local + 2 * REACH)
                for e in range(e_local):
                    high, low = halves(inner[e * orb : (e + 1) * orb])
                    both = jnp.concatenate([high, low], 1)
                    outer = jnp.dot(
                        left, jnp.concatenate([both, both], 0), preferred_element_type=jnp.float32
                    )
                    outer = outer[:, :orb] + outer[:, orb:]
                    for k, s in enumerate(SHIFTS):
                        d = e - s + REACH
                        term = (phonon[a, k, j] * live) * outer
                        sums[d] = term if sums[d] is None else sums[d] + term
                results.append((total, a, sums))
        for total, a, sums in results:
            for d, value in enumerate(sums):
                if value is not None:
                    total[d, a] += value

    lax.fori_loop(0, (found + size - 1) // size, batch, None)


def copy_all(sources, results, sems):
    copies = [
        pltpu.make_async_copy(source, result, sems.at[i])
        for i, (source, result) in enumerate(zip(sources, results))
    ]
    for copy in copies:
        copy.start()
    for copy in copies:
        copy.wait()


def part_kernel(green, part, sems):
    copy_all([green.at[0]], [part], sems)


def fetch_kernel(green, coupling, phonon, neighbours, *rest):
    copy_all([green.at[1], green, coupling, phonon, neighbours], rest[:-1], rest[-1])


def own_kernel(neighbours, phonon, coupling, green0, green1, total0, total1, blocks, picked):
    for c, (green, total) in enumerate(((green0, total0), (green1, total1))):
        put_blocks(blocks, c, green)
        total[...] = jnp.zeros_like(total)
    add_pairs(OWN, neighbours, phonon, coupling, blocks, (total0, total1), picked, 2)


def pair_kernel(neighbours, phonon, coupling, ahead, before, total, blocks, picked):
    total[...] = before[...]
    put_blocks(blocks, 0, ahead)
    add_pairs(PAIR, neighbours, phonon, coupling, blocks, (total,), picked, BATCH)


def turn_kernel(size, total0, green, by_core, by_cross, turned, partial):
    e_local, a_local = green.shape[1], green.shape[2]
    core, cross = partner_energies(turned.shape[1])
    has_core, has_cross = has_partners(size)
    for c in range(2):
        for a in range(a_local):
            for e in range(e_local):
                turned[c, REACH + e, a] = green[c, e, a].T
            for e in range(REACH):
                turned[c, core + e, a] = by_core[c, e, a].T * has_core
                turned[c, cross + e, a] = by_cross[c, e, a].T * has_cross
    for a in range(a_local):
        partial[a] = rate_sums(total0, turned, 0, a)


def partner_energies(spread):
    odd = lax.axis_index("energy") & 1
    return jnp.where(odd == 0, spread - REACH, 0), jnp.where(odd == 0, 0, spread - REACH)


def has_partners(size):
    me = lax.axis_index("energy")
    above, below = jnp.where(me < size - 1, 1.0, 0.0), jnp.where(me > 0, 1.0, 0.0)
    odd = me & 1
    return jnp.where(odd == 0, above, below), jnp.where(odd == 0, below, above)


def finish(total, core, cross):
    to_core, to_cross = partner_energies(total.shape[0])
    for e in range(REACH):
        core[e] = total[to_core + e]
        cross[e] = total[to_cross + e]


def rate_sums(total, turned, c, a):
    sums = total[0, a] * turned[c, 0, a]
    for d in range(1, total.shape[0]):
        sums += total[d, a] * turned[c, d, a]
    return sums


def far_kernel(neighbours, phonon, coupling, across, before, total, core, cross, blocks, picked):
    add_far(neighbours, phonon, coupling, across, before, total, blocks, picked)
    finish(total, core, cross)


def add_far(neighbours, phonon, coupling, across, before, total, blocks, picked):
    total[...] = before[...]
    put_blocks(blocks, 0, across)
    add_pairs(FAR, neighbours, phonon, coupling, blocks, (total,), picked, BATCH)


def last_kernel(
    scale, neighbours, phonon, coupling, across, before, turned, partial,
    total, core, cross, rate, blocks, picked,
):
    add_far(neighbours, phonon, coupling, across, before, total, blocks, picked)
    finish(total, core, cross)
    for a in range(partial.shape[0]):
        sums = partial[a] - rate_sums(total, turned, 1, a)
        rate[a : a + 1, :] = jnp.sum(sums.T, axis=0, keepdims=True) * scale


def addends(x, axis):
    size = lax.axis_size(axis)
    if size > FEW:
        return [lax.psum(x, axis)]
    if size & (size - 1):
        turns = [[(i, (i + k) % size) for i in range(size)] for k in range(1, size)]
    else:
        turns = [[(i, i ^ k) for i in range(size)] for k in range(1, size)]
    return [x] + [lax.ppermute(x, axis, turn) for turn in turns]


def end_kernel(size, total0, total1, cross0, core0, cross1, core1, *rest):
    *rates, out, rate = rest
    e_local = out.shape[1]
    has_core, has_cross = has_partners(size)
    for c, (total, cross, core) in enumerate(((total0, cross0, core0), (total1, cross1, core1))):
        for e in range(e_local):
            out[c, e] = total[REACH + e] + core[e] * has_core + cross[e] * has_cross
    rate[...] = sum(r[...] for r in rates)


def per_device(green, coupling, phonon, neighbours):
    _, e_local, a_local, orb, _ = green.shape
    energies = lax.axis_size("energy")
    points = e_local * energies
    spread = (e_local + 2 * REACH, a_local, orb, orb)
    edge = (REACH, a_local, orb, orb)

    def call(kernel, out, operands, parts=1):
        return pl.pallas_call(
            kernel,
            out_shape=[jax.ShapeDtypeStruct(shape, jnp.float32) for shape in out],
            in_specs=[SMEM, SMEM] + [VMEM] * (1 + len(operands)),
            out_specs=[VMEM] * len(out),
            scratch_shapes=[
                pltpu.VMEM((parts, a_local, e_local, orb, 2 * orb), jnp.bfloat16),
                pltpu.SMEM((a_local * neighbours.shape[1] + 1,), jnp.int32),
            ],
            compiler_params=pltpu.CompilerParams(vmem_limit_bytes=24 * 2**20),
            cost_estimate=pl.CostEstimate(flops=10**6, bytes_accessed=10**4, transcendentals=0),
        )(neighbours, phonon, coupling, *operands)

    def fetch(kernel, out, sources):
        return pl.pallas_call(
            kernel,
            out_shape=[jax.ShapeDtypeStruct(x.shape, x.dtype) for x in out],
            in_specs=[ANY] * len(sources),
            out_specs=[VMEM] * len(out),
            scratch_shapes=[pltpu.SemaphoreType.DMA((len(out),))],
            compiler_params=pltpu.CompilerParams(vmem_limit_bytes=24 * 2**20),
        )(*(pltpu.with_memory_space_constraint(x, pltpu.HBM) for x in sources))

    sources = (green, coupling, jnp.swapaxes(phonon, 1, 2), neighbours)
    part = jax.ShapeDtypeStruct(green.shape[1:], green.dtype)
    (green0,) = fetch(part_kernel, [part], [green])
    green0, *sources = lax.optimization_barrier((green0, *sources))
    green1, green, coupling, phonon, neighbours = fetch(fetch_kernel, [part, *sources], sources)
    ahead1 = swap(green1, "atom", 0)
    ahead0 = swap(green0, "atom", 0)
    by_core, by_cross = swap(green, "energy", 0), cross_swap(green, 2)
    total0, total1 = call(own_kernel, [spread] * 2, (green0, green1), parts=2)
    ahead0, total0, total1 = lax.optimization_barrier((ahead0, total0, total1))
    across0 = forward(ahead0, "atom")
    (total0,) = call(pair_kernel, [spread], (ahead0, total0))
    green1, total0 = lax.optimization_barrier((green1, total0))
    across1 = swap(green1, "atom", 1)
    (total1,) = call(pair_kernel, [spread], (ahead1, total1))
    total0, total1 = lax.optimization_barrier((total0, total1))
    total0, core0, cross0 = call(far_kernel, [spread, edge, edge], (across0, total0))
    core0, cross0 = swap(core0, "energy", 0), cross_swap(cross0, 2)
    turned, partial = pl.pallas_call(
        functools.partial(turn_kernel, energies),
        out_shape=[
            jax.ShapeDtypeStruct((2,) + spread, jnp.float32),
            jax.ShapeDtypeStruct((a_local, orb, orb), jnp.float32),
        ],
        in_specs=[VMEM] * 4,
        out_specs=[VMEM] * 2,
        compiler_params=pltpu.CompilerParams(vmem_limit_bytes=24 * 2**20),
        cost_estimate=pl.CostEstimate(flops=10**6, bytes_accessed=10**4, transcendentals=0),
    )(total0, green, by_core, by_cross)
    total1, core1, cross1, rate = call(
        functools.partial(last_kernel, 1.0 / (4.0 * points)),
        [spread, edge, edge, (a_local, orb)],
        (across1, total1, turned, partial),
    )
    core1, cross1 = swap(core1, "energy", 0), cross_swap(cross1, 1)
    core0, cross0, rate = lax.optimization_barrier((core0, cross0, rate))
    rates = addends(rate, "energy")
    return pl.pallas_call(
        functools.partial(end_kernel, energies),
        out_shape=[
            jax.ShapeDtypeStruct(green.shape, jnp.float32),
            jax.ShapeDtypeStruct((a_local, orb), jnp.float32),
        ],
        in_specs=[VMEM] * (6 + len(rates)),
        out_specs=[VMEM] * 2,
        compiler_params=pltpu.CompilerParams(vmem_limit_bytes=24 * 2**20),
        cost_estimate=pl.CostEstimate(flops=10**6, bytes_accessed=2 * 10**6, transcendentals=0),
    )(total0, total1, cross0, core0, cross1, core1, *rates)


def solution(mesh):
    return jax.shard_map(
        per_device,
        mesh=mesh,
        in_specs=(
            P(None, "energy", "atom", None, None),
            P("atom", None, None, None),
            P("atom", None, None),
            P("atom", None),
        ),
        out_specs=(P(None, "energy", "atom", None, None), P("atom", None)),
        check_vma=False,
    )
```
